256 devices in a mesh: slab: 16 (over x, y), col: 8 (over z), energy: 2 (over core).
Axes of the slice: x: 4, y: 4, z: 8, core: 2. Of those that a mesh axis runs over, the one named last changes fastest.
Arguments:
- diag_inverse: float32 [64, 2, 2048, 2048], P(('energy', 'slab'), None, None, 'col'), parts along dimension 0, may hold values from -2 to 2
- couplings: float32 [64, 2, 256, 256], P(('energy', 'slab')), parts along dimension 0, may hold values from -1 to 1
- sources: float32 [4, 2, 2048, 64], P('energy', None, 'col'), parts along dimension 0, may hold values from -6 to 6
- inject: int32 [2, 64], replicated, may hold values from 0 to 31, as said below
- leads: float32 [4, 2, 256, 64], P('energy'), parts along dimension 0, may hold values from -6 to 6
Outputs:
- left_states: float32 [64, 2, 2048, 64], P(('energy', 'slab'), None, 'col'), parts along dimension 0
- right_states: float32 [64, 2, 2048, 64], P(('energy', 'slab'), None, 'col'), parts along dimension 0
The draws below stay inside these ranges and needn't reach their ends.
There are 2 independent parts, one for each index of `energy`. The reference program is written for one: setup_inputs(seed, part) draws one part's arguments, and reference() takes and returns one part's arrays. A program takes and returns all parts, laid end to end along the dimension named above; an argument that names none is the same for every part. Nothing has to cross between parts.
Inputs may be any that keep to these rules, and one draw needn't show every extreme that they name: `inject`: slab index of each injected column; in each sweep column 0 goes into slab 0 and column 1 into the last slab.
All inputs are finite; a program needn't handle non-finite values.
Results may differ from the reference program's by a relative error of at most 0.0003.
Values sent between devices are 32-bit elements; how exact they have to be, the bound alone decides.
No kernel may reach another device: no remote copies, remote signals or barrier semaphores. Data moves between devices by JAX's collectives and lax.ppermute only.
A program may use at most 192 MiB of HBM per device.

```python
import jax
import jax.numpy as jnp
from jax import lax

ORB = 2048
IFACE = 256
MODES = 64
SLABS = 32


def draw_diag_inverse(key, part):
    key = jax.random.fold_in(key, 11)
    key_off, key_real, key_imag = jax.random.split(key, 3)
    shape = (SLABS, 2, ORB, ORB)
    spread = jnp.clip(jax.random.normal(key_off, shape, jnp.float32), -2.5, 2.5)
    spread = spread * (1.4 * ORB ** (-0.5))
    real_diag = jax.random.uniform(key_real, (SLABS, ORB), jnp.float32, 0.5, 1.5)
    imag_diag = jax.random.uniform(key_imag, (SLABS, ORB), jnp.float32, -0.5, 0.5)
    diagonal = jnp.stack([real_diag, imag_diag], axis=1)
    identity = jnp.eye(ORB, dtype=jnp.float32)
    return spread + diagonal[:, :, :, None] * identity[None, None, :, :]


def draw_inject(key, part):
    key = jax.random.fold_in(key, 5)
    values = jax.random.randint(key, (2, MODES), 0, SLABS, dtype=jnp.int32)
    values = values.at[:, 0].set(0)
    values = values.at[:, 1].set(SLABS - 1)
    return values.astype(jnp.int32)


def block_levels(key, extent, cuts, smallest, top_value):
    factor_of, own = 1.0, jax.random.fold_in(key, 6)
    for dim, blocks in cuts:
        draws = jnp.exp(jax.random.uniform(jax.random.fold_in(own, dim), (blocks,), jnp.float32, smallest / len(cuts), top_value / len(cuts)))
        factor_of = factor_of * jnp.repeat(draws, extent[dim] // blocks).reshape([-1 if axis == dim else 1 for axis in range(len(extent))])
    return factor_of


def normal_values(rng, extent, scale, bound, cuts=(), kind=jnp.bfloat16):
    loudness = block_levels(rng, extent, cuts, -0.22, 0.18) if cuts else 1.0
    drawn = jax.random.normal(rng, extent, jnp.float32) * scale * loudness
    return jnp.minimum(jnp.maximum(drawn, -bound), bound).astype(kind)


def setup_inputs(seed: int = 0, part: int = 0) -> dict:
    key_list = jax.random.split(jax.random.key(seed), 6)
    part_splits = jax.random.split(jax.random.fold_in(key_list[5], part), 6)
    diag_inverse = draw_diag_inverse(jax.random.fold_in(jax.random.fold_in(key_list[5], part), 71), part)
    couplings = normal_values(part_splits[1], (SLABS, 2, IFACE, IFACE), (0.36 * (ORB // IFACE) ** 0.5 * IFACE ** -0.5), 1.0, ((0, 16),), jnp.float32)
    sources = normal_values(part_splits[2], (2, 2, ORB, MODES), 1.0, 6.0, ((2, 8),), jnp.float32)
    inject = draw_inject(jax.random.fold_in(key_list[5], 71), part)
    leads = normal_values(part_splits[4], (2, 2, IFACE, MODES), 1.0, 6.0, (), jnp.float32)
    return {"diag_inverse": diag_inverse, "couplings": couplings, "sources": sources, "inject": inject, "leads": leads}


def real_dot(left, right):
    return jnp.dot(left, right, precision=lax.Precision.HIGHEST, preferred_element_type=jnp.float32)


def complex_product(matrix, block):
    real_part = real_dot(matrix[0], block[0]) - real_dot(matrix[1], block[1])
    imag_part = real_dot(matrix[0], block[1]) + real_dot(matrix[1], block[0])
    return jnp.stack([real_part, imag_part], axis=0)


def reference(diag_inverse, couplings, sources, inject, leads):
    stride = ORB // IFACE
    positions = jnp.arange(SLABS, dtype=jnp.int32)

    def left_step(inflow, items):
        block, coupling, position = items
        base = jnp.where((inject[0] == position)[None, None, :], sources[0], jnp.float32(0.0))
        feed = base.at[:, 0::stride, :].add(complex_product(coupling, inflow))
        result = complex_product(block, feed)
        return result[:, 1::stride, :], result

    def right_step(inflow, items):
        block, coupling, position = items
        base = jnp.where((inject[1] == position)[None, None, :], sources[1], jnp.float32(0.0))
        feed = base.at[:, 1::stride, :].add(inflow)
        result = complex_product(block, feed)
        adjoint = jnp.stack([coupling[0].T, -coupling[1].T], axis=0)
        return complex_product(adjoint, result[:, 0::stride, :]), result

    last_left, left_states = lax.scan(left_step, leads[0], (diag_inverse, couplings, positions))
    last_right, right_states = lax.scan(right_step, leads[1], (diag_inverse, couplings, positions), reverse=True)
    return left_states, right_states
```

```python
import jax
import jax.numpy as jnp
from jax import lax
from jax.experimental import pallas as pl
from jax.experimental.pallas import tpu as pltpu
from jax.sharding import PartitionSpec as P

F32 = jnp.float32
BF16 = jnp.bfloat16
LIMIT = 48 * 1024 * 1024


def split(value):
    high = value.astype(BF16)
    return high, (value - high.astype(F32)).astype(BF16)


def mm(left, right):
    return lax.dot_general(left, right, (((1,), (0,)), ((), ())), preferred_element_type=F32)


def mm_t(left, right):
    return lax.dot_general(left, right, (((1,), (1,)), ((), ())), preferred_element_type=F32)


def mm3(left, right):
    return mm(left[0], right[0]) + (mm(left[0], right[1]) + mm(left[1], right[0]))


def mm3_t(left, right):
    return mm_t(left[0], right[0]) + (mm_t(left[0], right[1]) + mm_t(left[1], right[0]))


def complex_rows(left, right):
    half = left.shape[0] // 2
    parts = split(left)
    by_real = mm3(parts, split(right[0]))
    by_imag = mm3(parts, split(right[1]))
    return jnp.concatenate(
        [by_real[:half] - by_imag[half:], by_imag[:half] + by_real[half:]], axis=0
    )


def interface_kernel(
    first_ref, inject_ref, src_ref, g0_ref, g1_ref, out_ref, high_ref, low_ref, acc_ref
):
    step = pl.program_id(0)
    slab = step // 2
    plane = step % 2
    width = src_ref.shape[2]
    modes = src_ref.shape[3]

    @pl.when(step == 0)
    def _():
        rows = lax.broadcasted_iota(jnp.int32, (width // 8, width), 0)
        cols = lax.broadcasted_iota(jnp.int32, (width // 8, width), 1)
        for local in range(2):
            pieces = []
            for sweep in range(2):
                pieces.append((cols == rows * 8 + sweep).astype(F32))
                chosen = inject_ref[sweep : sweep + 1, :] == first_ref[0] + local
                for part in range(2):
                    pieces.append(jnp.where(chosen, src_ref[sweep, part], 0.0).T)
            high, low = split(jnp.concatenate(pieces, axis=0))
            high_ref[local] = high
            low_ref[local] = low
        acc_ref[...] = jnp.zeros_like(acc_ref)

    half = high_ref.shape[1] // 2
    lead = width // 8
    count = g0_ref.shape[2] // 8
    for sweep in range(2):
        rows = jnp.concatenate(
            [ref[0, 0, pl.ds(1 - sweep, count, stride=8), :] for ref in (g0_ref, g1_ref)], axis=1
        )
        picked = pl.ds(sweep * half, half)
        term = mm3_t((high_ref[slab, picked, :], low_ref[slab, picked, :]), split(rows))
        order = slab if sweep == 0 else 1 - slab
        place = pl.ds(pl.multiple_of((order * 2 + plane) * lead, lead), lead)
        for member in range(4):
            out_ref[sweep * 4 + member, place, :] = term[:lead]
        real, imag = term[lead : lead + modes], term[lead + modes :]

        @pl.when(plane == 0)
        def _():
            acc_ref[sweep, :modes] += real
            acc_ref[sweep, modes:] += imag

        @pl.when(plane == 1)
        def _():
            acc_ref[sweep, :modes] -= imag
            acc_ref[sweep, modes:] += real

    @pl.when(step == 3)
    def _():
        for dest in range(8):
            sweep, member = divmod(dest, 4)
            for part in range(2):
                start = part * modes + member * 16
                out_ref[dest, 4 * lead + part * 16 : 4 * lead + (part + 1) * 16, :] = acc_ref[
                    sweep, start : start + 16, :
                ]


def spread_kernel(high_ref, low_ref, g_ref, out_ref):
    half = high_ref.shape[1] // 2
    lead = g_ref.shape[3] // 8
    modes = (half - lead) // 2
    total = [0.0] * 4
    for slab in range(2):
        parts = (high_ref[slab], low_ref[slab])
        real = mm3_t(parts, split(g_ref[slab, 0]))
        imag = mm3_t(parts, split(g_ref[slab, 1]))
        for sweep in range(2):
            base = sweep * half
            place = slab * 4 * lead + sweep * 2 * lead
            out_ref[0, place : place + lead, :] = real[base : base + lead]
            out_ref[0, place + lead : place + 2 * lead, :] = imag[base : base + lead]
            one, two, three = base + lead, base + lead + modes, base + half
            total[2 * sweep] += real[one:two] - imag[two:three]
            total[2 * sweep + 1] += real[two:three] + imag[one:two]
    for item in range(4):
        place = 8 * lead + item * modes
        out_ref[0, place : place + modes, :] = total[item]


def stacked(ref, start, count):
    return jnp.concatenate([ref[block, start : start + count, :] for block in range(8)], axis=0)


def pair_map_kernel(team_ref, recv_ref, c_ref, mask_ref, out_ref, x_ref, qa_ref):
    left = team_ref[0] == 0
    size = c_ref.shape[3]
    lead = size // 8
    coupled = []
    for slab in range(2):
        real = jnp.where(left, c_ref[slab, 0].T, c_ref[slab, 0])
        imag = jnp.where(left, c_ref[slab, 1].T, -c_ref[slab, 1])
        x_ref[slab, :size] = real
        x_ref[slab, size:] = imag
        coupled.append((real, imag))
    blocks = [
        (stacked(recv_ref, 2 * item * lead, lead), stacked(recv_ref, (2 * item + 1) * lead, lead))
        for item in range(2)
    ]
    flow = recv_ref[0, 4 * lead :, :]
    for block in range(1, 8):
        flow = flow + recv_ref[block, 4 * lead :, :]
    flow_a = jnp.where(mask_ref[0] != 0, flow, 0.0)
    flow_b = jnp.where(mask_ref[1] != 0, flow, 0.0)
    qa_ref[...] = flow_a

    def pick(one, two):
        return (jnp.where(left, one[0], two[0]), jnp.where(left, one[1], two[1]))

    def times(one, two):
        both = complex_rows(jnp.concatenate(one, axis=0), two)
        return both, (both[:size], both[size:])

    first, _ = times(pick(coupled[0], blocks[0]), pick(blocks[0], coupled[1]))
    _, second = times(pick(coupled[1], blocks[1]), pick(blocks[1], coupled[0]))
    out_ref[: 2 * size, :] = complex_rows(first, second)
    flow_a = jnp.where(left, flow_a, complex_rows(flow_a, coupled[1]))
    flow_b = jnp.where(left, flow_b, complex_rows(flow_b, coupled[0]))
    out_ref[2 * size :, :] = complex_rows(flow_a, second) + flow_b


def chain_kernel(order_ref, lead_ref, map_ref, recv_ref, x_ref, qa_ref, out_ref, state_ref):
    step = pl.program_id(0)
    size = x_ref.shape[2]
    lead = size // 8

    @pl.when(step == 0)
    def _():
        state_ref[...] = lead_ref[...]

    @pl.when(step < order_ref[16])
    def _():
        flow = complex_rows(state_ref[...], (map_ref[0, :size], map_ref[0, size : 2 * size]))
        state_ref[...] = flow + map_ref[0, 2 * size :]

    @pl.when(step == 14)
    def _():
        left = order_ref[17] == 0
        state = state_ref[...]
        turned = complex_rows(state, (x_ref[0, :size], x_ref[0, size:]))
        inner_a = jnp.where(left, turned, state)
        block = (stacked(recv_ref, 0, lead), stacked(recv_ref, lead, lead))
        middle = complex_rows(inner_a, block) + qa_ref[...]
        inner_b = complex_rows(middle, (x_ref[1, :size], x_ref[1, size:]))
        for dest in range(8):
            out_ref[dest, :32, :] = inner_a
            out_ref[dest, 32:, :] = inner_b


def arrange_kernel(first_ref, inject_ref, recv_ref, high_ref, low_ref, base_ref):
    lead = recv_ref.shape[2] // 8
    modes = inject_ref.shape[1]
    for slab in range(2):
        for kind in range(4):
            value = stacked(recv_ref, (slab * 4 + kind) * lead, lead)
            high, low = split(value)
            sweep, part = divmod(kind, 2)
            high_ref[slab, sweep, part] = high
            low_ref[slab, sweep, part] = low
    total = recv_ref[0, 8 * lead :, :]
    for block in range(1, 8):
        total = total + recv_ref[block, 8 * lead :, :]
    for sweep in range(2):
        for part in range(2):
            start = (2 * sweep + part) * modes
            turned = total[start : start + modes].T
            for slab in range(2):
                chosen = inject_ref[sweep : sweep + 1, :] == first_ref[0] + slab
                base_ref[sweep, slab, part] = jnp.where(chosen, turned, 0.0)


def state_kernel(inner_ref, high_ref, low_ref, base_ref, left_ref, right_ref):
    for sweep, out_ref in enumerate((left_ref, right_ref)):
        for slab in range(2):
            item = slab if sweep == 0 else 1 - slab
            pieces = []
            for part in range(2):
                start = item * 32 + part * 16
                for member in range(4):
                    pieces.append(inner_ref[sweep * 4 + member, start : start + 16, :])
            parts = split(jnp.concatenate(pieces, axis=0))
            half = parts[0].shape[0] // 2
            by = []
            for part in range(2):
                by.append(mm3(parts, (high_ref[slab, sweep, part], low_ref[slab, sweep, part])))
            out_ref[slab, 0] = base_ref[sweep, slab, 0] + (by[0][:half] - by[1][half:]).T
            out_ref[slab, 1] = base_ref[sweep, slab, 1] + (by[1][:half] + by[0][half:]).T


def params(**extra):
    return pltpu.CompilerParams(vmem_limit_bytes=LIMIT, **extra)


def whole(shape):
    zeros = (0,) * len(shape)
    return pl.BlockSpec(shape, lambda *_: zeros)


SMEM = pl.BlockSpec(memory_space=pltpu.SMEM)
VMEM = pl.BlockSpec(memory_space=pltpu.VMEM)


def exchange(value):
    return lax.all_to_all(value, "col", split_axis=0, concat_axis=0, tiled=True)


def on_device(diag_inverse, couplings, sources, inject, leads):
    orbitals = diag_inverse.shape[2]
    width = diag_inverse.shape[3]
    size = couplings.shape[2]
    modes = sources.shape[3]
    lead = size // 8
    slabs = lax.axis_size("slab")
    slab_index = lax.axis_index("slab")
    col_index = lax.axis_index("col")
    team = col_index // 4
    member = col_index % 4
    first = jnp.reshape(slab_index * 2, (1,)).astype(jnp.int32)
    team_flag = jnp.reshape(team, (1,)).astype(jnp.int32)
    stack = 2 * (lead + 2 * modes)
    block_rows = 4 * lead + 32

    sent, high, low = pl.pallas_call(
        interface_kernel,
        grid=(4,),
        in_specs=[
            SMEM,
            whole(inject.shape),
            whole(sources.shape),
            pl.BlockSpec((1, 1, orbitals, width // 2), lambda step: (step // 2, step % 2, 0, 0)),
            pl.BlockSpec((1, 1, orbitals, width // 2), lambda step: (step // 2, step % 2, 0, 1)),
        ],
        out_specs=[
            whole((8, block_rows, size)),
            whole((2, stack, width)),
            whole((2, stack, width)),
        ],
        out_shape=[
            jax.ShapeDtypeStruct((8, block_rows, size), F32),
            jax.ShapeDtypeStruct((2, stack, width), BF16),
            jax.ShapeDtypeStruct((2, stack, width), BF16),
        ],
        scratch_shapes=[pltpu.VMEM((2, 2 * modes, size), F32)],
        compiler_params=params(),
        name="interface_terms",
    )(first, inject, sources, diag_inverse, diag_inverse)
    received = exchange(sent)

    own_inject = lax.dynamic_slice(inject, (team, member * 16), (1, 16))[0]
    own_inject = jnp.concatenate([own_inject, own_inject])
    slab_a = first[0] + team
    slab_b = first[0] + 1 - team
    marks = jnp.stack([own_inject == slab_a, own_inject == slab_b]).astype(F32)
    marks = jnp.broadcast_to(marks[:, :, None], (2, 32, size))
    packed, turned, flow_a = pl.pallas_call(
        pair_map_kernel,
        in_specs=[SMEM, VMEM, VMEM, VMEM],
        out_specs=[VMEM, VMEM, VMEM],
        out_shape=[
            jax.ShapeDtypeStruct((2 * size + 32, size), F32),
            jax.ShapeDtypeStruct((2, 2 * size, size), F32),
            jax.ShapeDtypeStruct((32, size), F32),
        ],
        compiler_params=params(),
        name="pair_map",
    )(team_flag, received, couplings, marks)
    high, low, packed = lax.optimization_barrier((high, low, packed))
    maps = lax.all_gather(packed, "slab", axis=0)

    spread = pl.pallas_call(
        spread_kernel,
        grid=(8,),
        in_specs=[
            whole((2, stack, width)),
            whole((2, stack, width)),
            pl.BlockSpec((2, 2, orbitals // 8, width), lambda step: (0, 0, step, 0)),
        ],
        out_specs=pl.BlockSpec((1, 8 * lead + 4 * modes, orbitals // 8), lambda step: (step, 0, 0)),
        out_shape=jax.ShapeDtypeStruct((8, 8 * lead + 4 * modes, orbitals // 8), F32),
        compiler_params=params(),
        name="spread_terms",
    )(high, low, diag_inverse)
    rows = exchange(spread)
    part_rows = orbitals // 8
    row_high, row_low, base = pl.pallas_call(
        arrange_kernel,
        in_specs=[SMEM, VMEM, VMEM],
        out_specs=[VMEM, VMEM, VMEM],
        out_shape=[
            jax.ShapeDtypeStruct((2, 2, 2, size, part_rows), BF16),
            jax.ShapeDtypeStruct((2, 2, 2, size, part_rows), BF16),
            jax.ShapeDtypeStruct((2, 2, 2, part_rows, modes), F32),
        ],
        compiler_params=params(),
        name="arrange_rows",
    )(first, inject, rows)

    own_lead = lax.dynamic_slice(
        leads, (team, 0, 0, member * 16), (1, 2, size, 16)
    )[0]
    own_lead = jnp.transpose(own_lead, (0, 2, 1)).reshape(32, size)
    position = jnp.where(team == 0, slab_index, slabs - 1 - slab_index)
    steps = jnp.minimum(jnp.arange(16, dtype=jnp.int32), jnp.maximum(position - 1, 0))
    steps = jnp.where(team == 0, steps, slabs - 1 - steps)
    order = jnp.concatenate([steps, jnp.stack([position, team])]).astype(jnp.int32)
    inner = pl.pallas_call(
        chain_kernel,
        grid_spec=pltpu.PrefetchScalarGridSpec(
            num_scalar_prefetch=1,
            grid=(15,),
            in_specs=[
                whole((32, size)),
                pl.BlockSpec((1, 2 * size + 32, size), lambda step, order: (order[step], 0, 0)),
                whole((8, block_rows, size)),
                whole((2, 2 * size, size)),
                whole((32, size)),
            ],
            out_specs=whole((8, 64, size)),
            scratch_shapes=[pltpu.VMEM((32, size), F32)],
        ),
        out_shape=jax.ShapeDtypeStruct((8, 64, size), F32),
        compiler_params=params(),
        name="chain",
    )(order, own_lead, maps, received, turned, flow_a)
    inner = exchange(inner)

    shape = (2, 2, part_rows, modes)
    return pl.pallas_call(
        state_kernel,
        in_specs=[VMEM, VMEM, VMEM, VMEM],
        out_specs=[VMEM, VMEM],
        out_shape=[jax.ShapeDtypeStruct(shape, F32), jax.ShapeDtypeStruct(shape, F32)],
        compiler_params=params(),
        name="states",
    )(inner, row_high, row_low, base)


def solution(mesh):
    placed = (
        P(("energy", "slab"), None, None, "col"),
        P(("energy", "slab"), None, None, None),
        P("energy", None, "col", None),
        P(),
        P("energy", None, None, None),
    )

    def run(*args):
        left, right = on_device(*args)
        return left, right

    return jax.shard_map(
        run,
        mesh=mesh,
        in_specs=placed,
        out_specs=(
            P(("energy", "slab"), None, "col", None),
            P(("energy", "slab"), None, "col", None),
        ),
        check_vma=False,
    )
```

```python
import jax
import jax.numpy as jnp
from jax import lax
from jax.experimental import pallas as pl
from jax.experimental.pallas import tpu as pltpu
from jax.sharding import PartitionSpec as P

F32 = jnp.float32
BF16 = jnp.bfloat16
LIMIT = 48 * 1024 * 1024


def split(value):
    high = value.astype(BF16)
    return high, (value - high.astype(F32)).astype(BF16)


def mm(left, right, transposed=False):
    dims = (((1,), (1 if transposed else 0,)), ((), ()))
    return lax.dot_general(left, right, dims, preferred_element_type=F32)


def mm3(left, right, transposed=False):
    rows = left[0].shape[0]
    wide = mm(jnp.concatenate(left, axis=0), right[0], transposed)
    return wide[:rows] + (wide[rows:] + mm(left[0], right[1], transposed))


def complex_rows(left, right):
    half = left.shape[0] // 2
    parts = split(left)
    by_real = mm3(parts, split(right[0]))
    by_imag = mm3(parts, split(right[1]))
    return jnp.concatenate(
        [by_real[:half] - by_imag[half:], by_imag[:half] + by_real[half:]], axis=0
    )


def interface_kernel(
    first_ref, inject_ref, src_ref, g0_ref, g1_ref, out_ref, high_ref, low_ref, acc_ref
):
    step = pl.program_id(0)
    slab = step // 2
    plane = step % 2
    modes = src_ref.shape[2]
    width = src_ref.shape[3]

    @pl.when(step == 0)
    def _():
        rows = lax.broadcasted_iota(jnp.int32, (width // 8, width), 0)
        cols = lax.broadcasted_iota(jnp.int32, (width // 8, width), 1)
        targets = [
            jnp.broadcast_to(inject_ref[sweep : sweep + 1, :].astype(F32), (width, modes)).T
            for sweep in range(2)
        ]
        for local in range(2):
            pieces = []
            for sweep in range(2):
                pieces.append((cols == rows * 8 + sweep).astype(F32))
                chosen = targets[sweep] == (first_ref[0] + local).astype(F32)
                for part in range(2):
                    pieces.append(jnp.where(chosen, src_ref[sweep, part], 0.0))
            high, low = split(jnp.concatenate(pieces, axis=0))
            high_ref[local] = high
            low_ref[local] = low
        acc_ref[...] = jnp.zeros_like(acc_ref)

    half = high_ref.shape[1] // 2
    lead = width // 8
    count = g0_ref.shape[2] // 8
    for sweep in range(2):
        rows = jnp.concatenate(
            [ref[0, 0, pl.ds(1 - sweep, count, stride=8), :] for ref in (g0_ref, g1_ref)], axis=1
        )
        picked = pl.ds(sweep * half, half)
        term = mm3((high_ref[slab, picked, :], low_ref[slab, picked, :]), split(rows), True)
        order = slab if sweep == 0 else 1 - slab
        place = pl.ds(pl.multiple_of((order * 2 + plane) * lead, lead), lead)
        for member in range(4):
            out_ref[sweep * 4 + member, place, :] = term[:lead]
        real, imag = term[lead : lead + modes], term[lead + modes :]

        @pl.when(plane == 0)
        def _():
            acc_ref[sweep, :modes] += real
            acc_ref[sweep, modes:] += imag

        @pl.when(plane == 1)
        def _():
            acc_ref[sweep, :modes] -= imag
            acc_ref[sweep, modes:] += real

    @pl.when(step == 3)
    def _():
        for dest in range(8):
            sweep, member = divmod(dest, 4)
            for part in range(2):
                start = part * modes + member * 16
                out_ref[dest, 4 * lead + part * 16 : 4 * lead + (part + 1) * 16, :] = acc_ref[
                    sweep, start : start + 16, :
                ]


def spread_kernel(high_ref, low_ref, g_ref, out_ref, flow_ref):
    half = high_ref.shape[1] // 2
    lead = g_ref.shape[3] // 8
    modes = (half - lead) // 2
    total = [0.0] * 4
    for slab in range(2):
        parts = (high_ref[slab], low_ref[slab])
        real = mm3(parts, split(g_ref[slab, 0]), True)
        imag = mm3(parts, split(g_ref[slab, 1]), True)
        for sweep in range(2):
            base = sweep * half
            place = slab * 4 * lead + sweep * 2 * lead
            out_ref[0, place : place + lead, :] = real[base : base + lead]
            out_ref[0, place + lead : place + 2 * lead, :] = imag[base : base + lead]
            one, two, three = base + lead, base + lead + modes, base + half
            total[2 * sweep] += real[one:two] - imag[two:three]
            total[2 * sweep + 1] += real[two:three] + imag[one:two]
    for item in range(4):
        flow_ref[0, item * modes : (item + 1) * modes, :] = total[item]


def coupling_kernel(team_ref, c_ref, x_ref):
    left = team_ref[0] == 0
    size = c_ref.shape[3]
    for slab in range(2):
        x_ref[slab, :size] = jnp.where(left, c_ref[slab, 0].T, c_ref[slab, 0])
        x_ref[slab, size:] = jnp.where(left, c_ref[slab, 1].T, -c_ref[slab, 1])


def stacked(ref, start, count):
    return jnp.concatenate([ref[block, start : start + count, :] for block in range(8)], axis=0)


def pair_map_kernel(team_ref, recv_ref, x_ref, mask_ref, out_ref, qa_ref):
    left = team_ref[0] == 0
    size = x_ref.shape[2]
    lead = size // 8
    coupled = [(x_ref[slab, :size], x_ref[slab, size:]) for slab in range(2)]
    blocks = [
        (stacked(recv_ref, 2 * item * lead, lead), stacked(recv_ref, (2 * item + 1) * lead, lead))
        for item in range(2)
    ]
    flow = recv_ref[0, 4 * lead :, :]
    for block in range(1, 8):
        flow = flow + recv_ref[block, 4 * lead :, :]
    flow_a = jnp.where(mask_ref[0] != 0, flow, 0.0)
    flow_b = jnp.where(mask_ref[1] != 0, flow, 0.0)
    qa_ref[...] = flow_a

    def pick(one, two):
        return (jnp.where(left, one[0], two[0]), jnp.where(left, one[1], two[1]))

    def times(one, two):
        both = complex_rows(jnp.concatenate(one, axis=0), two)
        return both, (both[:size], both[size:])

    first, _ = times(pick(coupled[0], blocks[0]), pick(blocks[0], coupled[1]))
    _, second = times(pick(coupled[1], blocks[1]), pick(blocks[1], coupled[0]))
    out_ref[: 2 * size, :] = complex_rows(first, second)
    flow_a = jnp.where(left, flow_a, complex_rows(flow_a, coupled[1]))
    flow_b = jnp.where(left, flow_b, complex_rows(flow_b, coupled[0]))
    out_ref[2 * size :, :] = complex_rows(flow_a, second) + flow_b


def advance(state, maps_ref, index):
    size = maps_ref.shape[2]
    flow = complex_rows(state, (maps_ref[index, :size], maps_ref[index, size : 2 * size]))
    return flow + maps_ref[index, 2 * size :]


def row_kernel(info_ref, lead_ref, flow_ref, maps_ref, out_ref):
    state = jnp.where(info_ref[1] == 0, lead_ref[...], flow_ref[...])
    for item in range(4):
        state = advance(state, maps_ref, jnp.where(info_ref[0] == 0, item, 3 - item))
    out_ref[...] = state


def inflow_kernel(info_ref, lead_ref, flow_ref, maps_ref, recv_ref, x_ref, qa_ref, out_ref):
    size = x_ref.shape[2]
    lead = size // 8
    left = info_ref[0] == 0
    state = jnp.where(info_ref[1] == 0, lead_ref[...], flow_ref[...])
    for item in range(3):
        later = advance(state, maps_ref, jnp.where(left, item, 3 - item))
        state = jnp.where(item < info_ref[2], later, state)
    turned = complex_rows(state, (x_ref[0, :size], x_ref[0, size:]))
    inner_a = jnp.where(left, turned, state)
    block = (stacked(recv_ref, 0, lead), stacked(recv_ref, lead, lead))
    middle = complex_rows(inner_a, block) + qa_ref[...]
    inner_b = complex_rows(middle, (x_ref[1, :size], x_ref[1, size:]))
    for dest in range(8):
        out_ref[dest, :32, :] = inner_a
        out_ref[dest, 32:, :] = inner_b


def arrange_kernel(recv_ref, high_ref, low_ref):
    lead = recv_ref.shape[2] // 8
    for slab in range(2):
        for kind in range(4):
            value = stacked(recv_ref, (slab * 4 + kind) * lead, lead)
            high, low = split(value)
            sweep, part = divmod(kind, 2)
            high_ref[slab, sweep, part] = high
            low_ref[slab, sweep, part] = low


def state_kernel(
    first_ref, inject_ref, inner_ref, high_ref, low_ref, base_ref, left_ref, right_ref
):
    modes = inject_ref.shape[1]
    width = base_ref.shape[1]
    for sweep, out_ref in enumerate((left_ref, right_ref)):
        target = jnp.broadcast_to(
            inject_ref[sweep : sweep + 1, :].astype(F32), (width, modes)
        ).T
        for slab in range(2):
            item = slab if sweep == 0 else 1 - slab
            pieces = []
            for part in range(2):
                start = item * 32 + part * 16
                for member in range(4):
                    pieces.append(inner_ref[sweep * 4 + member, start : start + 16, :])
            parts = split(jnp.concatenate(pieces, axis=0))
            by = []
            for part in range(2):
                by.append(mm3(parts, (high_ref[slab, sweep, part], low_ref[slab, sweep, part])))
            chosen = target == (first_ref[0] + slab).astype(F32)
            for part in range(2):
                start = (2 * sweep + part) * modes
                base = jnp.where(chosen, base_ref[start : start + modes, :], 0.0)
                if part == 0:
                    out_ref[slab, part] = base + (by[0][:modes] - by[1][modes:])
                else:
                    out_ref[slab, part] = base + (by[1][:modes] + by[0][modes:])


def params(**extra):
    return pltpu.CompilerParams(vmem_limit_bytes=LIMIT, **extra)


def whole(shape):
    zeros = (0,) * len(shape)
    return pl.BlockSpec(shape, lambda *_: zeros)


SMEM = pl.BlockSpec(memory_space=pltpu.SMEM)
VMEM = pl.BlockSpec(memory_space=pltpu.VMEM)


def exchange(value):
    return lax.all_to_all(value, "col", split_axis=0, concat_axis=0, tiled=True)


def on_device(diag_inverse, couplings, sources, inject, leads):
    orbitals = diag_inverse.shape[2]
    width = diag_inverse.shape[3]
    size = couplings.shape[2]
    modes = sources.shape[3]
    lead = size // 8
    part_rows = orbitals // 8
    slabs = lax.axis_size("slab")
    slab_index = lax.axis_index("slab")
    col_index = lax.axis_index("col")
    team = col_index // 4
    member = col_index % 4
    first = jnp.reshape(slab_index * 2, (1,)).astype(jnp.int32)
    position = jnp.where(team == 0, slab_index, slabs - 1 - slab_index)
    info = jnp.stack([team, position // 4, position % 4]).astype(jnp.int32)
    stack = 2 * (lead + 2 * modes)
    block_rows = 4 * lead + 32
    sources = jnp.transpose(sources, (0, 1, 3, 2))
    leads = jnp.transpose(leads, (0, 1, 3, 2))

    sent, high, low = pl.pallas_call(
        interface_kernel,
        grid=(4,),
        in_specs=[
            SMEM,
            whole(inject.shape),
            whole(sources.shape),
            pl.BlockSpec((1, 1, orbitals, width // 2), lambda step: (step // 2, step % 2, 0, 0)),
            pl.BlockSpec((1, 1, orbitals, width // 2), lambda step: (step // 2, step % 2, 0, 1)),
        ],
        out_specs=[
            whole((8, block_rows, size)),
            whole((2, stack, width)),
            whole((2, stack, width)),
        ],
        out_shape=[
            jax.ShapeDtypeStruct((8, block_rows, size), F32),
            jax.ShapeDtypeStruct((2, stack, width), BF16),
            jax.ShapeDtypeStruct((2, stack, width), BF16),
        ],
        scratch_shapes=[pltpu.VMEM((2, 2 * modes, size), F32)],
        compiler_params=params(),
        name="interface_terms",
    )(first, inject, sources, diag_inverse, diag_inverse)
    received = exchange(sent)

    spread, flows = pl.pallas_call(
        spread_kernel,
        grid=(8,),
        in_specs=[
            whole((2, stack, width)),
            whole((2, stack, width)),
            pl.BlockSpec((2, 2, part_rows, width), lambda step: (0, 0, step, 0)),
        ],
        out_specs=[
            pl.BlockSpec((1, 8 * lead, part_rows), lambda step: (step, 0, 0)),
            pl.BlockSpec((1, 4 * modes, part_rows), lambda step: (step, 0, 0)),
        ],
        out_shape=[
            jax.ShapeDtypeStruct((8, 8 * lead, part_rows), F32),
            jax.ShapeDtypeStruct((8, 4 * modes, part_rows), F32),
        ],
        compiler_params=params(),
        name="spread_terms",
    )(high, low, diag_inverse)
    turned = pl.pallas_call(
        coupling_kernel,
        in_specs=[SMEM, VMEM],
        out_specs=VMEM,
        out_shape=jax.ShapeDtypeStruct((2, 2 * size, size), F32),
        compiler_params=params(),
        name="coupling_rows",
    )(info, couplings)
    own_inject = lax.dynamic_slice(inject, (team, member * 16), (1, 16))[0]
    own_inject = jnp.concatenate([own_inject, own_inject])
    marks = jnp.stack([own_inject == first[0] + team, own_inject == first[0] + 1 - team])
    marks = jnp.broadcast_to(marks.astype(F32)[:, :, None], (2, 32, size))
    own_lead = lax.dynamic_slice(leads, (team, 0, member * 16, 0), (1, 2, 16, size))
    own_lead = own_lead.reshape(32, size)
    received, spread, turned, marks, own_lead = lax.optimization_barrier(
        (received, spread, turned, marks, own_lead)
    )

    packed, flow_a = pl.pallas_call(
        pair_map_kernel,
        in_specs=[SMEM, VMEM, VMEM, VMEM],
        out_specs=[VMEM, VMEM],
        out_shape=[
            jax.ShapeDtypeStruct((2 * size + 32, size), F32),
            jax.ShapeDtypeStruct((32, size), F32),
        ],
        compiler_params=params(),
        name="pair_map",
    )(info, received, turned, marks)
    rows = exchange(spread)
    groups = [[4 * row + item for item in range(4)] for row in range(slabs // 4)]
    maps = lax.all_gather(packed, "slab", axis=0, axis_index_groups=groups)
    maps, flows = lax.optimization_barrier((maps, flows))
    base = lax.psum_scatter(flows, "col", scatter_dimension=0, tiled=False)

    cols = lax.axis_size("col")
    pairs = []
    for slab in range(slabs):
        for col in range(cols):
            target = (slab + (4 if col < 4 else -4)) % slabs
            pairs.append((slab * cols + col, target * cols + col))
    flow = own_lead
    for _ in range(slabs // 4 - 1):
        flow = pl.pallas_call(
            row_kernel,
            in_specs=[SMEM, VMEM, VMEM, VMEM],
            out_specs=VMEM,
            out_shape=jax.ShapeDtypeStruct((32, size), F32),
            compiler_params=params(),
            name="row_step",
        )(info, own_lead, flow, maps)
        flow = lax.ppermute(flow, ("slab", "col"), pairs)
    inner = pl.pallas_call(
        inflow_kernel,
        in_specs=[SMEM] + [VMEM] * 6,
        out_specs=VMEM,
        out_shape=jax.ShapeDtypeStruct((8, 64, size), F32),
        compiler_params=params(),
        name="inflow",
    )(info, own_lead, flow, maps, received, turned, flow_a)
    rows, inner = lax.optimization_barrier((rows, inner))
    inner = exchange(inner)
    row_high, row_low = pl.pallas_call(
        arrange_kernel,
        in_specs=[VMEM],
        out_specs=[VMEM, VMEM],
        out_shape=[
            jax.ShapeDtypeStruct((2, 2, 2, size, part_rows), BF16),
            jax.ShapeDtypeStruct((2, 2, 2, size, part_rows), BF16),
        ],
        compiler_params=params(),
        name="arrange_rows",
    )(rows)

    shape = (2, 2, modes, part_rows)
    left, right = pl.pallas_call(
        state_kernel,
        in_specs=[SMEM, VMEM, VMEM, VMEM, VMEM, VMEM],
        out_specs=[VMEM, VMEM],
        out_shape=[jax.ShapeDtypeStruct(shape, F32), jax.ShapeDtypeStruct(shape, F32)],
        compiler_params=params(),
        name="states",
    )(first, inject, inner, row_high, row_low, base)
    return jnp.transpose(left, (0, 1, 3, 2)), jnp.transpose(right, (0, 1, 3, 2))


def solution(mesh):
    placed = (
        P(("energy", "slab"), None, None, "col"),
        P(("energy", "slab"), None, None, None),
        P("energy", None, "col", None),
        P(),
        P("energy", None, None, None),
    )

    return jax.shard_map(
        on_device,
        mesh=mesh,
        in_specs=placed,
        out_specs=(
            P(("energy", "slab"), None, "col", None),
            P(("energy", "slab"), None, "col", None),
        ),
        check_vma=False,
    )
```

```python
import jax
import jax.numpy as jnp
from jax import lax
from jax.experimental import pallas as pl
from jax.experimental.pallas import tpu as pltpu
from jax.sharding import PartitionSpec as P

F32 = jnp.float32
BF16 = jnp.bfloat16
LIMIT = 48 * 1024 * 1024


def split(value):
    high = value.astype(BF16)
    return high, (value - high.astype(F32)).astype(BF16)


def mm(left, right, transposed=False):
    dims = (((1,), (1 if transposed else 0,)), ((), ()))
    return lax.dot_general(left, right, dims, preferred_element_type=F32)


def mm3(left, right, transposed=False):
    rows = left[0].shape[0]
    wide = mm(jnp.concatenate(left, axis=0), right[0], transposed)
    return wide[:rows] + (wide[rows:] + mm(left[0], right[1], transposed))


def complex_rows(left, right):
    half = left.shape[0] // 2
    parts = split(left)
    by_real = mm3(parts, split(right[0]))
    by_imag = mm3(parts, split(right[1]))
    return jnp.concatenate(
        [by_real[:half] - by_imag[half:], by_imag[:half] + by_real[half:]], axis=0
    )


def interface_kernel(
    first_ref, inject_ref, src_ref, g0_ref, g1_ref, out_ref, high_ref, low_ref, acc_ref
):
    step = pl.program_id(0)
    slab = step // 2
    plane = step % 2
    modes = src_ref.shape[2]
    width = src_ref.shape[3]

    @pl.when(step == 0)
    def _():
        rows = lax.broadcasted_iota(jnp.int32, (width // 8, width), 0)
        cols = lax.broadcasted_iota(jnp.int32, (width // 8, width), 1)
        targets = [
            jnp.broadcast_to(inject_ref[sweep : sweep + 1, :].astype(F32), (width, modes)).T
            for sweep in range(2)
        ]
        for local in range(2):
            pieces = []
            for sweep in range(2):
                pieces.append((cols == rows * 8 + sweep).astype(F32))
                chosen = targets[sweep] == (first_ref[0] + local).astype(F32)
                for part in range(2):
                    pieces.append(jnp.where(chosen, src_ref[sweep, part], 0.0))
            high, low = split(jnp.concatenate(pieces, axis=0))
            high_ref[local] = high
            low_ref[local] = low
        acc_ref[...] = jnp.zeros_like(acc_ref)

    half = high_ref.shape[1] // 2
    lead = width // 8
    count = g0_ref.shape[2] // 8
    for sweep in range(2):
        rows = jnp.concatenate(
            [ref[0, 0, pl.ds(1 - sweep, count, stride=8), :] for ref in (g0_ref, g1_ref)], axis=1
        )
        picked = pl.ds(sweep * half, half)
        term = mm3((high_ref[slab, picked, :], low_ref[slab, picked, :]), split(rows), True)
        order = slab if sweep == 0 else 1 - slab
        place = pl.ds(pl.multiple_of((order * 2 + plane) * lead, lead), lead)
        for member in range(4):
            out_ref[sweep * 4 + member, place, :] = term[:lead]
        real, imag = term[lead : lead + modes], term[lead + modes :]

        @pl.when(plane == 0)
        def _():
            acc_ref[sweep, :modes] += real
            acc_ref[sweep, modes:] += imag

        @pl.when(plane == 1)
        def _():
            acc_ref[sweep, :modes] -= imag
            acc_ref[sweep, modes:] += real

    @pl.when(step == 3)
    def _():
        for dest in range(8):
            sweep, member = divmod(dest, 4)
            for part in range(2):
                start = part * modes + member * 16
                out_ref[dest, 4 * lead + part * 16 : 4 * lead + (part + 1) * 16, :] = acc_ref[
                    sweep, start : start + 16, :
                ]


def spread_kernel(high_ref, low_ref, g_ref, out_ref, flow_ref):
    half = high_ref.shape[1] // 2
    lead = g_ref.shape[3] // 8
    modes = (half - lead) // 2
    total = [0.0] * 4
    for slab in range(2):
        parts = (high_ref[slab], low_ref[slab])
        real = mm3(parts, split(g_ref[slab, 0]), True)
        imag = mm3(parts, split(g_ref[slab, 1]), True)
        for sweep in range(2):
            base = sweep * half
            place = slab * 4 * lead + sweep * 2 * lead
            out_ref[0, place : place + lead, :] = real[base : base + lead]
            out_ref[0, place + lead : place + 2 * lead, :] = imag[base : base + lead]
            one, two, three = base + lead, base + lead + modes, base + half
            total[2 * sweep] += real[one:two] - imag[two:three]
            total[2 * sweep + 1] += real[two:three] + imag[one:two]
    for item in range(4):
        flow_ref[0, item * modes : (item + 1) * modes, :] = total[item]


def coupling_kernel(team_ref, c_ref, x_ref):
    left = team_ref[0] == 0
    size = c_ref.shape[3]
    for slab in range(2):
        x_ref[slab, :size] = jnp.where(left, c_ref[slab, 0].T, c_ref[slab, 0])
        x_ref[slab, size:] = jnp.where(left, c_ref[slab, 1].T, -c_ref[slab, 1])


def stacked(ref, start, count):
    return jnp.concatenate([ref[block, start : start + count, :] for block in range(8)], axis=0)


def pair_map_kernel(team_ref, recv_ref, x_ref, mask_ref, out_ref, qa_ref):
    left = team_ref[0] == 0
    size = x_ref.shape[2]
    lead = size // 8
    coupled = [(x_ref[slab, :size], x_ref[slab, size:]) for slab in range(2)]
    blocks = [
        (stacked(recv_ref, 2 * item * lead, lead), stacked(recv_ref, (2 * item + 1) * lead, lead))
        for item in range(2)
    ]
    flow = recv_ref[0, 4 * lead :, :]
    for block in range(1, 8):
        flow = flow + recv_ref[block, 4 * lead :, :]
    flow_a = jnp.where(mask_ref[0] != 0, flow, 0.0)
    flow_b = jnp.where(mask_ref[1] != 0, flow, 0.0)
    qa_ref[...] = flow_a

    def pick(one, two):
        return (jnp.where(left, one[0], two[0]), jnp.where(left, one[1], two[1]))

    def times(one, two):
        both = complex_rows(jnp.concatenate(one, axis=0), two)
        return both, (both[:size], both[size:])

    first, _ = times(pick(coupled[0], blocks[0]), pick(blocks[0], coupled[1]))
    _, second = times(pick(coupled[1], blocks[1]), pick(blocks[1], coupled[0]))
    out_ref[: 2 * size, :] = complex_rows(first, second)
    flow_a = jnp.where(left, flow_a, complex_rows(flow_a, coupled[1]))
    flow_b = jnp.where(left, flow_b, complex_rows(flow_b, coupled[0]))
    out_ref[2 * size :, :] = complex_rows(flow_a, second) + flow_b


def advance(state, maps, flow):
    size = maps[0].shape[1]
    half = state.shape[0] // 2
    parts = split(state)
    by_real = mm3(parts, tuple(ref[:size, :] for ref in maps))
    by_imag = mm3(parts, tuple(ref[size:, :] for ref in maps))
    moved = jnp.concatenate(
        [by_real[:half] - by_imag[half:], by_imag[:half] + by_real[half:]], axis=0
    )
    return moved + flow


def item_of(info_ref, item):
    return jnp.where(info_ref[0] == 0, item, 3 - item)


def row_state(info_ref, state, high_ref, low_ref, flow_ref):
    for item in range(4):
        index = item_of(info_ref, item)
        state = advance(state, (high_ref.at[index], low_ref.at[index]), flow_ref[index])
    return state


def gather_kernel(info_ref, lead_ref, own_ref, *refs):
    pieces, (high_ref, low_ref, flow_ref, out_ref) = refs[:6], refs[6:]
    size = own_ref.shape[1]
    half = pieces[0].shape[0]
    for shift in range(4):
        place = lax.rem(info_ref[3] + shift, 4)
        if shift == 0:
            top, bottom = own_ref[:half, :], own_ref[half:, :]
        else:
            top, bottom = pieces[2 * shift - 2][...], pieces[2 * shift - 1][...]
        rest = 2 * size - half
        high, low = split(top)
        high_ref[place, :half, :] = high
        low_ref[place, :half, :] = low
        high, low = split(bottom[:rest])
        high_ref[place, half:, :] = high
        low_ref[place, half:, :] = low
        flow_ref[place] = bottom[rest:]
    out_ref[...] = row_state(info_ref, lead_ref[...], high_ref, low_ref, flow_ref)


def row_kernel(info_ref, lead_ref, state_ref, high_ref, low_ref, flow_ref, out_ref):
    state = jnp.where(info_ref[1] == 0, lead_ref[...], state_ref[...])
    out_ref[...] = row_state(info_ref, state, high_ref, low_ref, flow_ref)


def inflow_kernel(
    info_ref,
    lead_ref,
    state_ref,
    high_ref,
    low_ref,
    flow_ref,
    recv_ref,
    x_ref,
    qa_ref,
    out_ref,
):
    size = x_ref.shape[2]
    lead = size // 8
    left = info_ref[0] == 0
    state = jnp.where(info_ref[1] == 0, lead_ref[...], state_ref[...])
    for item in range(3):
        index = item_of(info_ref, item)
        later = advance(state, (high_ref.at[index], low_ref.at[index]), flow_ref[index])
        state = jnp.where(item < info_ref[2], later, state)
    turned = complex_rows(state, (x_ref[0, :size], x_ref[0, size:]))
    inner_a = jnp.where(left, turned, state)
    block = (stacked(recv_ref, 0, lead), stacked(recv_ref, lead, lead))
    middle = complex_rows(inner_a, block) + qa_ref[...]
    inner_b = complex_rows(middle, (x_ref[1, :size], x_ref[1, size:]))
    for dest in range(8):
        out_ref[dest, :32, :] = inner_a
        out_ref[dest, 32:, :] = inner_b


def arrange_kernel(recv_ref, high_ref, low_ref):
    lead = recv_ref.shape[2] // 8
    for slab in range(2):
        for kind in range(4):
            value = stacked(recv_ref, (slab * 4 + kind) * lead, lead)
            high, low = split(value)
            sweep, part = divmod(kind, 2)
            high_ref[slab, sweep, part] = high
            low_ref[slab, sweep, part] = low


def state_kernel(
    first_ref, inject_ref, inner_ref, high_ref, low_ref, base_ref, left_ref, right_ref
):
    modes = inject_ref.shape[1]
    width = base_ref.shape[1]
    for sweep, out_ref in enumerate((left_ref, right_ref)):
        target = jnp.broadcast_to(
            inject_ref[sweep : sweep + 1, :].astype(F32), (width, modes)
        ).T
        for slab in range(2):
            item = slab if sweep == 0 else 1 - slab
            pieces = []
            for part in range(2):
                start = item * 32 + part * 16
                for member in range(4):
                    pieces.append(inner_ref[sweep * 4 + member, start : start + 16, :])
            parts = split(jnp.concatenate(pieces, axis=0))
            by = []
            for part in range(2):
                by.append(mm3(parts, (high_ref[slab, sweep, part], low_ref[slab, sweep, part])))
            chosen = target == (first_ref[0] + slab).astype(F32)
            for part in range(2):
                start = (2 * sweep + part) * modes
                base = jnp.where(chosen, base_ref[start : start + modes, :], 0.0)
                if part == 0:
                    out_ref[slab, part] = base + (by[0][:modes] - by[1][modes:])
                else:
                    out_ref[slab, part] = base + (by[1][:modes] + by[0][modes:])


def params(**extra):
    return pltpu.CompilerParams(vmem_limit_bytes=LIMIT, **extra)


def whole(shape):
    zeros = (0,) * len(shape)
    return pl.BlockSpec(shape, lambda *_: zeros)


SMEM = pl.BlockSpec(memory_space=pltpu.SMEM)
VMEM = pl.BlockSpec(memory_space=pltpu.VMEM)


def exchange(value):
    return lax.all_to_all(value, "col", split_axis=0, concat_axis=0, tiled=True)


def on_device(diag_inverse, couplings, sources, inject, leads):
    orbitals = diag_inverse.shape[2]
    width = diag_inverse.shape[3]
    size = couplings.shape[2]
    modes = sources.shape[3]
    lead = size // 8
    part_rows = orbitals // 8
    slabs = lax.axis_size("slab")
    slab_index = lax.axis_index("slab")
    col_index = lax.axis_index("col")
    team = col_index // 4
    member = col_index % 4
    first = jnp.reshape(slab_index * 2, (1,)).astype(jnp.int32)
    position = jnp.where(team == 0, slab_index, slabs - 1 - slab_index)
    info = jnp.stack([team, position // 4, position % 4, slab_index % 4]).astype(jnp.int32)
    stack = 2 * (lead + 2 * modes)
    block_rows = 4 * lead + 32
    sources = jnp.transpose(sources, (0, 1, 3, 2))
    leads = jnp.transpose(leads, (0, 1, 3, 2))

    sent, high, low = pl.pallas_call(
        interface_kernel,
        grid=(4,),
        in_specs=[
            SMEM,
            whole(inject.shape),
            whole(sources.shape),
            pl.BlockSpec((1, 1, orbitals, width // 2), lambda step: (step // 2, step % 2, 0, 0)),
            pl.BlockSpec((1, 1, orbitals, width // 2), lambda step: (step // 2, step % 2, 0, 1)),
        ],
        out_specs=[
            whole((8, block_rows, size)),
            whole((2, stack, width)),
            whole((2, stack, width)),
        ],
        out_shape=[
            jax.ShapeDtypeStruct((8, block_rows, size), F32),
            jax.ShapeDtypeStruct((2, stack, width), BF16),
            jax.ShapeDtypeStruct((2, stack, width), BF16),
        ],
        scratch_shapes=[pltpu.VMEM((2, 2 * modes, size), F32)],
        compiler_params=params(),
        name="interface_terms",
    )(first, inject, sources, diag_inverse, diag_inverse)
    received = exchange(sent)

    spread, flows = pl.pallas_call(
        spread_kernel,
        grid=(8,),
        in_specs=[
            whole((2, stack, width)),
            whole((2, stack, width)),
            pl.BlockSpec((2, 2, part_rows, width), lambda step: (0, 0, step, 0)),
        ],
        out_specs=[
            pl.BlockSpec((1, 8 * lead, part_rows), lambda step: (step, 0, 0)),
            pl.BlockSpec((1, 4 * modes, part_rows), lambda step: (step, 0, 0)),
        ],
        out_shape=[
            jax.ShapeDtypeStruct((8, 8 * lead, part_rows), F32),
            jax.ShapeDtypeStruct((8, 4 * modes, part_rows), F32),
        ],
        compiler_params=params(),
        name="spread_terms",
    )(high, low, diag_inverse)
    turned = pl.pallas_call(
        coupling_kernel,
        in_specs=[SMEM, VMEM],
        out_specs=VMEM,
        out_shape=jax.ShapeDtypeStruct((2, 2 * size, size), F32),
        compiler_params=params(),
        name="coupling_rows",
    )(info, couplings)
    own_inject = lax.dynamic_slice(inject, (team, member * 16), (1, 16))[0]
    own_inject = jnp.concatenate([own_inject, own_inject])
    marks = jnp.stack([own_inject == first[0] + team, own_inject == first[0] + 1 - team])
    marks = jnp.broadcast_to(marks.astype(F32)[:, :, None], (2, 32, size))
    own_lead = lax.dynamic_slice(leads, (team, 0, member * 16, 0), (1, 2, 16, size))
    own_lead = own_lead.reshape(32, size)
    received, spread, flows, turned, marks, own_lead = lax.optimization_barrier(
        (received, spread, flows, turned, marks, own_lead)
    )

    packed, flow_a = pl.pallas_call(
        pair_map_kernel,
        in_specs=[SMEM, VMEM, VMEM, VMEM],
        out_specs=[VMEM, VMEM],
        out_shape=[
            jax.ShapeDtypeStruct((2 * size + 32, size), F32),
            jax.ShapeDtypeStruct((32, size), F32),
        ],
        compiler_params=params(),
        name="pair_map",
    )(info, received, turned, marks)
    packed, spread = lax.optimization_barrier((packed, spread))
    rows = exchange(spread)
    base = lax.psum_scatter(flows, "col", scatter_dimension=0, tiled=False)

    def turn(value, step):
        return lax.ppermute(
            value, "slab", [(slab, slab // 4 * 4 + (slab + step) % 4) for slab in range(slabs)]
        )

    top, bottom = packed[: size + 16], packed[size + 16 :]
    before_top, after_bottom = turn(top, 1), turn(bottom, -1)
    before_bottom, after_top = turn(bottom, 1), turn(top, -1)
    across_top, across_bottom = turn(before_top, 1), turn(after_bottom, -1)
    pieces = (after_top, after_bottom, across_top, across_bottom, before_top, before_bottom)
    row_maps = [
        jax.ShapeDtypeStruct((4, 2 * size, size), BF16),
        jax.ShapeDtypeStruct((4, 2 * size, size), BF16),
        jax.ShapeDtypeStruct((4, 32, size), F32),
    ]
    state_shape = jax.ShapeDtypeStruct((32, size), F32)
    *maps, flow = pl.pallas_call(
        gather_kernel,
        in_specs=[SMEM] + [VMEM] * 8,
        out_specs=[VMEM] * 4,
        out_shape=row_maps + [state_shape],
        compiler_params=params(),
        name="gather_maps",
    )(info, own_lead, packed, *pieces)

    cols = lax.axis_size("col")
    pairs = []
    for slab in range(slabs):
        for col in range(cols):
            target = (slab + (4 if col < 4 else -4)) % slabs
            pairs.append((slab * cols + col, target * cols + col))
    flow = lax.ppermute(flow, ("slab", "col"), pairs)
    for _ in range(slabs // 4 - 2):
        flow = pl.pallas_call(
            row_kernel,
            in_specs=[SMEM] + [VMEM] * 5,
            out_specs=VMEM,
            out_shape=state_shape,
            compiler_params=params(),
            name="row_step",
        )(info, own_lead, flow, *maps)
        flow = lax.ppermute(flow, ("slab", "col"), pairs)
    inner = pl.pallas_call(
        inflow_kernel,
        in_specs=[SMEM] + [VMEM] * 8,
        out_specs=VMEM,
        out_shape=jax.ShapeDtypeStruct((8, 64, size), F32),
        compiler_params=params(),
        name="inflow",
    )(info, own_lead, flow, *maps, received, turned, flow_a)
    rows, inner = lax.optimization_barrier((rows, inner))
    inner = exchange(inner)
    row_high, row_low = pl.pallas_call(
        arrange_kernel,
        in_specs=[VMEM],
        out_specs=[VMEM, VMEM],
        out_shape=[
            jax.ShapeDtypeStruct((2, 2, 2, size, part_rows), BF16),
            jax.ShapeDtypeStruct((2, 2, 2, size, part_rows), BF16),
        ],
        compiler_params=params(),
        name="arrange_rows",
    )(rows)

    shape = (2, 2, modes, part_rows)
    left, right = pl.pallas_call(
        state_kernel,
        in_specs=[SMEM, VMEM, VMEM, VMEM, VMEM, VMEM],
        out_specs=[VMEM, VMEM],
        out_shape=[jax.ShapeDtypeStruct(shape, F32), jax.ShapeDtypeStruct(shape, F32)],
        compiler_params=params(),
        name="states",
    )(first, inject, inner, row_high, row_low, base)
    return jnp.transpose(left, (0, 1, 3, 2)), jnp.transpose(right, (0, 1, 3, 2))


def solution(mesh):
    placed = (
        P(("energy", "slab"), None, None, "col"),
        P(("energy", "slab"), None, None, None),
        P("energy", None, "col", None),
        P(),
        P("energy", None, None, None),
    )

    return jax.shard_map(
        on_device,
        mesh=mesh,
        in_specs=placed,
        out_specs=(
            P(("energy", "slab"), None, "col", None),
            P(("energy", "slab"), None, "col", None),
        ),
        check_vma=False,
    )
```

```python
import jax
import jax.numpy as jnp
from jax import lax
from jax.experimental import pallas as pl
from jax.experimental.pallas import tpu as pltpu
from jax.sharding import PartitionSpec as P

F32 = jnp.float32
BF16 = jnp.bfloat16
LIMIT = 48 * 1024 * 1024
PACK = 16


def split(value):
    high = value.astype(BF16)
    return high, (value - high.astype(F32)).astype(BF16)


def mm(left, right, transposed=False):
    dims = (((1,), (1 if transposed else 0,)), ((), ()))
    return lax.dot_general(left, right, dims, preferred_element_type=F32)


def mm3(left, right, transposed=False):
    rows = left[0].shape[0]
    wide = mm(jnp.concatenate(left, axis=0), right[0], transposed)
    return wide[:rows] + (wide[rows:] + mm(left[0], right[1], transposed))


def complex_rows(left, right):
    half = left.shape[0] // 2
    parts = split(left)
    by_real = mm3(parts, split(right[0]))
    by_imag = mm3(parts, split(right[1]))
    return jnp.concatenate(
        [by_real[:half] - by_imag[half:], by_imag[:half] + by_real[half:]], axis=0
    )


def interface_kernel(
    place_ref, inject_ref, src_ref, g0_ref, g1_ref, out_ref, high_ref, low_ref, acc_ref
):
    step = pl.program_id(0)
    slab = step // 2
    plane = step % 2
    modes = src_ref.shape[2]
    width = src_ref.shape[3]

    @pl.when(step == 0)
    def _():
        rows = lax.broadcasted_iota(jnp.int32, (width // 8, width), 0)
        cols = lax.broadcasted_iota(jnp.int32, (width // 8, width), 1)
        targets = [
            jnp.broadcast_to(inject_ref[sweep : sweep + 1, :].astype(F32), (width, modes)).T
            for sweep in range(2)
        ]
        for local in range(2):
            pieces = []
            for sweep in range(2):
                pieces.append((cols == rows * 8 + sweep).astype(F32))
                chosen = targets[sweep] == (place_ref[0] + local).astype(F32)
                for part in range(2):
                    pieces.append(jnp.where(chosen, src_ref[sweep, part], 0.0))
            high, low = split(jnp.concatenate(pieces, axis=0))
            high_ref[local] = high
            low_ref[local] = low
        acc_ref[...] = jnp.zeros_like(acc_ref)

    half = high_ref.shape[1] // 2
    lead = width // 8
    count = g0_ref.shape[2] // 8
    for sweep in range(2):
        rows = jnp.concatenate(
            [ref[0, 0, pl.ds(1 - sweep, count, stride=8), :] for ref in (g0_ref, g1_ref)], axis=1
        )
        picked = pl.ds(sweep * half, half)
        term = mm3((high_ref[slab, picked, :], low_ref[slab, picked, :]), split(rows), True)
        order = slab if sweep == 0 else 1 - slab
        place = pl.ds(pl.multiple_of((order * 2 + plane) * lead, lead), lead)
        for member in range(4):
            out_ref[sweep * 4 + member, place, :] = term[:lead]
        real, imag = term[lead : lead + modes], term[lead + modes :]

        @pl.when(plane == 0)
        def _():
            acc_ref[sweep, :modes] += real
            acc_ref[sweep, modes:] += imag

        @pl.when(plane == 1)
        def _():
            acc_ref[sweep, :modes] -= imag
            acc_ref[sweep, modes:] += real

    @pl.when(step == 3)
    def _():
        for dest in range(8):
            sweep, member = divmod(dest, 4)
            for part in range(2):
                start = part * modes + member * 16
                out_ref[dest, 4 * lead + part * 16 : 4 * lead + (part + 1) * 16, :] = acc_ref[
                    sweep, start : start + 16, :
                ]


def packed_columns(place_ref, inject_ref, sweep):
    modes = inject_ref.shape[1]
    target = inject_ref[sweep : sweep + 1, :]
    own = (target == place_ref[0]) | (target == place_ref[0] + 1)
    own = jnp.broadcast_to(own.astype(F32), (PACK, modes))
    earlier = lax.broadcasted_iota(jnp.int32, (modes, modes), 0)
    later = lax.broadcasted_iota(jnp.int32, (modes, modes), 1)
    rank = mm(own.astype(BF16), (earlier < later).astype(F32).astype(BF16))
    wanted = lax.broadcasted_iota(jnp.int32, (PACK, modes), 0) + PACK * place_ref[1]
    return jnp.where(rank == wanted.astype(F32), own, 0.0)


def unpacked_rows(place_ref, inject_ref, base_ref, sweep, part):
    back = packed_columns(place_ref, inject_ref, sweep).T.astype(BF16)
    start = (2 * sweep + part) * PACK
    high, low = split(base_ref[start : start + PACK, :])
    return mm(back, high) + mm(back, low)


def select_kernel(place_ref, inject_ref, src_ref, high_ref, low_ref):
    width = src_ref.shape[3]
    rows = lax.broadcasted_iota(jnp.int32, (width // 8, width), 0)
    cols = lax.broadcasted_iota(jnp.int32, (width // 8, width), 1)
    lead = width // 8
    for slab in range(2):
        for sweep in range(2):
            span = slice(sweep * lead, (sweep + 1) * lead)
            unit = (cols == rows * 8 + sweep).astype(F32)
            high_ref[slab, span, :] = unit.astype(BF16)
            low_ref[slab, span, :] = jnp.zeros_like(unit).astype(BF16)
            here = inject_ref[sweep : sweep + 1, :] == place_ref[0] + slab
            pick = jnp.where(here, packed_columns(place_ref, inject_ref, sweep), 0.0).astype(BF16)
            for part in range(2):
                start = 2 * lead + (2 * sweep + part) * PACK
                high, low = split(src_ref[sweep, part])
                high_ref[slab, start : start + PACK, :] = mm(pick, high).astype(BF16)
                low_ref[slab, start : start + PACK, :] = mm(pick, low).astype(BF16)


def spread_kernel(high_ref, low_ref, g_ref, out_ref, flow_ref):
    lead = g_ref.shape[3] // 8
    total = [0.0] * 4
    for slab in range(2):
        parts = (high_ref[slab], low_ref[slab])
        real = mm3(parts, split(g_ref[slab, 0]), True)
        imag = mm3(parts, split(g_ref[slab, 1]), True)
        for sweep in range(2):
            base = sweep * lead
            place = slab * 4 * lead + sweep * 2 * lead
            out_ref[0, place : place + lead, :] = real[base : base + lead]
            out_ref[0, place + lead : place + 2 * lead, :] = imag[base : base + lead]
            one = 2 * lead + 2 * sweep * PACK
            two, three = one + PACK, one + 2 * PACK
            total[2 * sweep] += real[one:two] - imag[two:three]
            total[2 * sweep + 1] += real[two:three] + imag[one:two]
    for item in range(4):
        flow_ref[0, item * PACK : (item + 1) * PACK, :] = total[item]


def expand_kernel(place_ref, inject_ref, base_ref, extra_ref, out_ref):
    modes = inject_ref.shape[1]
    for sweep in range(2):
        for part in range(2):
            span = slice((2 * sweep + part) * modes, (2 * sweep + part + 1) * modes)
            rows = unpacked_rows(place_ref, inject_ref, base_ref, sweep, part)
            out_ref[span, :] = extra_ref[span, :] + rows


def coupling_kernel(team_ref, c_ref, x_ref):
    left = team_ref[0] == 0
    size = c_ref.shape[3]
    for slab in range(2):
        x_ref[slab, :size] = jnp.where(left, c_ref[slab, 0].T, c_ref[slab, 0])
        x_ref[slab, size:] = jnp.where(left, c_ref[slab, 1].T, -c_ref[slab, 1])


def stacked(ref, start, count):
    return jnp.concatenate([ref[block, start : start + count, :] for block in range(8)], axis=0)


def pair_map_kernel(team_ref, recv_ref, x_ref, mask_ref, out_ref, qa_ref):
    left = team_ref[0] == 0
    size = x_ref.shape[2]
    lead = size // 8
    coupled = [(x_ref[slab, :size], x_ref[slab, size:]) for slab in range(2)]
    blocks = [
        (stacked(recv_ref, 2 * item * lead, lead), stacked(recv_ref, (2 * item + 1) * lead, lead))
        for item in range(2)
    ]
    flow = recv_ref[0, 4 * lead :, :]
    for block in range(1, 8):
        flow = flow + recv_ref[block, 4 * lead :, :]
    flow_a = jnp.where(mask_ref[0] != 0, flow, 0.0)
    flow_b = jnp.where(mask_ref[1] != 0, flow, 0.0)
    qa_ref[...] = flow_a

    def pick(one, two):
        return (jnp.where(left, one[0], two[0]), jnp.where(left, one[1], two[1]))

    def times(one, two):
        both = complex_rows(jnp.concatenate(one, axis=0), two)
        return both, (both[:size], both[size:])

    first, _ = times(pick(coupled[0], blocks[0]), pick(blocks[0], coupled[1]))
    _, second = times(pick(coupled[1], blocks[1]), pick(blocks[1], coupled[0]))
    out_ref[: 2 * size, :] = complex_rows(first, second)
    flow_a = jnp.where(left, flow_a, complex_rows(flow_a, coupled[1]))
    flow_b = jnp.where(left, flow_b, complex_rows(flow_b, coupled[0]))
    out_ref[2 * size :, :] = complex_rows(flow_a, second) + flow_b


def advance(state, maps, flow):
    size = maps[0].shape[1]
    half = state.shape[0] // 2
    parts = split(state)
    by_real = mm3(parts, tuple(ref[:size, :] for ref in maps))
    by_imag = mm3(parts, tuple(ref[size:, :] for ref in maps))
    moved = jnp.concatenate(
        [by_real[:half] - by_imag[half:], by_imag[:half] + by_real[half:]], axis=0
    )
    return moved + flow


def item_of(info_ref, item):
    return jnp.where(info_ref[0] == 0, item, 3 - item)


def row_state(info_ref, state, high_ref, low_ref, flow_ref):
    for item in range(4):
        index = item_of(info_ref, item)
        state = advance(state, (high_ref.at[index], low_ref.at[index]), flow_ref[index])
    return state


def gather_kernel(info_ref, lead_ref, own_ref, *refs):
    pieces, (high_ref, low_ref, flow_ref, out_ref) = refs[:6], refs[6:]
    size = own_ref.shape[1]
    half = pieces[0].shape[0]
    for shift in range(4):
        place = lax.rem(info_ref[3] + shift, 4)
        if shift == 0:
            top, bottom = own_ref[:half, :], own_ref[half:, :]
        else:
            top, bottom = pieces[2 * shift - 2][...], pieces[2 * shift - 1][...]
        rest = 2 * size - half
        high, low = split(top)
        high_ref[place, :half, :] = high
        low_ref[place, :half, :] = low
        high, low = split(bottom[:rest])
        high_ref[place, half:, :] = high
        low_ref[place, half:, :] = low
        flow_ref[place] = bottom[rest:]
    out_ref[...] = row_state(info_ref, lead_ref[...], high_ref, low_ref, flow_ref)


def row_kernel(info_ref, lead_ref, state_ref, high_ref, low_ref, flow_ref, out_ref):
    state = jnp.where(info_ref[1] == 0, lead_ref[...], state_ref[...])
    out_ref[...] = row_state(info_ref, state, high_ref, low_ref, flow_ref)


def inflow_kernel(
    info_ref,
    lead_ref,
    state_ref,
    high_ref,
    low_ref,
    flow_ref,
    recv_ref,
    x_ref,
    qa_ref,
    out_ref,
):
    size = x_ref.shape[2]
    lead = size // 8
    left = info_ref[0] == 0
    state = jnp.where(info_ref[1] == 0, lead_ref[...], state_ref[...])
    for item in range(3):
        index = item_of(info_ref, item)
        later = advance(state, (high_ref.at[index], low_ref.at[index]), flow_ref[index])
        state = jnp.where(item < info_ref[2], later, state)
    turned = complex_rows(state, (x_ref[0, :size], x_ref[0, size:]))
    inner_a = jnp.where(left, turned, state)
    block = (stacked(recv_ref, 0, lead), stacked(recv_ref, lead, lead))
    middle = complex_rows(inner_a, block) + qa_ref[...]
    inner_b = complex_rows(middle, (x_ref[1, :size], x_ref[1, size:]))
    for dest in range(8):
        out_ref[dest, :32, :] = inner_a
        out_ref[dest, 32:, :] = inner_b


def arrange_kernel(recv_ref, high_ref, low_ref):
    lead = recv_ref.shape[2] // 8
    for slab in range(2):
        for kind in range(4):
            value = stacked(recv_ref, (slab * 4 + kind) * lead, lead)
            high, low = split(value)
            sweep, part = divmod(kind, 2)
            high_ref[slab, sweep, part] = high
            low_ref[slab, sweep, part] = low


def state_kernel(
    place_ref, inject_ref, inner_ref, high_ref, low_ref, base_ref, extra_ref, left_ref, right_ref
):
    modes = inject_ref.shape[1]
    width = base_ref.shape[1]
    for sweep, out_ref in enumerate((left_ref, right_ref)):
        target = jnp.broadcast_to(
            inject_ref[sweep : sweep + 1, :].astype(F32), (width, modes)
        ).T
        bases = []
        for part in range(2):
            start = (2 * sweep + part) * modes
            rows = unpacked_rows(place_ref, inject_ref, base_ref, sweep, part)
            bases.append(rows + extra_ref[start : start + modes, :])
        for slab in range(2):
            item = slab if sweep == 0 else 1 - slab
            pieces = []
            for part in range(2):
                start = item * 32 + part * 16
                for member in range(4):
                    pieces.append(inner_ref[sweep * 4 + member, start : start + 16, :])
            parts = split(jnp.concatenate(pieces, axis=0))
            by = []
            for part in range(2):
                by.append(mm3(parts, (high_ref[slab, sweep, part], low_ref[slab, sweep, part])))
            chosen = target == (place_ref[0] + slab).astype(F32)
            for part in range(2):
                base = jnp.where(chosen, bases[part], 0.0)
                if part == 0:
                    out_ref[slab, part] = base + (by[0][:modes] - by[1][modes:])
                else:
                    out_ref[slab, part] = base + (by[1][:modes] + by[0][modes:])


def params(**extra):
    return pltpu.CompilerParams(vmem_limit_bytes=LIMIT, **extra)


def whole(shape):
    zeros = (0,) * len(shape)
    return pl.BlockSpec(shape, lambda *_: zeros)


SMEM = pl.BlockSpec(memory_space=pltpu.SMEM)
VMEM = pl.BlockSpec(memory_space=pltpu.VMEM)


def exchange(value):
    return lax.all_to_all(value, "col", split_axis=0, concat_axis=0, tiled=True)


def on_device(diag_inverse, couplings, sources, inject, leads):
    orbitals = diag_inverse.shape[2]
    width = diag_inverse.shape[3]
    size = couplings.shape[2]
    modes = sources.shape[3]
    lead = size // 8
    part_rows = orbitals // 8
    slabs = lax.axis_size("slab")
    slab_index = lax.axis_index("slab")
    col_index = lax.axis_index("col")
    team = col_index // 4
    member = col_index % 4
    first = slab_index * 2
    place = jnp.stack([first, jnp.zeros_like(first)]).astype(jnp.int32)
    position = jnp.where(team == 0, slab_index, slabs - 1 - slab_index)
    info = jnp.stack([team, position // 4, position % 4, slab_index % 4]).astype(jnp.int32)
    stack = 2 * (lead + 2 * modes)
    block_rows = 4 * lead + 32
    sources = jnp.transpose(sources, (0, 1, 3, 2))
    leads = jnp.transpose(leads, (0, 1, 3, 2))

    sent = pl.pallas_call(
        interface_kernel,
        grid=(4,),
        in_specs=[
            SMEM,
            whole(inject.shape),
            whole(sources.shape),
            pl.BlockSpec((1, 1, orbitals, width // 2), lambda step: (step // 2, step % 2, 0, 0)),
            pl.BlockSpec((1, 1, orbitals, width // 2), lambda step: (step // 2, step % 2, 0, 1)),
        ],
        out_specs=whole((8, block_rows, size)),
        out_shape=jax.ShapeDtypeStruct((8, block_rows, size), F32),
        scratch_shapes=[
            pltpu.VMEM((2, stack, width), BF16),
            pltpu.VMEM((2, stack, width), BF16),
            pltpu.VMEM((2, 2 * modes, size), F32),
        ],
        compiler_params=params(),
        name="interface_terms",
    )(place, inject, sources, diag_inverse, diag_inverse)
    sent, inject_after = lax.optimization_barrier((sent, inject))
    received = exchange(sent)

    def chunk_terms(place):
        terms = jax.ShapeDtypeStruct((2, 2 * lead + 4 * PACK, width), BF16)
        high, low = pl.pallas_call(
            select_kernel,
            in_specs=[SMEM, VMEM, VMEM],
            out_specs=[VMEM, VMEM],
            out_shape=[terms, terms],
            compiler_params=params(),
            name="select_terms",
        )(place, inject_after, sources)
        return pl.pallas_call(
            spread_kernel,
            grid=(8,),
            in_specs=[
                whole(terms.shape),
                whole(terms.shape),
                pl.BlockSpec((2, 2, part_rows, width), lambda step: (0, 0, step, 0)),
            ],
            out_specs=[
                pl.BlockSpec((1, 8 * lead, part_rows), lambda step: (step, 0, 0)),
                pl.BlockSpec((1, 4 * PACK, part_rows), lambda step: (step, 0, 0)),
            ],
            out_shape=[
                jax.ShapeDtypeStruct((8, 8 * lead, part_rows), F32),
                jax.ShapeDtypeStruct((8, 4 * PACK, part_rows), F32),
            ],
            compiler_params=params(),
            name="spread_terms",
        )(high, low, diag_inverse)

    def summed(flows):
        return lax.psum_scatter(flows, "col", scatter_dimension=0, tiled=False)

    spread, flows = chunk_terms(place)
    turned = pl.pallas_call(
        coupling_kernel,
        in_specs=[SMEM, VMEM],
        out_specs=VMEM,
        out_shape=jax.ShapeDtypeStruct((2, 2 * size, size), F32),
        compiler_params=params(),
        name="coupling_rows",
    )(info, couplings)
    own_inject = lax.dynamic_slice(inject, (team, member * 16), (1, 16))[0]
    own_inject = jnp.concatenate([own_inject, own_inject])
    marks = jnp.stack([own_inject == first + team, own_inject == first + 1 - team])
    marks = jnp.broadcast_to(marks.astype(F32)[:, :, None], (2, 32, size))
    own_lead = lax.dynamic_slice(leads, (team, 0, member * 16, 0), (1, 2, 16, size))
    own_lead = own_lead.reshape(32, size)
    received, spread, flows, turned, marks, own_lead = lax.optimization_barrier(
        (received, spread, flows, turned, marks, own_lead)
    )

    packed, flow_a = pl.pallas_call(
        pair_map_kernel,
        in_specs=[SMEM, VMEM, VMEM, VMEM],
        out_specs=[VMEM, VMEM],
        out_shape=[
            jax.ShapeDtypeStruct((2 * size + 32, size), F32),
            jax.ShapeDtypeStruct((32, size), F32),
        ],
        compiler_params=params(),
        name="pair_map",
    )(info, received, turned, marks)
    packed, spread = lax.optimization_barrier((packed, spread))
    rows = exchange(spread)
    base = summed(flows)

    def turn(value, step):
        return lax.ppermute(
            value, "slab", [(slab, slab // 4 * 4 + (slab + step) % 4) for slab in range(slabs)]
        )

    top, bottom = packed[: size + 16], packed[size + 16 :]
    before_top, after_bottom = turn(top, 1), turn(bottom, -1)
    before_top, after_bottom, top, bottom = lax.optimization_barrier(
        (before_top, after_bottom, top, bottom)
    )
    before_bottom, after_top = turn(bottom, 1), turn(top, -1)
    across_top, across_bottom = turn(before_top, 1), turn(after_bottom, -1)
    pieces = (after_top, after_bottom, across_top, across_bottom, before_top, before_bottom)
    row_maps = [
        jax.ShapeDtypeStruct((4, 2 * size, size), BF16),
        jax.ShapeDtypeStruct((4, 2 * size, size), BF16),
        jax.ShapeDtypeStruct((4, 32, size), F32),
    ]
    state_shape = jax.ShapeDtypeStruct((32, size), F32)
    *maps, flow = pl.pallas_call(
        gather_kernel,
        in_specs=[SMEM] + [VMEM] * 8,
        out_specs=[VMEM] * 4,
        out_shape=row_maps + [state_shape],
        compiler_params=params(),
        name="gather_maps",
    )(info, own_lead, packed, *pieces)

    cols = lax.axis_size("col")
    pairs = []
    for slab in range(slabs):
        for col in range(cols):
            target = (slab + (4 if col < 4 else -4)) % slabs
            pairs.append((slab * cols + col, target * cols + col))
    flow = lax.ppermute(flow, ("slab", "col"), pairs)
    for _ in range(slabs // 4 - 2):
        flow = pl.pallas_call(
            row_kernel,
            in_specs=[SMEM] + [VMEM] * 5,
            out_specs=VMEM,
            out_shape=state_shape,
            compiler_params=params(),
            name="row_step",
        )(info, own_lead, flow, *maps)
        flow = lax.ppermute(flow, ("slab", "col"), pairs)
    inner = pl.pallas_call(
        inflow_kernel,
        in_specs=[SMEM] + [VMEM] * 8,
        out_specs=VMEM,
        out_shape=jax.ShapeDtypeStruct((8, 64, size), F32),
        compiler_params=params(),
        name="inflow",
    )(info, own_lead, flow, *maps, received, turned, flow_a)
    rows, inner, base = lax.optimization_barrier((rows, inner, base))

    owners = jnp.arange(slabs, dtype=jnp.int32)[:, None, None]
    counts = jnp.sum((inject_after[None] >> 1 == owners).astype(jnp.int32), axis=2)
    chunks = (jnp.max(counts) + PACK - 1) // PACK

    def more(chunk, extra):
        place = jnp.stack([first, chunk]).astype(jnp.int32)
        _, flows = chunk_terms(place)
        return pl.pallas_call(
            expand_kernel,
            in_specs=[SMEM, VMEM, VMEM, VMEM],
            out_specs=VMEM,
            out_shape=jax.ShapeDtypeStruct((4 * modes, part_rows), F32),
            compiler_params=params(),
            name="expand_terms",
        )(place, inject, summed(flows), extra)

    extra = lax.fori_loop(1, chunks, more, jnp.zeros((4 * modes, part_rows), F32))
    inner = exchange(inner)
    row_high, row_low = pl.pallas_call(
        arrange_kernel,
        in_specs=[VMEM],
        out_specs=[VMEM, VMEM],
        out_shape=[
            jax.ShapeDtypeStruct((2, 2, 2, size, part_rows), BF16),
            jax.ShapeDtypeStruct((2, 2, 2, size, part_rows), BF16),
        ],
        compiler_params=params(),
        name="arrange_rows",
    )(rows)

    shape = (2, 2, modes, part_rows)
    left, right = pl.pallas_call(
        state_kernel,
        in_specs=[SMEM] + [VMEM] * 6,
        out_specs=[VMEM, VMEM],
        out_shape=[jax.ShapeDtypeStruct(shape, F32), jax.ShapeDtypeStruct(shape, F32)],
        compiler_params=params(),
        name="states",
    )(place, inject, inner, row_high, row_low, base, extra)
    return jnp.transpose(left, (0, 1, 3, 2)), jnp.transpose(right, (0, 1, 3, 2))


def solution(mesh):
    placed = (
        P(("energy", "slab"), None, None, "col"),
        P(("energy", "slab"), None, None, None),
        P("energy", None, "col", None),
        P(),
        P("energy", None, None, None),
    )

    return jax.shard_map(
        on_device,
        mesh=mesh,
        in_specs=placed,
        out_specs=(
            P(("energy", "slab"), None, "col", None),
            P(("energy", "slab"), None, "col", None),
        ),
        check_vma=False,
    )
```

```python
import jax
import jax.numpy as jnp
from jax import lax
from jax.experimental import pallas as pl
from jax.experimental.pallas import tpu as pltpu
from jax.sharding import PartitionSpec as P

F32 = jnp.float32
BF16 = jnp.bfloat16
LIMIT = 24 * 1024 * 1024
LARGE = 56 * 1024 * 1024
PACK = 16


def split(value):
    high = value.astype(BF16)
    return high, (value - high.astype(F32)).astype(BF16)


def mm(left, right, transposed=False):
    dims = (((1,), (1 if transposed else 0,)), ((), ()))
    return lax.dot_general(left, right, dims, preferred_element_type=F32)


def mm3(left, right, transposed=False):
    rows = left[0].shape[0]
    wide = mm(jnp.concatenate(left, axis=0), right[0], transposed)
    return wide[:rows] + (wide[rows:] + mm(left[0], right[1], transposed))


def combined(by_real, by_imag):
    half = by_real.shape[0] // 2
    return jnp.concatenate(
        [by_real[:half] - by_imag[half:], by_imag[:half] + by_real[half:]], axis=0
    )


def complex_rows(left, right):
    parts = split(left)
    return combined(mm3(parts, split(right[0])), mm3(parts, split(right[1])))


def times(left, right):
    size = right[0].shape[0] // 2
    by_real = mm3(left, (right[0][:size], right[1][:size]))
    by_imag = mm3(left, (right[0][size:], right[1][size:]))
    return combined(by_real, by_imag)


def interface_kernel(
    place_ref, inject_ref, src_ref, g0_ref, g1_ref, out_ref, high_ref, low_ref, acc_ref
):
    step = pl.program_id(0)
    slab = step // 2
    plane = step % 2
    modes = src_ref.shape[2]
    width = src_ref.shape[3]

    @pl.when(step == 0)
    def _():
        rows = lax.broadcasted_iota(jnp.int32, (width // 8, width), 0)
        cols = lax.broadcasted_iota(jnp.int32, (width // 8, width), 1)
        targets = [
            jnp.broadcast_to(inject_ref[sweep : sweep + 1, :].astype(F32), (width, modes)).T
            for sweep in range(2)
        ]
        for local in range(2):
            pieces = []
            for sweep in range(2):
                pieces.append((cols == rows * 8 + sweep).astype(F32))
                chosen = targets[sweep] == (place_ref[0] + local).astype(F32)
                for part in range(2):
                    pieces.append(jnp.where(chosen, src_ref[sweep, part], 0.0))
            high, low = split(jnp.concatenate(pieces, axis=0))
            high_ref[local] = high
            low_ref[local] = low
        acc_ref[...] = jnp.zeros_like(acc_ref)

    half = high_ref.shape[1] // 2
    lead = width // 8
    count = g0_ref.shape[2] // 8
    for sweep in range(2):
        rows = jnp.concatenate(
            [ref[0, 0, pl.ds(1 - sweep, count, stride=8), :] for ref in (g0_ref, g1_ref)], axis=1
        )
        picked = pl.ds(sweep * half, half)
        term = mm3((high_ref[slab, picked, :], low_ref[slab, picked, :]), split(rows), True)
        order = slab if sweep == 0 else 1 - slab
        place = pl.ds(pl.multiple_of((order * 2 + plane) * lead, lead), lead)
        for member in range(4):
            out_ref[sweep * 4 + member, place, :] = term[:lead]
        real, imag = term[lead : lead + modes], term[lead + modes :]

        @pl.when(plane == 0)
        def _():
            acc_ref[sweep, :modes] += real
            acc_ref[sweep, modes:] += imag

        @pl.when(plane == 1)
        def _():
            acc_ref[sweep, :modes] -= imag
            acc_ref[sweep, modes:] += real

    @pl.when(step == 3)
    def _():
        for dest in range(8):
            sweep, member = divmod(dest, 4)
            for part in range(2):
                start = part * modes + member * 16
                out_ref[dest, 4 * lead + part * 16 : 4 * lead + (part + 1) * 16, :] = acc_ref[
                    sweep, start : start + 16, :
                ]


def packed_columns(place_ref, inject_ref, sweep):
    modes = inject_ref.shape[1]
    target = inject_ref[sweep : sweep + 1, :]
    own = (target == place_ref[0]) | (target == place_ref[0] + 1)
    own = jnp.broadcast_to(own.astype(F32), (PACK, modes))
    earlier = lax.broadcasted_iota(jnp.int32, (modes, modes), 0)
    later = lax.broadcasted_iota(jnp.int32, (modes, modes), 1)
    rank = mm(own.astype(BF16), (earlier < later).astype(F32).astype(BF16))
    wanted = lax.broadcasted_iota(jnp.int32, (PACK, modes), 0) + PACK * place_ref[1]
    return jnp.where(rank == wanted.astype(F32), own, 0.0)


def unpacked_rows(place_ref, inject_ref, base_ref, sweep, part):
    back = packed_columns(place_ref, inject_ref, sweep).T.astype(BF16)
    start = (2 * sweep + part) * PACK
    high, low = split(base_ref[start : start + PACK, :])
    return mm(back, high) + mm(back, low)


def select_kernel(place_ref, inject_ref, src_ref, high_ref, low_ref):
    width = src_ref.shape[3]
    rows = lax.broadcasted_iota(jnp.int32, (width // 8, width), 0)
    cols = lax.broadcasted_iota(jnp.int32, (width // 8, width), 1)
    lead = width // 8
    for slab in range(2):
        for sweep in range(2):
            span = slice(sweep * lead, (sweep + 1) * lead)
            unit = (cols == rows * 8 + sweep).astype(F32)
            high_ref[slab, span, :] = unit.astype(BF16)
            low_ref[slab, span, :] = jnp.zeros_like(unit).astype(BF16)
            here = inject_ref[sweep : sweep + 1, :] == place_ref[0] + slab
            pick = jnp.where(here, packed_columns(place_ref, inject_ref, sweep), 0.0).astype(BF16)
            for part in range(2):
                start = 2 * lead + (2 * sweep + part) * PACK
                high, low = split(src_ref[sweep, part])
                high_ref[slab, start : start + PACK, :] = mm(pick, high).astype(BF16)
                low_ref[slab, start : start + PACK, :] = mm(pick, low).astype(BF16)


def spread_kernel(high_ref, low_ref, g_ref, out_ref, flow_ref):
    lead = g_ref.shape[3] // 8
    total = [0.0] * 4
    for slab in range(2):
        parts = (high_ref[slab], low_ref[slab])
        real = mm3(parts, split(g_ref[slab, 0]), True)
        imag = mm3(parts, split(g_ref[slab, 1]), True)
        for sweep in range(2):
            base = sweep * lead
            place = slab * 4 * lead + sweep * 2 * lead
            out_ref[0, place : place + lead, :] = real[base : base + lead]
            out_ref[0, place + lead : place + 2 * lead, :] = imag[base : base + lead]
            one = 2 * lead + 2 * sweep * PACK
            two, three = one + PACK, one + 2 * PACK
            total[2 * sweep] += real[one:two] - imag[two:three]
            total[2 * sweep + 1] += real[two:three] + imag[one:two]
    for item in range(4):
        flow_ref[0, item * PACK : (item + 1) * PACK, :] = total[item]


def expand_kernel(place_ref, inject_ref, base_ref, extra_ref, out_ref):
    modes = inject_ref.shape[1]
    for sweep in range(2):
        for part in range(2):
            span = slice((2 * sweep + part) * modes, (2 * sweep + part + 1) * modes)
            rows = unpacked_rows(place_ref, inject_ref, base_ref, sweep, part)
            out_ref[span, :] = extra_ref[span, :] + rows


def coupling_kernel(team_ref, c_ref, x_ref):
    left = team_ref[0] == 0
    size = c_ref.shape[3]
    for slab in range(2):
        x_ref[slab, :size] = jnp.where(left, c_ref[slab, 0].T, c_ref[slab, 0])
        x_ref[slab, size:] = jnp.where(left, c_ref[slab, 1].T, -c_ref[slab, 1])


def stacked(ref, start, count):
    return jnp.concatenate([ref[block, start : start + count, :] for block in range(8)], axis=0)


def pair_map_kernel(
    team_ref, recv_ref, x_ref, mask_ref, top_ref, bottom_ref, qa_ref, first_ref
):
    left = team_ref[0] == 0
    size = x_ref.shape[2]
    lead = size // 8
    coupled = [(x_ref[slab, :size], x_ref[slab, size:]) for slab in range(2)]
    blocks = [
        (stacked(recv_ref, 2 * item * lead, lead), stacked(recv_ref, (2 * item + 1) * lead, lead))
        for item in range(2)
    ]
    flow = recv_ref[0, 4 * lead :, :]
    for block in range(1, 8):
        flow = flow + recv_ref[block, 4 * lead :, :]
    flow_a = jnp.where(mask_ref[0] != 0, flow, 0.0)
    flow_b = jnp.where(mask_ref[1] != 0, flow, 0.0)
    qa_ref[...] = flow_a

    def pick(one, two):
        return (jnp.where(left, one[0], two[0]), jnp.where(left, one[1], two[1]))

    def product(one, two):
        return complex_rows(jnp.concatenate(one, axis=0), two)

    first = product(pick(coupled[0], blocks[0]), pick(blocks[0], coupled[1]))
    second = product(pick(coupled[1], blocks[1]), pick(blocks[1], coupled[0]))
    second = (second[:size], second[size:])
    first_ref[...] = first
    half = top_ref.shape[0]
    both = complex_rows(first, second)
    top_ref[...] = both[:half]
    bottom_ref[: 2 * size - half, :] = both[half:]
    flow_a = jnp.where(left, flow_a, complex_rows(flow_a, coupled[1]))
    flow_b = jnp.where(left, flow_b, complex_rows(flow_b, coupled[0]))
    bottom_ref[2 * size - half :, :] = complex_rows(flow_a, second) + flow_b


def after_kernel(value_ref, other_ref, out_ref):
    pass


def item_of(info_ref, item):
    return jnp.where(info_ref[0] == 0, item, 3 - item)


def entry_state(info_ref, lead_ref, state_ref):
    return jnp.where(info_ref[1] == 0, lead_ref[...], state_ref[...])


def gather_kernel(info_ref, lead_ref, *refs):
    pieces, (high_ref, low_ref, flow_ref, out_ref) = refs[:8], refs[8:]
    size = pieces[0].shape[1]
    half = pieces[0].shape[0]
    for shift in range(4):
        place = lax.rem(info_ref[3] + shift, 4)
        top, bottom = pieces[2 * shift][...], pieces[2 * shift + 1][...]
        rest = 2 * size - half
        high, low = split(top)
        high_ref[place, :half, :] = high
        low_ref[place, :half, :] = low
        high, low = split(bottom[:rest])
        high_ref[place, half:, :] = high
        low_ref[place, half:, :] = low
        flow_ref[place] = bottom[rest:]
    state = lead_ref[...]
    for item in range(4):
        index = item_of(info_ref, item)
        state = times(split(state), (high_ref[index], low_ref[index])) + flow_ref[index]
    out_ref[...] = state


def row_map_kernel(
    info_ref, high_ref, low_ref, flow_ref, row_high_ref, row_low_ref, row_flow_ref, half_ref
):
    maps, flows = [], []
    for item in range(4):
        index = item_of(info_ref, item)
        maps.append((high_ref[index], low_ref[index]))
        flows.append(flow_ref[index])
    size = high_ref.shape[2]
    early = times(maps[0], maps[1])
    early_flow = times(split(flows[0]), maps[1]) + flows[1]
    late = split(times(maps[2], maps[3]))
    late_flow = times(split(flows[2]), maps[3]) + flows[3]
    half_ref[: 2 * size, :] = early
    half_ref[2 * size :, :] = early_flow
    high, low = split(times(split(early), late))
    row_high_ref[...] = high
    row_low_ref[...] = low
    row_flow_ref[...] = times(split(early_flow), late) + late_flow


def row_kernel(info_ref, lead_ref, state_ref, high_ref, low_ref, flow_ref, out_ref):
    state = entry_state(info_ref, lead_ref, state_ref)
    out_ref[...] = times(split(state), (high_ref[...], low_ref[...])) + flow_ref[...]


def prefix_kernel(
    info_ref, high_ref, low_ref, flow_ref, half_ref, first_ref, x_ref, qa_ref, out_ref, inner_ref
):
    size = high_ref.shape[2]
    left = info_ref[0] == 0
    one, three = item_of(info_ref, 0), item_of(info_ref, 2)
    rows = lax.broadcasted_iota(jnp.int32, (2 * size + 32, size), 0)
    cols = lax.broadcasted_iota(jnp.int32, (2 * size + 32, size), 1)
    half = half_ref[...]
    third = (high_ref[three], low_ref[three])
    whole_row = times(split(half[: 2 * size]), third)
    whole_flow = times(split(half[2 * size :]), third) + flow_ref[three]
    none = (rows == cols).astype(F32)
    single = high_ref[one].astype(F32) + low_ref[one].astype(F32)
    single = jnp.concatenate([single, flow_ref[one]], axis=0)
    triple = jnp.concatenate([whole_row, whole_flow], axis=0)
    count = info_ref[2]
    low_half = jnp.where(count == 0, none, single)
    out_ref[...] = jnp.where(count < 2, low_half, jnp.where(count == 2, half, triple))
    second = split(x_ref[1])
    first = first_ref[...]
    inner_ref[: 2 * size, :] = jnp.where(left, times(split(first), second), first)
    inner_ref[2 * size :, :] = times(split(qa_ref[...]), second)


def entry_map_kernel(info_ref, prefix_ref, inner_ref, x_ref, high_ref, low_ref, flow_ref):
    size = x_ref.shape[2]
    left = info_ref[0] == 0
    prefix, flow = split(prefix_ref[: 2 * size, :]), split(prefix_ref[2 * size :, :])
    turn = split(x_ref[0])
    inner = split(inner_ref[: 2 * size, :])
    item_a = jnp.where(left, times(prefix, turn), prefix_ref[: 2 * size, :])
    flow_ref[0] = jnp.where(left, times(flow, turn), prefix_ref[2 * size :, :])
    item_b = times(prefix, inner)
    flow_ref[1] = times(flow, inner) + inner_ref[2 * size :, :]
    for item, value in enumerate((item_a, item_b)):
        high, low = split(value)
        high_ref[item] = high
        low_ref[item] = low


def inflow_kernel(info_ref, lead_ref, state_ref, high_ref, low_ref, flow_ref, out_ref):
    state = split(entry_state(info_ref, lead_ref, state_ref))
    for item in range(2):
        value = times(state, (high_ref[item], low_ref[item])) + flow_ref[item]
        for dest in range(8):
            out_ref[dest, 32 * item : 32 * (item + 1), :] = value


def arrange_kernel(
    place_ref, inject_ref, recv_ref, base_ref, extra_ref, high_ref, low_ref, out_ref
):
    lead = recv_ref.shape[2] // 8
    modes = inject_ref.shape[1]
    width = base_ref.shape[1]
    for slab in range(2):
        for kind in range(4):
            value = stacked(recv_ref, (slab * 4 + kind) * lead, lead)
            high, low = split(value)
            sweep, part = divmod(kind, 2)
            high_ref[slab, sweep, part] = high
            low_ref[slab, sweep, part] = low
    for sweep in range(2):
        target = jnp.broadcast_to(
            inject_ref[sweep : sweep + 1, :].astype(F32), (width, modes)
        ).T
        for part in range(2):
            start = (2 * sweep + part) * modes
            rows = unpacked_rows(place_ref, inject_ref, base_ref, sweep, part)
            rows = rows + extra_ref[start : start + modes, :]
            for slab in range(2):
                chosen = target == (place_ref[0] + slab).astype(F32)
                out_ref[sweep, slab, part] = jnp.where(chosen, rows, 0.0)


def state_kernel(inner_ref, high_ref, low_ref, base_ref, left_ref, right_ref):
    modes = base_ref.shape[3]
    for sweep, out_ref in enumerate((left_ref, right_ref)):
        for slab in range(2):
            item = slab if sweep == 0 else 1 - slab
            pieces = []
            for part in range(2):
                start = item * 32 + part * 16
                for member in range(4):
                    pieces.append(inner_ref[sweep * 4 + member, start : start + 16, :])
            parts = split(jnp.concatenate(pieces, axis=0))
            by = [
                mm3(parts, (high_ref[slab, sweep, part], low_ref[slab, sweep, part]))
                for part in range(2)
            ]
            value = combined(by[0], by[1])
            for part in range(2):
                rows = value[part * modes : (part + 1) * modes]
                out_ref[slab, part] = base_ref[sweep, slab, part] + rows


def params(limit=LIMIT):
    return pltpu.CompilerParams(vmem_limit_bytes=limit)


def whole(shape):
    zeros = (0,) * len(shape)
    return pl.BlockSpec(shape, lambda *_: zeros)


SMEM = pl.BlockSpec(memory_space=pltpu.SMEM)
VMEM = pl.BlockSpec(memory_space=pltpu.VMEM)
ANY = pl.BlockSpec(memory_space=pl.ANY)


def exchange(value):
    return lax.all_to_all(value, "col", split_axis=0, concat_axis=0, tiled=True)


def on_device(diag_inverse, couplings, sources, inject, leads):
    orbitals = diag_inverse.shape[2]
    width = diag_inverse.shape[3]
    size = couplings.shape[2]
    modes = sources.shape[3]
    lead = size // 8
    part_rows = orbitals // 8
    slabs = lax.axis_size("slab")
    slab_index = lax.axis_index("slab")
    col_index = lax.axis_index("col")
    team = col_index // 4
    member = col_index % 4
    first = slab_index * 2
    place = jnp.stack([first, jnp.zeros_like(first)]).astype(jnp.int32)
    position = jnp.where(team == 0, slab_index, slabs - 1 - slab_index)
    info = jnp.stack([team, position // 4, position % 4, slab_index % 4]).astype(jnp.int32)
    stack = 2 * (lead + 2 * modes)
    block_rows = 4 * lead + 32
    sources = jnp.transpose(sources, (0, 1, 3, 2))
    leads = jnp.transpose(leads, (0, 1, 3, 2))

    sent = pl.pallas_call(
        interface_kernel,
        grid=(4,),
        in_specs=[
            SMEM,
            whole(inject.shape),
            whole(sources.shape),
            pl.BlockSpec((1, 1, orbitals, width // 2), lambda step: (step // 2, step % 2, 0, 0)),
            pl.BlockSpec((1, 1, orbitals, width // 2), lambda step: (step // 2, step % 2, 0, 1)),
        ],
        out_specs=whole((8, block_rows, size)),
        out_shape=jax.ShapeDtypeStruct((8, block_rows, size), F32),
        scratch_shapes=[
            pltpu.VMEM((2, stack, width), BF16),
            pltpu.VMEM((2, stack, width), BF16),
            pltpu.VMEM((2, 2 * modes, size), F32),
        ],
        compiler_params=params(LARGE),
        name="interface_terms",
    )(place, inject, sources, diag_inverse, diag_inverse)
    sent, inject_after = lax.optimization_barrier((sent, inject))
    received = exchange(sent)

    def chunk_terms(place):
        terms = jax.ShapeDtypeStruct((2, 2 * lead + 4 * PACK, width), BF16)
        high, low = pl.pallas_call(
            select_kernel,
            in_specs=[SMEM, VMEM, VMEM],
            out_specs=[VMEM, VMEM],
            out_shape=[terms, terms],
            compiler_params=params(),
            name="select_terms",
        )(place, inject_after, sources)
        return pl.pallas_call(
            spread_kernel,
            grid=(8,),
            in_specs=[
                whole(terms.shape),
                whole(terms.shape),
                pl.BlockSpec((2, 2, part_rows, width), lambda step: (0, 0, step, 0)),
            ],
            out_specs=[
                pl.BlockSpec((1, 8 * lead, part_rows), lambda step: (step, 0, 0)),
                pl.BlockSpec((1, 4 * PACK, part_rows), lambda step: (step, 0, 0)),
            ],
            out_shape=[
                jax.ShapeDtypeStruct((8, 8 * lead, part_rows), F32),
                jax.ShapeDtypeStruct((8, 4 * PACK, part_rows), F32),
            ],
            compiler_params=params(LARGE),
            name="spread_terms",
        )(high, low, diag_inverse)

    def summed(flows):
        return lax.psum_scatter(flows, "col", scatter_dimension=0, tiled=False)

    spread, flows = chunk_terms(place)
    turned = pl.pallas_call(
        coupling_kernel,
        in_specs=[SMEM, VMEM],
        out_specs=VMEM,
        out_shape=jax.ShapeDtypeStruct((2, 2 * size, size), F32),
        compiler_params=params(),
        name="coupling_rows",
    )(info, couplings)
    own_inject = lax.dynamic_slice(inject, (team, member * 16), (1, 16))[0]
    own_inject = jnp.concatenate([own_inject, own_inject])
    marks = jnp.stack([own_inject == first + team, own_inject == first + 1 - team])
    marks = jnp.broadcast_to(marks.astype(F32)[:, :, None], (2, 32, size))
    own_lead = lax.dynamic_slice(leads, (team, 0, member * 16, 0), (1, 2, 16, size))
    own_lead = own_lead.reshape(32, size)
    base = summed(flows)
    owners = jnp.arange(slabs, dtype=jnp.int32)[:, None, None]
    counts = jnp.sum((inject_after[None] >> 1 == owners).astype(jnp.int32), axis=2)
    chunks = (jnp.max(counts) + PACK - 1) // PACK

    def more(chunk, extra):
        place = jnp.stack([first, chunk]).astype(jnp.int32)
        _, flows = chunk_terms(place)
        return pl.pallas_call(
            expand_kernel,
            in_specs=[SMEM, VMEM, VMEM, VMEM],
            out_specs=VMEM,
            out_shape=jax.ShapeDtypeStruct((4 * modes, part_rows), F32),
            compiler_params=params(),
            name="expand_terms",
        )(place, inject, summed(flows), extra)

    extra = lax.fori_loop(1, chunks, more, jnp.zeros((4 * modes, part_rows), F32))
    received, turned, marks, own_lead, spread, extra = lax.optimization_barrier(
        (received, turned, marks, own_lead, spread, extra)
    )

    top, bottom, flow_a, first_map = pl.pallas_call(
        pair_map_kernel,
        in_specs=[SMEM, VMEM, VMEM, VMEM],
        out_specs=[VMEM] * 4,
        out_shape=[
            jax.ShapeDtypeStruct((size + 16, size), F32),
            jax.ShapeDtypeStruct((size + 16, size), F32),
            jax.ShapeDtypeStruct((32, size), F32),
            jax.ShapeDtypeStruct((2 * size, size), F32),
        ],
        compiler_params=params(),
        name="pair_map",
    )(info, received, turned, marks)

    spread = pl.pallas_call(
        after_kernel,
        in_specs=[ANY, ANY],
        out_specs=ANY,
        out_shape=jax.ShapeDtypeStruct(spread.shape, F32),
        input_output_aliases={0: 0},
        name="after_pair_map",
    )(spread, bottom)
    rows = exchange(spread)

    def turn(value, step):
        return lax.ppermute(
            value, "slab", [(slab, slab // 4 * 4 + (slab + step) % 4) for slab in range(slabs)]
        )

    before_top, after_bottom = turn(top, 1), turn(bottom, -1)
    before_bottom, after_top = turn(bottom, 1), turn(top, -1)
    across_top, across_bottom = turn(before_top, 1), turn(after_bottom, -1)
    pieces = (after_top, after_bottom, across_top, across_bottom, before_top, before_bottom)
    row_maps = [
        jax.ShapeDtypeStruct((4, 2 * size, size), BF16),
        jax.ShapeDtypeStruct((4, 2 * size, size), BF16),
        jax.ShapeDtypeStruct((4, 32, size), F32),
    ]
    state_shape = jax.ShapeDtypeStruct((32, size), F32)
    *maps, flow = pl.pallas_call(
        gather_kernel,
        in_specs=[SMEM] + [VMEM] * 9,
        out_specs=[VMEM] * 4,
        out_shape=row_maps + [state_shape],
        compiler_params=params(),
        name="gather_maps",
    )(info, own_lead, top, bottom, *pieces)

    cols = lax.axis_size("col")
    pairs = []
    for slab in range(slabs):
        for col in range(cols):
            target = (slab + (4 if col < 4 else -4)) % slabs
            pairs.append((slab * cols + col, target * cols + col))

    def local(kernel, name, shapes, *args):
        single = not isinstance(shapes, list)
        return pl.pallas_call(
            kernel,
            in_specs=[SMEM] + [VMEM] * (len(args) - 1),
            out_specs=VMEM if single else [VMEM] * len(shapes),
            out_shape=shapes,
            compiler_params=params(),
            name=name,
        )(*args)

    def hop(value):
        return lax.ppermute(value, ("slab", "col"), pairs)

    full = jax.ShapeDtypeStruct((2 * size + 32, size), F32)
    half_map = jax.ShapeDtypeStruct((2 * size, size), BF16)
    flow = hop(flow)
    *row_map, half_row = local(
        row_map_kernel, "row_map", [half_map, half_map, state_shape, full], info, *maps
    )
    flow = local(row_kernel, "row_step", state_shape, info, own_lead, flow, *row_map)
    flow, half_row = lax.optimization_barrier((flow, half_row))
    flow = hop(flow)
    prefix, inner_map = local(
        prefix_kernel, "prefix_map", [full, full], info, *maps, half_row, first_map, turned, flow_a
    )
    flow = local(row_kernel, "row_step", state_shape, info, own_lead, flow, *row_map)
    flow, prefix, inner_map = lax.optimization_barrier((flow, prefix, inner_map))
    flow = hop(flow)
    two_maps = [
        jax.ShapeDtypeStruct((2, 2 * size, size), BF16),
        jax.ShapeDtypeStruct((2, 2 * size, size), BF16),
        jax.ShapeDtypeStruct((2, 32, size), F32),
    ]
    entry = local(entry_map_kernel, "entry_map", two_maps, info, prefix, inner_map, turned)
    inner = local(
        inflow_kernel,
        "inflow",
        jax.ShapeDtypeStruct((8, 64, size), F32),
        info,
        own_lead,
        flow,
        *entry,
    )
    rows, inner, base = lax.optimization_barrier((rows, inner, base))

    inner = exchange(inner)
    arranged = [
        jax.ShapeDtypeStruct((2, 2, 2, size, part_rows), BF16),
        jax.ShapeDtypeStruct((2, 2, 2, size, part_rows), BF16),
        jax.ShapeDtypeStruct((2, 2, 2, modes, part_rows), F32),
    ]
    arranged = local(
        arrange_kernel, "arrange_rows", arranged, place, inject, rows, base, extra
    )

    shape = (2, 2, modes, part_rows)
    left, right = pl.pallas_call(
        state_kernel,
        in_specs=[VMEM] * 4,
        out_specs=[VMEM, VMEM],
        out_shape=[jax.ShapeDtypeStruct(shape, F32), jax.ShapeDtypeStruct(shape, F32)],
        compiler_params=params(),
        name="states",
    )(inner, *arranged)
    return jnp.transpose(left, (0, 1, 3, 2)), jnp.transpose(right, (0, 1, 3, 2))


def solution(mesh):
    placed = (
        P(("energy", "slab"), None, None, "col"),
        P(("energy", "slab"), None, None, None),
        P("energy", None, "col", None),
        P(),
        P("energy", None, None, None),
    )

    return jax.shard_map(
        on_device,
        mesh=mesh,
        in_specs=placed,
        out_specs=(
            P(("energy", "slab"), None, "col", None),
            P(("energy", "slab"), None, "col", None),
        ),
        check_vma=False,
    )
```

```python
import jax
import jax.numpy as jnp
from jax import lax
from jax.experimental import pallas as pl
from jax.experimental.pallas import tpu as pltpu
from jax.sharding import PartitionSpec as P

F32 = jnp.float32
BF16 = jnp.bfloat16
LIMIT = 24 * 1024 * 1024
LARGE = 56 * 1024 * 1024
PACK = 16


def split(value):
    high = value.astype(BF16)
    return high, (value - high.astype(F32)).astype(BF16)


def mm(left, right, transposed=False):
    dims = (((1,), (1 if transposed else 0,)), ((), ()))
    return lax.dot_general(left, right, dims, preferred_element_type=F32)


def mm3(left, right, transposed=False):
    rows = left[0].shape[0]
    wide = mm(jnp.concatenate(left, axis=0), right[0], transposed)
    return wide[:rows] + (wide[rows:] + mm(left[0], right[1], transposed))


def combined(by_real, by_imag):
    half = by_real.shape[0] // 2
    return jnp.concatenate(
        [by_real[:half] - by_imag[half:], by_imag[:half] + by_real[half:]], axis=0
    )


def complex_rows(left, right):
    parts = split(left)
    return combined(mm3(parts, split(right[0])), mm3(parts, split(right[1])))


def times(left, right):
    size = right[0].shape[0] // 2
    by_real = mm3(left, (right[0][:size], right[1][:size]))
    by_imag = mm3(left, (right[0][size:], right[1][size:]))
    return combined(by_real, by_imag)


def interface_kernel(
    place_ref, inject_ref, src_ref, g0_ref, g1_ref, out_ref, high_ref, low_ref, acc_ref
):
    step = pl.program_id(0)
    slab = step // 2
    plane = step % 2
    modes = src_ref.shape[2]
    width = src_ref.shape[3]

    @pl.when(step == 0)
    def _():
        rows = lax.broadcasted_iota(jnp.int32, (width // 8, width), 0)
        cols = lax.broadcasted_iota(jnp.int32, (width // 8, width), 1)
        targets = [
            jnp.broadcast_to(inject_ref[sweep : sweep + 1, :].astype(F32), (width, modes)).T
            for sweep in range(2)
        ]
        for local in range(2):
            pieces = []
            for sweep in range(2):
                pieces.append((cols == rows * 8 + sweep).astype(F32))
                chosen = targets[sweep] == (place_ref[0] + local).astype(F32)
                for part in range(2):
                    pieces.append(jnp.where(chosen, src_ref[sweep, part], 0.0))
            high, low = split(jnp.concatenate(pieces, axis=0))
            high_ref[local] = high
            low_ref[local] = low
        acc_ref[...] = jnp.zeros_like(acc_ref)

    half = high_ref.shape[1] // 2
    lead = width // 8
    count = g0_ref.shape[2] // 8
    for sweep in range(2):
        rows = jnp.concatenate(
            [ref[0, 0, pl.ds(1 - sweep, count, stride=8), :] for ref in (g0_ref, g1_ref)], axis=1
        )
        picked = pl.ds(sweep * half, half)
        term = mm3((high_ref[slab, picked, :], low_ref[slab, picked, :]), split(rows), True)
        order = slab if sweep == 0 else 1 - slab
        place = pl.ds(pl.multiple_of((order * 2 + plane) * lead, lead), lead)
        for member in range(4):
            out_ref[sweep * 4 + member, place, :] = term[:lead]
        real, imag = term[lead : lead + modes], term[lead + modes :]

        @pl.when(plane == 0)
        def _():
            acc_ref[sweep, :modes] += real
            acc_ref[sweep, modes:] += imag

        @pl.when(plane == 1)
        def _():
            acc_ref[sweep, :modes] -= imag
            acc_ref[sweep, modes:] += real

    @pl.when(step == 3)
    def _():
        for dest in range(8):
            sweep, member = divmod(dest, 4)
            for part in range(2):
                start = part * modes + member * 16
                out_ref[dest, 4 * lead + part * 16 : 4 * lead + (part + 1) * 16, :] = acc_ref[
                    sweep, start : start + 16, :
                ]


def packed_columns(place_ref, inject_ref, sweep):
    modes = inject_ref.shape[1]
    target = inject_ref[sweep : sweep + 1, :]
    own = (target == place_ref[0]) | (target == place_ref[0] + 1)
    own = jnp.broadcast_to(own.astype(F32), (PACK, modes))
    earlier = lax.broadcasted_iota(jnp.int32, (modes, modes), 0)
    later = lax.broadcasted_iota(jnp.int32, (modes, modes), 1)
    rank = mm(own.astype(BF16), (earlier < later).astype(F32).astype(BF16))
    wanted = lax.broadcasted_iota(jnp.int32, (PACK, modes), 0) + PACK * place_ref[1]
    return jnp.where(rank == wanted.astype(F32), own, 0.0)


def unpacked_rows(place_ref, inject_ref, base_ref, sweep, part):
    back = packed_columns(place_ref, inject_ref, sweep).T.astype(BF16)
    start = (2 * sweep + part) * PACK
    high, low = split(base_ref[start : start + PACK, :])
    return mm(back, high) + mm(back, low)


def select_kernel(place_ref, inject_ref, src_ref, high_ref, low_ref):
    width = src_ref.shape[3]
    rows = lax.broadcasted_iota(jnp.int32, (width // 8, width), 0)
    cols = lax.broadcasted_iota(jnp.int32, (width // 8, width), 1)
    lead = width // 8
    for slab in range(2):
        for sweep in range(2):
            span = slice(sweep * lead, (sweep + 1) * lead)
            unit = (cols == rows * 8 + sweep).astype(F32)
            high_ref[slab, span, :] = unit.astype(BF16)
            low_ref[slab, span, :] = jnp.zeros_like(unit).astype(BF16)
            here = inject_ref[sweep : sweep + 1, :] == place_ref[0] + slab
            pick = jnp.where(here, packed_columns(place_ref, inject_ref, sweep), 0.0).astype(BF16)
            for part in range(2):
                start = 2 * lead + (2 * sweep + part) * PACK
                high, low = split(src_ref[sweep, part])
                high_ref[slab, start : start + PACK, :] = mm(pick, high).astype(BF16)
                low_ref[slab, start : start + PACK, :] = mm(pick, low).astype(BF16)


def spread_kernel(high_ref, low_ref, g_ref, early_ref, late_ref, flow_ref):
    lead = g_ref.shape[3] // 8
    total = [0.0] * 4
    for slab in range(2):
        parts = (high_ref[slab], low_ref[slab])
        real = mm3(parts, split(g_ref[slab, 0]), True)
        imag = mm3(parts, split(g_ref[slab, 1]), True)
        for sweep in range(2):
            base = sweep * lead
            place = slab * 4 * lead + sweep * 2 * lead
            out_ref = early_ref
            if slab == 1 and sweep == 1:
                out_ref, place = late_ref, 0
            out_ref[0, place : place + lead, :] = real[base : base + lead]
            out_ref[0, place + lead : place + 2 * lead, :] = imag[base : base + lead]
            one = 2 * lead + 2 * sweep * PACK
            two, three = one + PACK, one + 2 * PACK
            total[2 * sweep] += real[one:two] - imag[two:three]
            total[2 * sweep + 1] += real[two:three] + imag[one:two]
    for item in range(4):
        flow_ref[0, item * PACK : (item + 1) * PACK, :] = total[item]


def expand_kernel(place_ref, inject_ref, base_ref, extra_ref, out_ref):
    modes = inject_ref.shape[1]
    for sweep in range(2):
        for part in range(2):
            span = slice((2 * sweep + part) * modes, (2 * sweep + part + 1) * modes)
            rows = unpacked_rows(place_ref, inject_ref, base_ref, sweep, part)
            out_ref[span, :] = extra_ref[span, :] + rows


def coupling_kernel(team_ref, c_ref, x_ref):
    left = team_ref[0] == 0
    size = c_ref.shape[3]
    for slab in range(2):
        x_ref[slab, :size] = jnp.where(left, c_ref[slab, 0].T, c_ref[slab, 0])
        x_ref[slab, size:] = jnp.where(left, c_ref[slab, 1].T, -c_ref[slab, 1])


def stacked(ref, start, count):
    return jnp.concatenate([ref[block, start : start + count, :] for block in range(8)], axis=0)


def pair_map_kernel(
    team_ref, recv_ref, x_ref, mask_ref, top_ref, bottom_ref, qa_ref, first_ref
):
    left = team_ref[0] == 0
    size = x_ref.shape[2]
    lead = size // 8
    coupled = [(x_ref[slab, :size], x_ref[slab, size:]) for slab in range(2)]
    blocks = [
        (stacked(recv_ref, 2 * item * lead, lead), stacked(recv_ref, (2 * item + 1) * lead, lead))
        for item in range(2)
    ]
    flow = recv_ref[0, 4 * lead :, :]
    for block in range(1, 8):
        flow = flow + recv_ref[block, 4 * lead :, :]
    flow_a = jnp.where(mask_ref[0] != 0, flow, 0.0)
    flow_b = jnp.where(mask_ref[1] != 0, flow, 0.0)
    qa_ref[...] = flow_a

    def pick(one, two):
        return (jnp.where(left, one[0], two[0]), jnp.where(left, one[1], two[1]))

    def product(one, two):
        return complex_rows(jnp.concatenate(one, axis=0), two)

    first = product(pick(coupled[0], blocks[0]), pick(blocks[0], coupled[1]))
    second = product(pick(coupled[1], blocks[1]), pick(blocks[1], coupled[0]))
    second = (second[:size], second[size:])
    first_ref[...] = first
    half = top_ref.shape[0]
    both = complex_rows(first, second)
    top_ref[...] = both[:half]
    bottom_ref[: 2 * size - half, :] = both[half:]
    flow_a = jnp.where(left, flow_a, complex_rows(flow_a, coupled[1]))
    flow_b = jnp.where(left, flow_b, complex_rows(flow_b, coupled[0]))
    bottom_ref[2 * size - half :, :] = complex_rows(flow_a, second) + flow_b


def item_of(info_ref, item):
    return jnp.where(info_ref[0] == 0, item, 3 - item)


def entry_state(info_ref, lead_ref, state_ref):
    return jnp.where(info_ref[1] == 0, lead_ref[...], state_ref[...])


def gather_kernel(info_ref, lead_ref, *refs):
    pieces, (high_ref, low_ref, flow_ref, out_ref) = refs[:8], refs[8:]
    size = pieces[0].shape[1]
    half = pieces[0].shape[0]
    for shift in range(4):
        place = lax.rem(info_ref[3] + shift, 4)
        top, bottom = pieces[2 * shift][...], pieces[2 * shift + 1][...]
        rest = 2 * size - half
        high, low = split(top)
        high_ref[place, :half, :] = high
        low_ref[place, :half, :] = low
        high, low = split(bottom[:rest])
        high_ref[place, half:, :] = high
        low_ref[place, half:, :] = low
        flow_ref[place] = bottom[rest:]
    state = lead_ref[...]
    for item in range(4):
        index = item_of(info_ref, item)
        state = times(split(state), (high_ref[index], low_ref[index])) + flow_ref[index]
    out_ref[...] = state


def row_map_kernel(
    info_ref, high_ref, low_ref, flow_ref, row_high_ref, row_low_ref, row_flow_ref, half_ref
):
    maps, flows = [], []
    for item in range(4):
        index = item_of(info_ref, item)
        maps.append((high_ref[index], low_ref[index]))
        flows.append(flow_ref[index])
    size = high_ref.shape[2]
    early = times(maps[0], maps[1])
    early_flow = times(split(flows[0]), maps[1]) + flows[1]
    late = split(times(maps[2], maps[3]))
    late_flow = times(split(flows[2]), maps[3]) + flows[3]
    half_ref[: 2 * size, :] = early
    half_ref[2 * size :, :] = early_flow
    high, low = split(times(split(early), late))
    row_high_ref[...] = high
    row_low_ref[...] = low
    row_flow_ref[...] = times(split(early_flow), late) + late_flow


def row_kernel(info_ref, lead_ref, state_ref, high_ref, low_ref, flow_ref, out_ref):
    state = entry_state(info_ref, lead_ref, state_ref)
    out_ref[...] = times(split(state), (high_ref[...], low_ref[...])) + flow_ref[...]


def prefix_kernel(
    info_ref, high_ref, low_ref, flow_ref, half_ref, first_ref, x_ref, qa_ref, out_ref, inner_ref
):
    size = high_ref.shape[2]
    left = info_ref[0] == 0
    one, three = item_of(info_ref, 0), item_of(info_ref, 2)
    rows = lax.broadcasted_iota(jnp.int32, (2 * size + 32, size), 0)
    cols = lax.broadcasted_iota(jnp.int32, (2 * size + 32, size), 1)
    half = half_ref[...]
    third = (high_ref[three], low_ref[three])
    whole_row = times(split(half[: 2 * size]), third)
    whole_flow = times(split(half[2 * size :]), third) + flow_ref[three]
    none = (rows == cols).astype(F32)
    single = high_ref[one].astype(F32) + low_ref[one].astype(F32)
    single = jnp.concatenate([single, flow_ref[one]], axis=0)
    triple = jnp.concatenate([whole_row, whole_flow], axis=0)
    count = info_ref[2]
    low_half = jnp.where(count == 0, none, single)
    out_ref[...] = jnp.where(count < 2, low_half, jnp.where(count == 2, half, triple))
    second = split(x_ref[1])
    first = first_ref[...]
    inner_ref[: 2 * size, :] = jnp.where(left, times(split(first), second), first)
    inner_ref[2 * size :, :] = times(split(qa_ref[...]), second)


def entry_map_kernel(info_ref, prefix_ref, inner_ref, x_ref, high_ref, low_ref, flow_ref):
    size = x_ref.shape[2]
    left = info_ref[0] == 0
    prefix, flow = split(prefix_ref[: 2 * size, :]), split(prefix_ref[2 * size :, :])
    turn = split(x_ref[0])
    inner = split(inner_ref[: 2 * size, :])
    item_a = jnp.where(left, times(prefix, turn), prefix_ref[: 2 * size, :])
    flow_ref[0] = jnp.where(left, times(flow, turn), prefix_ref[2 * size :, :])
    item_b = times(prefix, inner)
    flow_ref[1] = times(flow, inner) + inner_ref[2 * size :, :]
    for item, value in enumerate((item_a, item_b)):
        high, low = split(value)
        high_ref[item] = high
        low_ref[item] = low


def inflow_kernel(
    info_ref, lead_ref, state_ref, high_ref, low_ref, flow_ref, spread_ref, out_ref
):
    out_ref[:, 64:, :] = spread_ref[...]
    state = split(entry_state(info_ref, lead_ref, state_ref))
    for item in range(2):
        value = times(state, (high_ref[item], low_ref[item])) + flow_ref[item]
        for dest in range(8):
            out_ref[dest, 32 * item : 32 * (item + 1), :] = value


def state_kernel(
    place_ref, inject_ref, last_ref, rows_ref, base_ref, extra_ref, left_ref, right_ref
):
    modes = inject_ref.shape[1]
    width = base_ref.shape[1]
    lead = rows_ref.shape[1] // 6
    for sweep, out_ref in enumerate((left_ref, right_ref)):
        target = jnp.broadcast_to(
            inject_ref[sweep : sweep + 1, :].astype(F32), (width, modes)
        ).T
        bases = []
        for part in range(2):
            start = (2 * sweep + part) * modes
            rows = unpacked_rows(place_ref, inject_ref, base_ref, sweep, part)
            bases.append(rows + extra_ref[start : start + modes, :])
        for slab in range(2):
            item = slab if sweep == 0 else 1 - slab
            pieces = []
            for part in range(2):
                start = item * 32 + part * 16
                for member in range(4):
                    pieces.append(last_ref[sweep * 4 + member, start : start + 16, :])
            parts = split(jnp.concatenate(pieces, axis=0))
            by = []
            for part in range(2):
                kind = 2 * sweep + part
                if slab == 1 and sweep == 1:
                    matrix = stacked(last_ref, 64 + part * lead, lead)
                else:
                    matrix = stacked(rows_ref, (4 * slab + kind) * lead, lead)
                by.append(mm3(parts, split(matrix)))
            value = combined(by[0], by[1])
            chosen = target == (place_ref[0] + slab).astype(F32)
            for part in range(2):
                rows = value[part * modes : (part + 1) * modes]
                out_ref[slab, part] = jnp.where(chosen, bases[part], 0.0) + rows


def params(limit=LIMIT):
    return pltpu.CompilerParams(vmem_limit_bytes=limit)


def whole(shape):
    zeros = (0,) * len(shape)
    return pl.BlockSpec(shape, lambda *_: zeros)


SMEM = pl.BlockSpec(memory_space=pltpu.SMEM)
VMEM = pl.BlockSpec(memory_space=pltpu.VMEM)


def exchange(value):
    return lax.all_to_all(value, "col", split_axis=0, concat_axis=0, tiled=True)


def on_device(diag_inverse, couplings, sources, inject, leads):
    orbitals = diag_inverse.shape[2]
    width = diag_inverse.shape[3]
    size = couplings.shape[2]
    modes = sources.shape[3]
    lead = size // 8
    part_rows = orbitals // 8
    slabs = lax.axis_size("slab")
    slab_index = lax.axis_index("slab")
    col_index = lax.axis_index("col")
    team = col_index // 4
    member = col_index % 4
    first = slab_index * 2
    place = jnp.stack([first, jnp.zeros_like(first)]).astype(jnp.int32)
    position = jnp.where(team == 0, slab_index, slabs - 1 - slab_index)
    info = jnp.stack([team, position // 4, position % 4, slab_index % 4]).astype(jnp.int32)
    stack = 2 * (lead + 2 * modes)
    block_rows = 4 * lead + 32
    sources = jnp.transpose(sources, (0, 1, 3, 2))
    leads = jnp.transpose(leads, (0, 1, 3, 2))

    sent = pl.pallas_call(
        interface_kernel,
        grid=(4,),
        in_specs=[
            SMEM,
            whole(inject.shape),
            whole(sources.shape),
            pl.BlockSpec((1, 1, orbitals, width // 2), lambda step: (step // 2, step % 2, 0, 0)),
            pl.BlockSpec((1, 1, orbitals, width // 2), lambda step: (step // 2, step % 2, 0, 1)),
        ],
        out_specs=whole((8, block_rows, size)),
        out_shape=jax.ShapeDtypeStruct((8, block_rows, size), F32),
        scratch_shapes=[
            pltpu.VMEM((2, stack, width), BF16),
            pltpu.VMEM((2, stack, width), BF16),
            pltpu.VMEM((2, 2 * modes, size), F32),
        ],
        compiler_params=params(LARGE),
        name="interface_terms",
    )(place, inject, sources, diag_inverse, diag_inverse)
    sent, inject_after = lax.optimization_barrier((sent, inject))
    received = exchange(sent)

    def chunk_terms(place):
        terms = jax.ShapeDtypeStruct((2, 2 * lead + 4 * PACK, width), BF16)
        high, low = pl.pallas_call(
            select_kernel,
            in_specs=[SMEM, VMEM, VMEM],
            out_specs=[VMEM, VMEM],
            out_shape=[terms, terms],
            compiler_params=params(),
            name="select_terms",
        )(place, inject_after, sources)
        return pl.pallas_call(
            spread_kernel,
            grid=(8,),
            in_specs=[
                whole(terms.shape),
                whole(terms.shape),
                pl.BlockSpec((2, 2, part_rows, width), lambda step: (0, 0, step, 0)),
            ],
            out_specs=[
                pl.BlockSpec((1, 6 * lead, part_rows), lambda step: (step, 0, 0)),
                pl.BlockSpec((1, 2 * lead, part_rows), lambda step: (step, 0, 0)),
                pl.BlockSpec((1, 4 * PACK, part_rows), lambda step: (step, 0, 0)),
            ],
            out_shape=[
                jax.ShapeDtypeStruct((8, 6 * lead, part_rows), F32),
                jax.ShapeDtypeStruct((8, 2 * lead, part_rows), F32),
                jax.ShapeDtypeStruct((8, 4 * PACK, part_rows), F32),
            ],
            compiler_params=params(LARGE),
            name="spread_terms",
        )(high, low, diag_inverse)

    def summed(flows):
        return lax.psum_scatter(flows, "col", scatter_dimension=0, tiled=False)

    early, late, flows = chunk_terms(place)
    turned = pl.pallas_call(
        coupling_kernel,
        in_specs=[SMEM, VMEM],
        out_specs=VMEM,
        out_shape=jax.ShapeDtypeStruct((2, 2 * size, size), F32),
        compiler_params=params(),
        name="coupling_rows",
    )(info, couplings)
    own_inject = lax.dynamic_slice(inject, (team, member * 16), (1, 16))[0]
    own_inject = jnp.concatenate([own_inject, own_inject])
    marks = jnp.stack([own_inject == first + team, own_inject == first + 1 - team])
    marks = jnp.broadcast_to(marks.astype(F32)[:, :, None], (2, 32, size))
    own_lead = lax.dynamic_slice(leads, (team, 0, member * 16, 0), (1, 2, 16, size))
    own_lead = own_lead.reshape(32, size)
    base = summed(flows)
    owners = jnp.arange(slabs, dtype=jnp.int32)[:, None, None]
    counts = jnp.sum((inject_after[None] >> 1 == owners).astype(jnp.int32), axis=2)
    chunks = (jnp.max(counts) + PACK - 1) // PACK

    def more(chunk, extra):
        place = jnp.stack([first, chunk]).astype(jnp.int32)
        flows = chunk_terms(place)[2]
        return pl.pallas_call(
            expand_kernel,
            in_specs=[SMEM, VMEM, VMEM, VMEM],
            out_specs=VMEM,
            out_shape=jax.ShapeDtypeStruct((4 * modes, part_rows), F32),
            compiler_params=params(),
            name="expand_terms",
        )(place, inject, summed(flows), extra)

    extra = lax.fori_loop(1, chunks, more, jnp.zeros((4 * modes, part_rows), F32))
    received, turned, marks, own_lead, early, extra = lax.optimization_barrier(
        (received, turned, marks, own_lead, early, extra)
    )
    rows = exchange(early)

    top, bottom, flow_a, first_map = pl.pallas_call(
        pair_map_kernel,
        in_specs=[SMEM, VMEM, VMEM, VMEM],
        out_specs=[VMEM] * 4,
        out_shape=[
            jax.ShapeDtypeStruct((size + 16, size), F32),
            jax.ShapeDtypeStruct((size + 16, size), F32),
            jax.ShapeDtypeStruct((32, size), F32),
            jax.ShapeDtypeStruct((2 * size, size), F32),
        ],
        compiler_params=params(),
        name="pair_map",
    )(info, received, turned, marks)

    def turn(value, step):
        return lax.ppermute(
            value, "slab", [(slab, slab // 4 * 4 + (slab + step) % 4) for slab in range(slabs)]
        )

    before_top, after_bottom = turn(top, 1), turn(bottom, -1)
    before_bottom, after_top = turn(bottom, 1), turn(top, -1)
    across_top, across_bottom = turn(before_top, 1), turn(after_bottom, -1)
    pieces = (after_top, after_bottom, across_top, across_bottom, before_top, before_bottom)
    row_maps = [
        jax.ShapeDtypeStruct((4, 2 * size, size), BF16),
        jax.ShapeDtypeStruct((4, 2 * size, size), BF16),
        jax.ShapeDtypeStruct((4, 32, size), F32),
    ]
    state_shape = jax.ShapeDtypeStruct((32, size), F32)
    *maps, flow = pl.pallas_call(
        gather_kernel,
        in_specs=[SMEM] + [VMEM] * 9,
        out_specs=[VMEM] * 4,
        out_shape=row_maps + [state_shape],
        compiler_params=params(),
        name="gather_maps",
    )(info, own_lead, top, bottom, *pieces)

    cols = lax.axis_size("col")
    pairs = []
    for slab in range(slabs):
        for col in range(cols):
            target = (slab + (4 if col < 4 else -4)) % slabs
            pairs.append((slab * cols + col, target * cols + col))

    def local(kernel, name, shapes, *args):
        single = not isinstance(shapes, list)
        return pl.pallas_call(
            kernel,
            in_specs=[SMEM] + [VMEM] * (len(args) - 1),
            out_specs=VMEM if single else [VMEM] * len(shapes),
            out_shape=shapes,
            compiler_params=params(),
            name=name,
        )(*args)

    def hop(value):
        return lax.ppermute(value, ("slab", "col"), pairs)

    full = jax.ShapeDtypeStruct((2 * size + 32, size), F32)
    half_map = jax.ShapeDtypeStruct((2 * size, size), BF16)
    flow = hop(flow)
    *row_map, half_row = local(
        row_map_kernel, "row_map", [half_map, half_map, state_shape, full], info, *maps
    )
    flow = local(row_kernel, "row_step", state_shape, info, own_lead, flow, *row_map)
    flow, half_row = lax.optimization_barrier((flow, half_row))
    flow = hop(flow)
    prefix, inner_map = local(
        prefix_kernel, "prefix_map", [full, full], info, *maps, half_row, first_map, turned, flow_a
    )
    flow = local(row_kernel, "row_step", state_shape, info, own_lead, flow, *row_map)
    flow, prefix, inner_map = lax.optimization_barrier((flow, prefix, inner_map))
    flow = hop(flow)
    two_maps = [
        jax.ShapeDtypeStruct((2, 2 * size, size), BF16),
        jax.ShapeDtypeStruct((2, 2 * size, size), BF16),
        jax.ShapeDtypeStruct((2, 32, size), F32),
    ]
    entry = local(entry_map_kernel, "entry_map", two_maps, info, prefix, inner_map, turned)
    last = local(
        inflow_kernel,
        "inflow",
        jax.ShapeDtypeStruct((8, 64 + 2 * lead, size), F32),
        info,
        own_lead,
        flow,
        *entry,
        late,
    )
    rows, base, last = lax.optimization_barrier((rows, base, last))
    last = exchange(last)
    last, rows, base, extra, inject = lax.optimization_barrier((last, rows, base, extra, inject))

    shape = jax.ShapeDtypeStruct((2, 2, modes, part_rows), F32)
    left, right = local(
        state_kernel, "states", [shape, shape], place, inject, last, rows, base, extra
    )
    return jnp.transpose(left, (0, 1, 3, 2)), jnp.transpose(right, (0, 1, 3, 2))


def solution(mesh):
    placed = (
        P(("energy", "slab"), None, None, "col"),
        P(("energy", "slab"), None, None, None),
        P("energy", None, "col", None),
        P(),
        P("energy", None, None, None),
    )

    return jax.shard_map(
        on_device,
        mesh=mesh,
        in_specs=placed,
        out_specs=(
            P(("energy", "slab"), None, "col", None),
            P(("energy", "slab"), None, "col", None),
        ),
        check_vma=False,
    )
```

```python
import jax
import jax.numpy as jnp
from jax import lax
from jax.experimental import pallas as pl
from jax.experimental.pallas import tpu as pltpu
from jax.sharding import PartitionSpec as P

F32 = jnp.float32
BF16 = jnp.bfloat16
LIMIT = 24 * 1024 * 1024
LARGE = 56 * 1024 * 1024
PACK = 16
NEAR = (1, 7, 2)


def split(value):
    high = value.astype(BF16)
    return high, (value - high.astype(F32)).astype(BF16)


def mm(left, right, transposed=False):
    dims = (((1,), (1 if transposed else 0,)), ((), ()))
    return lax.dot_general(left, right, dims, preferred_element_type=F32)


def mm3(left, right, transposed=False):
    rows = left[0].shape[0]
    wide = mm(jnp.concatenate(left, axis=0), right[0], transposed)
    return wide[:rows] + (wide[rows:] + mm(left[0], right[1], transposed))


def combined(by_real, by_imag):
    half = by_real.shape[0] // 2
    return jnp.concatenate(
        [by_real[:half] - by_imag[half:], by_imag[:half] + by_real[half:]], axis=0
    )


def complex_rows(left, right):
    parts = split(left)
    return combined(mm3(parts, split(right[0])), mm3(parts, split(right[1])))


def times(left, right):
    size = right[0].shape[0] // 2
    by_real = mm3(left, (right[0][:size], right[1][:size]))
    by_imag = mm3(left, (right[0][size:], right[1][size:]))
    return combined(by_real, by_imag)


def interface_kernel(
    place_ref, inject_ref, src_ref, g0_ref, g1_ref, out_ref, high_ref, low_ref, acc_ref
):
    step = pl.program_id(0)
    slab = step // 2
    plane = step % 2
    modes = src_ref.shape[2]
    width = src_ref.shape[3]

    @pl.when(step == 0)
    def _():
        rows = lax.broadcasted_iota(jnp.int32, (width // 8, width), 0)
        cols = lax.broadcasted_iota(jnp.int32, (width // 8, width), 1)
        targets = [
            jnp.broadcast_to(inject_ref[sweep : sweep + 1, :].astype(F32), (width, modes)).T
            for sweep in range(2)
        ]
        for local in range(2):
            pieces = []
            for sweep in range(2):
                pieces.append((cols == rows * 8 + sweep).astype(F32))
                chosen = targets[sweep] == (place_ref[0] + local).astype(F32)
                for part in range(2):
                    pieces.append(jnp.where(chosen, src_ref[sweep, part], 0.0))
            high, low = split(jnp.concatenate(pieces, axis=0))
            high_ref[local] = high
            low_ref[local] = low
        acc_ref[...] = jnp.zeros_like(acc_ref)

    half = high_ref.shape[1] // 2
    lead = width // 8
    count = g0_ref.shape[2] // 8
    for sweep in range(2):
        rows = jnp.concatenate(
            [ref[0, 0, pl.ds(1 - sweep, count, stride=8), :] for ref in (g0_ref, g1_ref)], axis=1
        )
        picked = pl.ds(sweep * half, half)
        term = mm3((high_ref[slab, picked, :], low_ref[slab, picked, :]), split(rows), True)
        order = slab if sweep == 0 else 1 - slab
        place = pl.ds(pl.multiple_of((order * 2 + plane) * lead, lead), lead)
        for member in range(4):
            out_ref[sweep * 4 + member, place, :] = term[:lead]
        real, imag = term[lead : lead + modes], term[lead + modes :]

        @pl.when(plane == 0)
        def _():
            acc_ref[sweep, :modes] += real
            acc_ref[sweep, modes:] += imag

        @pl.when(plane == 1)
        def _():
            acc_ref[sweep, :modes] -= imag
            acc_ref[sweep, modes:] += real

    @pl.when(step == 3)
    def _():
        for dest in range(8):
            sweep, member = divmod(dest, 4)
            for part in range(2):
                start = part * modes + member * 16
                out_ref[dest, 4 * lead + part * 16 : 4 * lead + (part + 1) * 16, :] = acc_ref[
                    sweep, start : start + 16, :
                ]


def packed_columns(place_ref, inject_ref, sweep):
    modes = inject_ref.shape[1]
    target = inject_ref[sweep : sweep + 1, :]
    own = (target == place_ref[0]) | (target == place_ref[0] + 1)
    own = jnp.broadcast_to(own.astype(F32), (PACK, modes))
    earlier = lax.broadcasted_iota(jnp.int32, (modes, modes), 0)
    later = lax.broadcasted_iota(jnp.int32, (modes, modes), 1)
    rank = mm(own.astype(BF16), (earlier < later).astype(F32).astype(BF16))
    wanted = lax.broadcasted_iota(jnp.int32, (PACK, modes), 0) + PACK * place_ref[1]
    return jnp.where(rank == wanted.astype(F32), own, 0.0)


def unpacked_rows(place_ref, inject_ref, base_ref, sweep, part):
    back = packed_columns(place_ref, inject_ref, sweep).T.astype(BF16)
    start = (2 * sweep + part) * PACK
    high, low = split(base_ref[start : start + PACK, :])
    return mm(back, high) + mm(back, low)


def select_kernel(place_ref, inject_ref, src_ref, high_ref, low_ref):
    width = src_ref.shape[3]
    rows = lax.broadcasted_iota(jnp.int32, (width // 8, width), 0)
    cols = lax.broadcasted_iota(jnp.int32, (width // 8, width), 1)
    lead = width // 8
    for slab in range(2):
        for sweep in range(2):
            span = slice(sweep * lead, (sweep + 1) * lead)
            unit = (cols == rows * 8 + sweep).astype(F32)
            high_ref[slab, span, :] = unit.astype(BF16)
            low_ref[slab, span, :] = jnp.zeros_like(unit).astype(BF16)
            here = inject_ref[sweep : sweep + 1, :] == place_ref[0] + slab
            pick = jnp.where(here, packed_columns(place_ref, inject_ref, sweep), 0.0).astype(BF16)
            for part in range(2):
                start = 2 * lead + (2 * sweep + part) * PACK
                high, low = split(src_ref[sweep, part])
                high_ref[slab, start : start + PACK, :] = mm(pick, high).astype(BF16)
                low_ref[slab, start : start + PACK, :] = mm(pick, low).astype(BF16)


def spread_kernel(order_ref, high_ref, low_ref, g_ref, *refs):
    early_refs, (late_ref, flow_ref) = refs[:8], refs[8:]
    step = pl.program_id(0)
    lead = g_ref.shape[3] // 8
    total = [0.0] * 4
    pieces = []
    for slab in range(2):
        parts = (high_ref[slab], low_ref[slab])
        real = mm3(parts, split(g_ref[slab, 0]), True)
        imag = mm3(parts, split(g_ref[slab, 1]), True)
        for sweep in range(2):
            span = slice(sweep * lead, (sweep + 1) * lead)
            pieces += [real[span], imag[span]]
            one = 2 * lead + 2 * sweep * PACK
            two, three = one + PACK, one + 2 * PACK
            total[2 * sweep] += real[one:two] - imag[two:three]
            total[2 * sweep + 1] += real[two:three] + imag[one:two]
    early = jnp.concatenate(pieces[:6], axis=0)
    for away in range(8):

        @pl.when(step == away)
        def _(away=away):
            early_refs[away][...] = early

    late_ref[0] = jnp.concatenate(pieces[6:], axis=0)
    for item in range(4):
        flow_ref[0, item * PACK : (item + 1) * PACK, :] = total[item]


def expand_kernel(place_ref, inject_ref, base_ref, extra_ref, out_ref):
    modes = inject_ref.shape[1]
    for sweep in range(2):
        for part in range(2):
            span = slice((2 * sweep + part) * modes, (2 * sweep + part + 1) * modes)
            rows = unpacked_rows(place_ref, inject_ref, base_ref, sweep, part)
            out_ref[span, :] = extra_ref[span, :] + rows


def coupling_kernel(team_ref, c_ref, x_ref):
    left = team_ref[0] == 0
    size = c_ref.shape[3]
    for slab in range(2):
        x_ref[slab, :size] = jnp.where(left, c_ref[slab, 0].T, c_ref[slab, 0])
        x_ref[slab, size:] = jnp.where(left, c_ref[slab, 1].T, -c_ref[slab, 1])


def stacked(ref, start, count):
    return jnp.concatenate([ref[block, start : start + count, :] for block in range(8)], axis=0)


def pair_map_kernel(
    team_ref, recv_ref, x_ref, mask_ref, top_ref, bottom_ref, qa_ref, first_ref
):
    left = team_ref[0] == 0
    size = x_ref.shape[2]
    lead = size // 8
    coupled = [(x_ref[slab, :size], x_ref[slab, size:]) for slab in range(2)]
    blocks = [
        (stacked(recv_ref, 2 * item * lead, lead), stacked(recv_ref, (2 * item + 1) * lead, lead))
        for item in range(2)
    ]
    flow = recv_ref[0, 4 * lead :, :]
    for block in range(1, 8):
        flow = flow + recv_ref[block, 4 * lead :, :]
    flow_a = jnp.where(mask_ref[0] != 0, flow, 0.0)
    flow_b = jnp.where(mask_ref[1] != 0, flow, 0.0)
    qa_ref[...] = flow_a

    def pick(one, two):
        return (jnp.where(left, one[0], two[0]), jnp.where(left, one[1], two[1]))

    def product(one, two):
        return complex_rows(jnp.concatenate(one, axis=0), two)

    first = product(pick(coupled[0], blocks[0]), pick(blocks[0], coupled[1]))
    second = product(pick(coupled[1], blocks[1]), pick(blocks[1], coupled[0]))
    second = (second[:size], second[size:])
    first_ref[...] = first
    half = top_ref.shape[0]
    both = complex_rows(first, second)
    top_ref[...] = both[:half]
    bottom_ref[: 2 * size - half, :] = both[half:]
    flow_a = jnp.where(left, flow_a, complex_rows(flow_a, coupled[1]))
    flow_b = jnp.where(left, flow_b, complex_rows(flow_b, coupled[0]))
    bottom_ref[2 * size - half :, :] = complex_rows(flow_a, second) + flow_b


def item_of(info_ref, item):
    return jnp.where(info_ref[0] == 0, item, 3 - item)


def entry_state(info_ref, lead_ref, state_ref):
    return jnp.where(info_ref[1] == 0, lead_ref[...], state_ref[...])


def gather_kernel(info_ref, lead_ref, *refs):
    pieces, (high_ref, low_ref, flow_ref, out_ref) = refs[:8], refs[8:]
    size = pieces[0].shape[1]
    half = pieces[0].shape[0]
    for shift in range(4):
        place = lax.rem(info_ref[3] + shift, 4)
        top, bottom = pieces[2 * shift][...], pieces[2 * shift + 1][...]
        rest = 2 * size - half
        high, low = split(top)
        high_ref[place, :half, :] = high
        low_ref[place, :half, :] = low
        high, low = split(bottom[:rest])
        high_ref[place, half:, :] = high
        low_ref[place, half:, :] = low
        flow_ref[place] = bottom[rest:]
    state = lead_ref[...]
    for item in range(4):
        index = item_of(info_ref, item)
        state = times(split(state), (high_ref[index], low_ref[index])) + flow_ref[index]
    out_ref[...] = state


def row_map_kernel(
    info_ref, high_ref, low_ref, flow_ref, row_high_ref, row_low_ref, row_flow_ref, half_ref
):
    maps, flows = [], []
    for item in range(4):
        index = item_of(info_ref, item)
        maps.append((high_ref[index], low_ref[index]))
        flows.append(flow_ref[index])
    size = high_ref.shape[2]
    early = times(maps[0], maps[1])
    early_flow = times(split(flows[0]), maps[1]) + flows[1]
    late = split(times(maps[2], maps[3]))
    late_flow = times(split(flows[2]), maps[3]) + flows[3]
    half_ref[: 2 * size, :] = early
    half_ref[2 * size :, :] = early_flow
    high, low = split(times(split(early), late))
    row_high_ref[...] = high
    row_low_ref[...] = low
    row_flow_ref[...] = times(split(early_flow), late) + late_flow


def row_kernel(info_ref, lead_ref, state_ref, high_ref, low_ref, flow_ref, out_ref):
    state = entry_state(info_ref, lead_ref, state_ref)
    out_ref[...] = times(split(state), (high_ref[...], low_ref[...])) + flow_ref[...]


def prefix_kernel(
    info_ref, high_ref, low_ref, flow_ref, half_ref, first_ref, x_ref, qa_ref, out_ref, inner_ref
):
    size = high_ref.shape[2]
    left = info_ref[0] == 0
    one, three = item_of(info_ref, 0), item_of(info_ref, 2)
    rows = lax.broadcasted_iota(jnp.int32, (2 * size + 32, size), 0)
    cols = lax.broadcasted_iota(jnp.int32, (2 * size + 32, size), 1)
    half = half_ref[...]
    third = (high_ref[three], low_ref[three])
    whole_row = times(split(half[: 2 * size]), third)
    whole_flow = times(split(half[2 * size :]), third) + flow_ref[three]
    none = (rows == cols).astype(F32)
    single = high_ref[one].astype(F32) + low_ref[one].astype(F32)
    single = jnp.concatenate([single, flow_ref[one]], axis=0)
    triple = jnp.concatenate([whole_row, whole_flow], axis=0)
    count = info_ref[2]
    low_half = jnp.where(count == 0, none, single)
    out_ref[...] = jnp.where(count < 2, low_half, jnp.where(count == 2, half, triple))
    second = split(x_ref[1])
    first = first_ref[...]
    inner_ref[: 2 * size, :] = jnp.where(left, times(split(first), second), first)
    inner_ref[2 * size :, :] = times(split(qa_ref[...]), second)


def entry_map_kernel(info_ref, prefix_ref, inner_ref, x_ref, high_ref, low_ref, flow_ref):
    size = x_ref.shape[2]
    left = info_ref[0] == 0
    prefix, flow = split(prefix_ref[: 2 * size, :]), split(prefix_ref[2 * size :, :])
    turn = split(x_ref[0])
    inner = split(inner_ref[: 2 * size, :])
    item_a = jnp.where(left, times(prefix, turn), prefix_ref[: 2 * size, :])
    flow_ref[0] = jnp.where(left, times(flow, turn), prefix_ref[2 * size :, :])
    item_b = times(prefix, inner)
    flow_ref[1] = times(flow, inner) + inner_ref[2 * size :, :]
    for item, value in enumerate((item_a, item_b)):
        high, low = split(value)
        high_ref[item] = high
        low_ref[item] = low


def inflow_kernel(
    info_ref, lead_ref, state_ref, high_ref, low_ref, flow_ref, spread_ref, out_ref
):
    out_ref[:, 64:, :] = spread_ref[...]
    state = split(entry_state(info_ref, lead_ref, state_ref))
    for item in range(2):
        value = times(state, (high_ref[item], low_ref[item])) + flow_ref[item]
        for dest in range(8):
            out_ref[dest, 32 * item : 32 * (item + 1), :] = value


def state_kernel(
    place_ref, inject_ref, last_ref, base_ref, extra_ref, *refs
):
    piece_refs, (left_ref, right_ref, rows_ref) = refs[:8], refs[8:]
    modes = inject_ref.shape[1]
    width = base_ref.shape[1]
    lead = piece_refs[0].shape[0] // 6
    for away in range(8):
        source = lax.rem(place_ref[2] + 8 - away, 8)
        for kind in range(6):
            span = pl.ds(pl.multiple_of(source * lead, lead), lead)
            rows_ref[kind, span, :] = piece_refs[away][kind * lead : (kind + 1) * lead, :]
    for sweep, out_ref in enumerate((left_ref, right_ref)):
        target = jnp.broadcast_to(
            inject_ref[sweep : sweep + 1, :].astype(F32), (width, modes)
        ).T
        bases = []
        for part in range(2):
            start = (2 * sweep + part) * modes
            rows = unpacked_rows(place_ref, inject_ref, base_ref, sweep, part)
            bases.append(rows + extra_ref[start : start + modes, :])
        for slab in range(2):
            item = slab if sweep == 0 else 1 - slab
            pieces = []
            for part in range(2):
                start = item * 32 + part * 16
                for member in range(4):
                    pieces.append(last_ref[sweep * 4 + member, start : start + 16, :])
            parts = split(jnp.concatenate(pieces, axis=0))
            by = []
            for part in range(2):
                kind = 2 * sweep + part
                if slab == 1 and sweep == 1:
                    matrix = stacked(last_ref, 64 + part * lead, lead)
                else:
                    matrix = rows_ref[4 * slab + kind]
                by.append(mm3(parts, split(matrix)))
            value = combined(by[0], by[1])
            chosen = target == (place_ref[0] + slab).astype(F32)
            for part in range(2):
                rows = value[part * modes : (part + 1) * modes]
                out_ref[slab, part] = jnp.where(chosen, bases[part], 0.0) + rows


def params(limit=LIMIT):
    return pltpu.CompilerParams(vmem_limit_bytes=limit)


def whole(shape):
    zeros = (0,) * len(shape)
    return pl.BlockSpec(shape, lambda *_: zeros)


SMEM = pl.BlockSpec(memory_space=pltpu.SMEM)
VMEM = pl.BlockSpec(memory_space=pltpu.VMEM)


def exchange(value):
    return lax.all_to_all(value, "col", split_axis=0, concat_axis=0, tiled=True)


def on_device(diag_inverse, couplings, sources, inject, leads):
    orbitals = diag_inverse.shape[2]
    width = diag_inverse.shape[3]
    size = couplings.shape[2]
    modes = sources.shape[3]
    lead = size // 8
    part_rows = orbitals // 8
    slabs = lax.axis_size("slab")
    slab_index = lax.axis_index("slab")
    col_index = lax.axis_index("col")
    team = col_index // 4
    member = col_index % 4
    first = slab_index * 2
    place = jnp.stack([first, jnp.zeros_like(first), col_index]).astype(jnp.int32)
    position = jnp.where(team == 0, slab_index, slabs - 1 - slab_index)
    info = jnp.stack([team, position // 4, position % 4, slab_index % 4]).astype(jnp.int32)
    stack = 2 * (lead + 2 * modes)
    block_rows = 4 * lead + 32
    sources = jnp.transpose(sources, (0, 1, 3, 2))
    leads = jnp.transpose(leads, (0, 1, 3, 2))

    sent = pl.pallas_call(
        interface_kernel,
        grid=(4,),
        in_specs=[
            SMEM,
            whole(inject.shape),
            whole(sources.shape),
            pl.BlockSpec((1, 1, orbitals, width // 2), lambda step: (step // 2, step % 2, 0, 0)),
            pl.BlockSpec((1, 1, orbitals, width // 2), lambda step: (step // 2, step % 2, 0, 1)),
        ],
        out_specs=whole((8, block_rows, size)),
        out_shape=jax.ShapeDtypeStruct((8, block_rows, size), F32),
        scratch_shapes=[
            pltpu.VMEM((2, stack, width), BF16),
            pltpu.VMEM((2, stack, width), BF16),
            pltpu.VMEM((2, 2 * modes, size), F32),
        ],
        compiler_params=params(LARGE),
        name="interface_terms",
    )(place, inject, sources, diag_inverse, diag_inverse)
    sent, inject_after = lax.optimization_barrier((sent, inject))
    received = exchange(sent)

    ring = (col_index + jnp.arange(8, dtype=jnp.int32)) % 8

    def chunk_terms(place):
        terms = jax.ShapeDtypeStruct((2, 2 * lead + 4 * PACK, width), BF16)
        high, low = pl.pallas_call(
            select_kernel,
            in_specs=[SMEM, VMEM, VMEM],
            out_specs=[VMEM, VMEM],
            out_shape=[terms, terms],
            compiler_params=params(),
            name="select_terms",
        )(place, inject_after, sources)
        return pl.pallas_call(
            spread_kernel,
            grid_spec=pltpu.PrefetchScalarGridSpec(
                num_scalar_prefetch=1,
                grid=(8,),
                in_specs=[
                    whole(terms.shape),
                    whole(terms.shape),
                    pl.BlockSpec(
                        (2, 2, part_rows, width), lambda step, order: (0, 0, order[step], 0)
                    ),
                ],
                out_specs=[whole((6 * lead, part_rows))] * 8
                + [
                    pl.BlockSpec((1, rows, part_rows), lambda step, order: (order[step], 0, 0))
                    for rows in (2 * lead, 4 * PACK)
                ],
            ),
            out_shape=[jax.ShapeDtypeStruct((6 * lead, part_rows), F32)] * 8
            + [
                jax.ShapeDtypeStruct((8, rows, part_rows), F32) for rows in (2 * lead, 4 * PACK)
            ],
            compiler_params=params(LARGE),
            name="spread_terms",
        )(ring, high, low, diag_inverse)

    def summed(flows):
        return lax.psum_scatter(flows, "col", scatter_dimension=0, tiled=False)

    *early, late, flows = chunk_terms(place)
    turned = pl.pallas_call(
        coupling_kernel,
        in_specs=[SMEM, VMEM],
        out_specs=VMEM,
        out_shape=jax.ShapeDtypeStruct((2, 2 * size, size), F32),
        compiler_params=params(),
        name="coupling_rows",
    )(info, couplings)
    own_inject = lax.dynamic_slice(inject, (team, member * 16), (1, 16))[0]
    own_inject = jnp.concatenate([own_inject, own_inject])
    marks = jnp.stack([own_inject == first + team, own_inject == first + 1 - team])
    marks = jnp.broadcast_to(marks.astype(F32)[:, :, None], (2, 32, size))
    own_lead = lax.dynamic_slice(leads, (team, 0, member * 16, 0), (1, 2, 16, size))
    own_lead = own_lead.reshape(32, size)
    base = summed(flows)
    owners = jnp.arange(slabs, dtype=jnp.int32)[:, None, None]
    counts = jnp.sum((inject_after[None] >> 1 == owners).astype(jnp.int32), axis=2)
    chunks = (jnp.max(counts) + PACK - 1) // PACK

    def more(chunk, extra):
        place = jnp.stack([first, chunk]).astype(jnp.int32)
        flows = chunk_terms(place)[9]
        return pl.pallas_call(
            expand_kernel,
            in_specs=[SMEM, VMEM, VMEM, VMEM],
            out_specs=VMEM,
            out_shape=jax.ShapeDtypeStruct((4 * modes, part_rows), F32),
            compiler_params=params(),
            name="expand_terms",
        )(place, inject, summed(flows), extra)

    extra = lax.fori_loop(1, chunks, more, jnp.zeros((4 * modes, part_rows), F32))
    received, turned, marks, own_lead, early, extra = lax.optimization_barrier(
        (received, turned, marks, own_lead, early, extra)
    )

    def further(away):
        return lax.ppermute(early[away], "col", [(col, (col + away) % 8) for col in range(8)])

    rows = [early[0]] + [further(away) for away in range(1, 8)]

    top, bottom, flow_a, first_map = pl.pallas_call(
        pair_map_kernel,
        in_specs=[SMEM, VMEM, VMEM, VMEM],
        out_specs=[VMEM] * 4,
        out_shape=[
            jax.ShapeDtypeStruct((size + 16, size), F32),
            jax.ShapeDtypeStruct((size + 16, size), F32),
            jax.ShapeDtypeStruct((32, size), F32),
            jax.ShapeDtypeStruct((2 * size, size), F32),
        ],
        compiler_params=params(),
        name="pair_map",
    )(info, received, turned, marks)

    def turn(value, step):
        return lax.ppermute(
            value, "slab", [(slab, slab // 4 * 4 + (slab + step) % 4) for slab in range(slabs)]
        )

    before_top, after_bottom = turn(top, 1), turn(bottom, -1)
    before_bottom, after_top = turn(bottom, 1), turn(top, -1)
    across_top, across_bottom = turn(before_top, 1), turn(after_bottom, -1)
    pieces = (after_top, after_bottom, across_top, across_bottom, before_top, before_bottom)
    pieces, near = lax.optimization_barrier((pieces, [rows[away] for away in NEAR]))
    for away, value in zip(NEAR, near):
        rows[away] = value
    row_maps = [
        jax.ShapeDtypeStruct((4, 2 * size, size), BF16),
        jax.ShapeDtypeStruct((4, 2 * size, size), BF16),
        jax.ShapeDtypeStruct((4, 32, size), F32),
    ]
    state_shape = jax.ShapeDtypeStruct((32, size), F32)
    *maps, flow = pl.pallas_call(
        gather_kernel,
        in_specs=[SMEM] + [VMEM] * 9,
        out_specs=[VMEM] * 4,
        out_shape=row_maps + [state_shape],
        compiler_params=params(),
        name="gather_maps",
    )(info, own_lead, top, bottom, *pieces)

    cols = lax.axis_size("col")
    pairs = []
    for slab in range(slabs):
        for col in range(cols):
            target = (slab + (4 if col < 4 else -4)) % slabs
            pairs.append((slab * cols + col, target * cols + col))

    def local(kernel, name, shapes, *args):
        single = not isinstance(shapes, list)
        return pl.pallas_call(
            kernel,
            in_specs=[SMEM] + [VMEM] * (len(args) - 1),
            out_specs=VMEM if single else [VMEM] * len(shapes),
            out_shape=shapes,
            compiler_params=params(),
            name=name,
        )(*args)

    def hop(value):
        return lax.ppermute(value, ("slab", "col"), pairs)

    full = jax.ShapeDtypeStruct((2 * size + 32, size), F32)
    half_map = jax.ShapeDtypeStruct((2 * size, size), BF16)
    flow = hop(flow)
    *row_map, half_row = local(
        row_map_kernel, "row_map", [half_map, half_map, state_shape, full], info, *maps
    )
    flow = local(row_kernel, "row_step", state_shape, info, own_lead, flow, *row_map)
    flow, half_row = lax.optimization_barrier((flow, half_row))
    flow = hop(flow)
    prefix, inner_map = local(
        prefix_kernel, "prefix_map", [full, full], info, *maps, half_row, first_map, turned, flow_a
    )
    flow = local(row_kernel, "row_step", state_shape, info, own_lead, flow, *row_map)
    flow, prefix, inner_map = lax.optimization_barrier((flow, prefix, inner_map))
    flow = hop(flow)
    two_maps = [
        jax.ShapeDtypeStruct((2, 2 * size, size), BF16),
        jax.ShapeDtypeStruct((2, 2 * size, size), BF16),
        jax.ShapeDtypeStruct((2, 32, size), F32),
    ]
    entry = local(entry_map_kernel, "entry_map", two_maps, info, prefix, inner_map, turned)
    last = local(
        inflow_kernel,
        "inflow",
        jax.ShapeDtypeStruct((8, 64 + 2 * lead, size), F32),
        info,
        own_lead,
        flow,
        *entry,
        late,
    )
    rows, base, last = lax.optimization_barrier((rows, base, last))
    last = exchange(last)
    last, rows, base, extra, inject = lax.optimization_barrier((last, rows, base, extra, inject))

    shape = jax.ShapeDtypeStruct((2, 2, modes, part_rows), F32)
    left, right = pl.pallas_call(
        state_kernel,
        in_specs=[SMEM] + [VMEM] * 12,
        out_specs=[VMEM, VMEM],
        out_shape=[shape, shape],
        scratch_shapes=[pltpu.VMEM((6, size, part_rows), F32)],
        compiler_params=params(),
        name="states",
    )(place, inject, last, base, extra, *rows)
    return jnp.transpose(left, (0, 1, 3, 2)), jnp.transpose(right, (0, 1, 3, 2))


def solution(mesh):
    placed = (
        P(("energy", "slab"), None, None, "col"),
        P(("energy", "slab"), None, None, None),
        P("energy", None, "col", None),
        P(),
        P("energy", None, None, None),
    )

    return jax.shard_map(
        on_device,
        mesh=mesh,
        in_specs=placed,
        out_specs=(
            P(("energy", "slab"), None, "col", None),
            P(("energy", "slab"), None, "col", None),
        ),
        check_vma=False,
    )
```

```python
import jax
import jax.numpy as jnp
from jax import lax
from jax.experimental import pallas as pl
from jax.experimental.pallas import tpu as pltpu
from jax.sharding import PartitionSpec as P

F32 = jnp.float32
BF16 = jnp.bfloat16
LIMIT = 24 * 1024 * 1024
LARGE = 56 * 1024 * 1024
PACK = 16


def split(value):
    high = value.astype(BF16)
    return high, (value - high.astype(F32)).astype(BF16)


def mm(left, right, transposed=False):
    dims = (((1,), (1 if transposed else 0,)), ((), ()))
    return lax.dot_general(left, right, dims, preferred_element_type=F32)


def mm3(left, right, transposed=False):
    rows = left[0].shape[0]
    wide = mm(jnp.concatenate(left, axis=0), right[0], transposed)
    return wide[:rows] + (wide[rows:] + mm(left[0], right[1], transposed))


def combined(by_real, by_imag):
    half = by_real.shape[0] // 2
    return jnp.concatenate(
        [by_real[:half] - by_imag[half:], by_imag[:half] + by_real[half:]], axis=0
    )


def complex_rows(left, right):
    parts = split(left)
    return combined(mm3(parts, split(right[0])), mm3(parts, split(right[1])))


def times(left, right):
    size = right[0].shape[0] // 2
    by_real = mm3(left, (right[0][:size], right[1][:size]))
    by_imag = mm3(left, (right[0][size:], right[1][size:]))
    return combined(by_real, by_imag)


def interface_kernel(
    place_ref, inject_ref, src_ref, g0_ref, g1_ref, out_ref, high_ref, low_ref, acc_ref
):
    step = pl.program_id(0)
    slab = step // 2
    plane = step % 2
    modes = src_ref.shape[2]
    width = src_ref.shape[3]

    @pl.when(step == 0)
    def _():
        rows = lax.broadcasted_iota(jnp.int32, (width // 8, width), 0)
        cols = lax.broadcasted_iota(jnp.int32, (width // 8, width), 1)
        targets = [
            jnp.broadcast_to(inject_ref[sweep : sweep + 1, :].astype(F32), (width, modes)).T
            for sweep in range(2)
        ]
        for local in range(2):
            pieces = []
            for sweep in range(2):
                pieces.append((cols == rows * 8 + sweep).astype(F32))
                chosen = targets[sweep] == (place_ref[0] + local).astype(F32)
                for part in range(2):
                    pieces.append(jnp.where(chosen, src_ref[sweep, part], 0.0))
            high, low = split(jnp.concatenate(pieces, axis=0))
            high_ref[local] = high
            low_ref[local] = low
        acc_ref[...] = jnp.zeros_like(acc_ref)

    half = high_ref.shape[1] // 2
    lead = width // 8
    count = g0_ref.shape[2] // 8
    for sweep in range(2):
        rows = jnp.concatenate(
            [ref[0, 0, pl.ds(1 - sweep, count, stride=8), :] for ref in (g0_ref, g1_ref)], axis=1
        )
        picked = pl.ds(sweep * half, half)
        term = mm3((high_ref[slab, picked, :], low_ref[slab, picked, :]), split(rows), True)
        order = slab if sweep == 0 else 1 - slab
        place = pl.ds(pl.multiple_of((order * 2 + plane) * lead, lead), lead)
        for member in range(4):
            out_ref[sweep * 4 + member, place, :] = term[:lead]
        real, imag = term[lead : lead + modes], term[lead + modes :]

        @pl.when(plane == 0)
        def _():
            acc_ref[sweep, :modes] += real
            acc_ref[sweep, modes:] += imag

        @pl.when(plane == 1)
        def _():
            acc_ref[sweep, :modes] -= imag
            acc_ref[sweep, modes:] += real

    @pl.when(step == 3)
    def _():
        for dest in range(8):
            sweep, member = divmod(dest, 4)
            for part in range(2):
                start = part * modes + member * 16
                out_ref[dest, 4 * lead + part * 16 : 4 * lead + (part + 1) * 16, :] = acc_ref[
                    sweep, start : start + 16, :
                ]


def packed_columns(place_ref, inject_ref, sweep):
    modes = inject_ref.shape[1]
    target = inject_ref[sweep : sweep + 1, :]
    own = (target == place_ref[0]) | (target == place_ref[0] + 1)
    own = jnp.broadcast_to(own.astype(F32), (PACK, modes))
    earlier = lax.broadcasted_iota(jnp.int32, (modes, modes), 0)
    later = lax.broadcasted_iota(jnp.int32, (modes, modes), 1)
    rank = mm(own.astype(BF16), (earlier < later).astype(F32).astype(BF16))
    wanted = lax.broadcasted_iota(jnp.int32, (PACK, modes), 0) + PACK * place_ref[1]
    return jnp.where(rank == wanted.astype(F32), own, 0.0)


def unpacked_rows(place_ref, inject_ref, base_ref, sweep, part):
    back = packed_columns(place_ref, inject_ref, sweep).T.astype(BF16)
    start = (2 * sweep + part) * PACK
    high, low = split(base_ref[start : start + PACK, :])
    return mm(back, high) + mm(back, low)


def select_kernel(place_ref, inject_ref, src_ref, high_ref, low_ref):
    width = src_ref.shape[3]
    rows = lax.broadcasted_iota(jnp.int32, (width // 8, width), 0)
    cols = lax.broadcasted_iota(jnp.int32, (width // 8, width), 1)
    lead = width // 8
    for slab in range(2):
        for sweep in range(2):
            span = slice(sweep * lead, (sweep + 1) * lead)
            unit = (cols == rows * 8 + sweep).astype(F32)
            high_ref[slab, span, :] = unit.astype(BF16)
            low_ref[slab, span, :] = jnp.zeros_like(unit).astype(BF16)
            here = inject_ref[sweep : sweep + 1, :] == place_ref[0] + slab
            pick = jnp.where(here, packed_columns(place_ref, inject_ref, sweep), 0.0).astype(BF16)
            for part in range(2):
                start = 2 * lead + (2 * sweep + part) * PACK
                high, low = split(src_ref[sweep, part])
                high_ref[slab, start : start + PACK, :] = mm(pick, high).astype(BF16)
                low_ref[slab, start : start + PACK, :] = mm(pick, low).astype(BF16)


def spread_kernel(high_ref, low_ref, g_ref, early_ref, late_ref, flow_ref):
    lead = g_ref.shape[3] // 8
    total = [0.0] * 4
    for slab in range(2):
        parts = (high_ref[slab], low_ref[slab])
        real = mm3(parts, split(g_ref[slab, 0]), True)
        imag = mm3(parts, split(g_ref[slab, 1]), True)
        for sweep in range(2):
            base = sweep * lead
            place = sweep * 2 * lead
            out_ref = (early_ref, late_ref)[slab]
            out_ref[0, place : place + lead, :] = real[base : base + lead]
            out_ref[0, place + lead : place + 2 * lead, :] = imag[base : base + lead]
            one = 2 * lead + 2 * sweep * PACK
            two, three = one + PACK, one + 2 * PACK
            total[2 * sweep] += real[one:two] - imag[two:three]
            total[2 * sweep + 1] += real[two:three] + imag[one:two]
    for item in range(4):
        flow_ref[0, item * PACK : (item + 1) * PACK, :] = total[item]


def expand_kernel(place_ref, inject_ref, base_ref, extra_ref, out_ref):
    modes = inject_ref.shape[1]
    for sweep in range(2):
        for part in range(2):
            span = slice((2 * sweep + part) * modes, (2 * sweep + part + 1) * modes)
            rows = unpacked_rows(place_ref, inject_ref, base_ref, sweep, part)
            out_ref[span, :] = extra_ref[span, :] + rows


def coupling_kernel(team_ref, c_ref, x_ref):
    left = team_ref[0] == 0
    size = c_ref.shape[3]
    for slab in range(2):
        x_ref[slab, :size] = jnp.where(left, c_ref[slab, 0].T, c_ref[slab, 0])
        x_ref[slab, size:] = jnp.where(left, c_ref[slab, 1].T, -c_ref[slab, 1])


def stacked(ref, start, count):
    return jnp.concatenate([ref[block, start : start + count, :] for block in range(8)], axis=0)


def pair_map_kernel(
    team_ref, recv_ref, x_ref, mask_ref, top_ref, bottom_ref, qa_ref, first_ref
):
    left = team_ref[0] == 0
    size = x_ref.shape[2]
    lead = size // 8
    coupled = [(x_ref[slab, :size], x_ref[slab, size:]) for slab in range(2)]
    blocks = [
        (stacked(recv_ref, 2 * item * lead, lead), stacked(recv_ref, (2 * item + 1) * lead, lead))
        for item in range(2)
    ]
    flow = recv_ref[0, 4 * lead :, :]
    for block in range(1, 8):
        flow = flow + recv_ref[block, 4 * lead :, :]
    flow_a = jnp.where(mask_ref[0] != 0, flow, 0.0)
    flow_b = jnp.where(mask_ref[1] != 0, flow, 0.0)
    qa_ref[...] = flow_a

    def pick(one, two):
        return (jnp.where(left, one[0], two[0]), jnp.where(left, one[1], two[1]))

    def product(one, two):
        return complex_rows(jnp.concatenate(one, axis=0), two)

    first = product(pick(coupled[0], blocks[0]), pick(blocks[0], coupled[1]))
    second = product(pick(coupled[1], blocks[1]), pick(blocks[1], coupled[0]))
    second = (second[:size], second[size:])
    first_ref[...] = first
    half = top_ref.shape[0]
    both = complex_rows(first, second)
    top_ref[...] = both[:half]
    bottom_ref[: 2 * size - half, :] = both[half:]
    flow_a = jnp.where(left, flow_a, complex_rows(flow_a, coupled[1]))
    flow_b = jnp.where(left, flow_b, complex_rows(flow_b, coupled[0]))
    bottom_ref[2 * size - half :, :] = complex_rows(flow_a, second) + flow_b


def item_of(info_ref, item):
    return jnp.where(info_ref[0] == 0, item, 3 - item)


def entry_state(info_ref, lead_ref, state_ref):
    return jnp.where(info_ref[1] == 0, lead_ref[...], state_ref[...])


def gather_kernel(info_ref, lead_ref, *refs):
    pieces, (high_ref, low_ref, flow_ref, out_ref) = refs[:8], refs[8:]
    size = pieces[0].shape[1]
    half = pieces[0].shape[0]
    for shift in range(4):
        place = lax.rem(info_ref[3] + shift, 4)
        top, bottom = pieces[2 * shift][...], pieces[2 * shift + 1][...]
        rest = 2 * size - half
        high, low = split(top)
        high_ref[place, :half, :] = high
        low_ref[place, :half, :] = low
        high, low = split(bottom[:rest])
        high_ref[place, half:, :] = high
        low_ref[place, half:, :] = low
        flow_ref[place] = bottom[rest:]
    state = lead_ref[...]
    for item in range(4):
        index = item_of(info_ref, item)
        state = times(split(state), (high_ref[index], low_ref[index])) + flow_ref[index]
    out_ref[...] = state


def row_map_kernel(
    info_ref, high_ref, low_ref, flow_ref, row_high_ref, row_low_ref, row_flow_ref, half_ref
):
    maps, flows = [], []
    for item in range(4):
        index = item_of(info_ref, item)
        maps.append((high_ref[index], low_ref[index]))
        flows.append(flow_ref[index])
    size = high_ref.shape[2]
    early = times(maps[0], maps[1])
    early_flow = times(split(flows[0]), maps[1]) + flows[1]
    late = split(times(maps[2], maps[3]))
    late_flow = times(split(flows[2]), maps[3]) + flows[3]
    half_ref[: 2 * size, :] = early
    half_ref[2 * size :, :] = early_flow
    high, low = split(times(split(early), late))
    row_high_ref[...] = high
    row_low_ref[...] = low
    row_flow_ref[...] = times(split(early_flow), late) + late_flow


def row_kernel(info_ref, lead_ref, state_ref, high_ref, low_ref, flow_ref, out_ref):
    state = entry_state(info_ref, lead_ref, state_ref)
    out_ref[...] = times(split(state), (high_ref[...], low_ref[...])) + flow_ref[...]


def prefix_kernel(
    info_ref, high_ref, low_ref, flow_ref, half_ref, first_ref, x_ref, qa_ref, out_ref, inner_ref
):
    size = high_ref.shape[2]
    left = info_ref[0] == 0
    one, three = item_of(info_ref, 0), item_of(info_ref, 2)
    rows = lax.broadcasted_iota(jnp.int32, (2 * size + 32, size), 0)
    cols = lax.broadcasted_iota(jnp.int32, (2 * size + 32, size), 1)
    half = half_ref[...]
    third = (high_ref[three], low_ref[three])
    whole_row = times(split(half[: 2 * size]), third)
    whole_flow = times(split(half[2 * size :]), third) + flow_ref[three]
    none = (rows == cols).astype(F32)
    single = high_ref[one].astype(F32) + low_ref[one].astype(F32)
    single = jnp.concatenate([single, flow_ref[one]], axis=0)
    triple = jnp.concatenate([whole_row, whole_flow], axis=0)
    count = info_ref[2]
    low_half = jnp.where(count == 0, none, single)
    out_ref[...] = jnp.where(count < 2, low_half, jnp.where(count == 2, half, triple))
    second = split(x_ref[1])
    first = first_ref[...]
    inner_ref[: 2 * size, :] = jnp.where(left, times(split(first), second), first)
    inner_ref[2 * size :, :] = times(split(qa_ref[...]), second)


def entry_map_kernel(info_ref, prefix_ref, inner_ref, x_ref, high_ref, low_ref, flow_ref):
    size = x_ref.shape[2]
    left = info_ref[0] == 0
    prefix, flow = split(prefix_ref[: 2 * size, :]), split(prefix_ref[2 * size :, :])
    turn = split(x_ref[0])
    inner = split(inner_ref[: 2 * size, :])
    item_a = jnp.where(left, times(prefix, turn), prefix_ref[: 2 * size, :])
    flow_ref[0] = jnp.where(left, times(flow, turn), prefix_ref[2 * size :, :])
    item_b = times(prefix, inner)
    flow_ref[1] = times(flow, inner) + inner_ref[2 * size :, :]
    for item, value in enumerate((item_a, item_b)):
        high, low = split(value)
        high_ref[item] = high
        low_ref[item] = low


def inflow_kernel(
    info_ref, lead_ref, state_ref, high_ref, low_ref, flow_ref, spread_ref, out_ref
):
    out_ref[:, 64:, :] = spread_ref[...]
    state = split(entry_state(info_ref, lead_ref, state_ref))
    for item in range(2):
        value = times(state, (high_ref[item], low_ref[item])) + flow_ref[item]
        for dest in range(8):
            out_ref[dest, 32 * item : 32 * (item + 1), :] = value


def state_kernel(
    place_ref, inject_ref, last_ref, rows_ref, base_ref, extra_ref, left_ref, right_ref
):
    modes = inject_ref.shape[1]
    width = base_ref.shape[1]
    lead = rows_ref.shape[1] // 4
    for sweep, out_ref in enumerate((left_ref, right_ref)):
        target = jnp.broadcast_to(
            inject_ref[sweep : sweep + 1, :].astype(F32), (width, modes)
        ).T
        bases = []
        for part in range(2):
            start = (2 * sweep + part) * modes
            rows = unpacked_rows(place_ref, inject_ref, base_ref, sweep, part)
            bases.append(rows + extra_ref[start : start + modes, :])
        for slab in range(2):
            item = slab if sweep == 0 else 1 - slab
            pieces = []
            for part in range(2):
                start = item * 32 + part * 16
                for member in range(4):
                    pieces.append(last_ref[sweep * 4 + member, start : start + 16, :])
            parts = split(jnp.concatenate(pieces, axis=0))
            by = []
            for part in range(2):
                kind = 2 * sweep + part
                if slab == 0:
                    matrix = stacked(rows_ref, kind * lead, lead)
                else:
                    matrix = stacked(last_ref, 64 + kind * lead, lead)
                by.append(mm3(parts, split(matrix)))
            value = combined(by[0], by[1])
            chosen = target == (place_ref[0] + slab).astype(F32)
            for part in range(2):
                rows = value[part * modes : (part + 1) * modes]
                out_ref[slab, part] = jnp.where(chosen, bases[part], 0.0) + rows


def params(limit=LIMIT):
    return pltpu.CompilerParams(vmem_limit_bytes=limit)


def whole(shape):
    zeros = (0,) * len(shape)
    return pl.BlockSpec(shape, lambda *_: zeros)


SMEM = pl.BlockSpec(memory_space=pltpu.SMEM)
VMEM = pl.BlockSpec(memory_space=pltpu.VMEM)


def exchange(value):
    return lax.all_to_all(value, "col", split_axis=0, concat_axis=0, tiled=True)


def on_device(diag_inverse, couplings, sources, inject, leads):
    orbitals = diag_inverse.shape[2]
    width = diag_inverse.shape[3]
    size = couplings.shape[2]
    modes = sources.shape[3]
    lead = size // 8
    part_rows = orbitals // 8
    slabs = lax.axis_size("slab")
    slab_index = lax.axis_index("slab")
    col_index = lax.axis_index("col")
    team = col_index // 4
    member = col_index % 4
    first = slab_index * 2
    place = jnp.stack([first, jnp.zeros_like(first)]).astype(jnp.int32)
    position = jnp.where(team == 0, slab_index, slabs - 1 - slab_index)
    info = jnp.stack([team, position // 4, position % 4, slab_index % 4]).astype(jnp.int32)
    stack = 2 * (lead + 2 * modes)
    block_rows = 4 * lead + 32
    sources = jnp.transpose(sources, (0, 1, 3, 2))
    leads = jnp.transpose(leads, (0, 1, 3, 2))

    sent = pl.pallas_call(
        interface_kernel,
        grid=(4,),
        in_specs=[
            SMEM,
            whole(inject.shape),
            whole(sources.shape),
            pl.BlockSpec((1, 1, orbitals, width // 2), lambda step: (step // 2, step % 2, 0, 0)),
            pl.BlockSpec((1, 1, orbitals, width // 2), lambda step: (step // 2, step % 2, 0, 1)),
        ],
        out_specs=whole((8, block_rows, size)),
        out_shape=jax.ShapeDtypeStruct((8, block_rows, size), F32),
        scratch_shapes=[
            pltpu.VMEM((2, stack, width), BF16),
            pltpu.VMEM((2, stack, width), BF16),
            pltpu.VMEM((2, 2 * modes, size), F32),
        ],
        compiler_params=params(LARGE),
        name="interface_terms",
    )(place, inject, sources, diag_inverse, diag_inverse)
    sent, inject_after = lax.optimization_barrier((sent, inject))
    received = exchange(sent)

    def chunk_terms(place):
        terms = jax.ShapeDtypeStruct((2, 2 * lead + 4 * PACK, width), BF16)
        high, low = pl.pallas_call(
            select_kernel,
            in_specs=[SMEM, VMEM, VMEM],
            out_specs=[VMEM, VMEM],
            out_shape=[terms, terms],
            compiler_params=params(),
            name="select_terms",
        )(place, inject_after, sources)
        return pl.pallas_call(
            spread_kernel,
            grid=(8,),
            in_specs=[
                whole(terms.shape),
                whole(terms.shape),
                pl.BlockSpec((2, 2, part_rows, width), lambda step: (0, 0, step, 0)),
            ],
            out_specs=[
                pl.BlockSpec((1, 4 * lead, part_rows), lambda step: (step, 0, 0)),
                pl.BlockSpec((1, 4 * lead, part_rows), lambda step: (step, 0, 0)),
                pl.BlockSpec((1, 4 * PACK, part_rows), lambda step: (step, 0, 0)),
            ],
            out_shape=[
                jax.ShapeDtypeStruct((8, 4 * lead, part_rows), F32),
                jax.ShapeDtypeStruct((8, 4 * lead, part_rows), F32),
                jax.ShapeDtypeStruct((8, 4 * PACK, part_rows), F32),
            ],
            compiler_params=params(LARGE),
            name="spread_terms",
        )(high, low, diag_inverse)

    def summed(flows):
        return lax.psum_scatter(flows, "col", scatter_dimension=0, tiled=False)

    early, late, flows = chunk_terms(place)
    turned = pl.pallas_call(
        coupling_kernel,
        in_specs=[SMEM, VMEM],
        out_specs=VMEM,
        out_shape=jax.ShapeDtypeStruct((2, 2 * size, size), F32),
        compiler_params=params(),
        name="coupling_rows",
    )(info, couplings)
    own_inject = lax.dynamic_slice(inject, (team, member * 16), (1, 16))[0]
    own_inject = jnp.concatenate([own_inject, own_inject])
    marks = jnp.stack([own_inject == first + team, own_inject == first + 1 - team])
    marks = jnp.broadcast_to(marks.astype(F32)[:, :, None], (2, 32, size))
    own_lead = lax.dynamic_slice(leads, (team, 0, member * 16, 0), (1, 2, 16, size))
    own_lead = own_lead.reshape(32, size)
    base = summed(flows)
    owners = jnp.arange(slabs, dtype=jnp.int32)[:, None, None]
    counts = jnp.sum((inject_after[None] >> 1 == owners).astype(jnp.int32), axis=2)
    chunks = (jnp.max(counts) + PACK - 1) // PACK

    def more(chunk, extra):
        place = jnp.stack([first, chunk]).astype(jnp.int32)
        flows = chunk_terms(place)[2]
        return pl.pallas_call(
            expand_kernel,
            in_specs=[SMEM, VMEM, VMEM, VMEM],
            out_specs=VMEM,
            out_shape=jax.ShapeDtypeStruct((4 * modes, part_rows), F32),
            compiler_params=params(),
            name="expand_terms",
        )(place, inject, summed(flows), extra)

    extra = lax.fori_loop(1, chunks, more, jnp.zeros((4 * modes, part_rows), F32))
    received, turned, marks, own_lead, early, extra = lax.optimization_barrier(
        (received, turned, marks, own_lead, early, extra)
    )
    rows = exchange(early)

    top, bottom, flow_a, first_map = pl.pallas_call(
        pair_map_kernel,
        in_specs=[SMEM, VMEM, VMEM, VMEM],
        out_specs=[VMEM] * 4,
        out_shape=[
            jax.ShapeDtypeStruct((size + 16, size), F32),
            jax.ShapeDtypeStruct((size + 16, size), F32),
            jax.ShapeDtypeStruct((32, size), F32),
            jax.ShapeDtypeStruct((2 * size, size), F32),
        ],
        compiler_params=params(),
        name="pair_map",
    )(info, received, turned, marks)

    def turn(value, step):
        return lax.ppermute(
            value, "slab", [(slab, slab // 4 * 4 + (slab + step) % 4) for slab in range(slabs)]
        )

    before_top, after_bottom = turn(top, 1), turn(bottom, -1)
    before_bottom, after_top = turn(bottom, 1), turn(top, -1)
    across_top, across_bottom = turn(before_top, 1), turn(after_bottom, -1)
    pieces = (after_top, after_bottom, across_top, across_bottom, before_top, before_bottom)
    pieces, base = lax.optimization_barrier((pieces, base))
    row_maps = [
        jax.ShapeDtypeStruct((4, 2 * size, size), BF16),
        jax.ShapeDtypeStruct((4, 2 * size, size), BF16),
        jax.ShapeDtypeStruct((4, 32, size), F32),
    ]
    state_shape = jax.ShapeDtypeStruct((32, size), F32)
    *maps, flow = pl.pallas_call(
        gather_kernel,
        in_specs=[SMEM] + [VMEM] * 9,
        out_specs=[VMEM] * 4,
        out_shape=row_maps + [state_shape],
        compiler_params=params(),
        cost_estimate=pl.CostEstimate(flops=30000000000, bytes_accessed=0, transcendentals=0),
        name="gather_maps",
    )(info, own_lead, top, bottom, *pieces)

    cols = lax.axis_size("col")
    pairs = []
    for slab in range(slabs):
        for col in range(cols):
            target = (slab + (4 if col < 4 else -4)) % slabs
            pairs.append((slab * cols + col, target * cols + col))

    def local(kernel, name, shapes, *args):
        single = not isinstance(shapes, list)
        return pl.pallas_call(
            kernel,
            in_specs=[SMEM] + [VMEM] * (len(args) - 1),
            out_specs=VMEM if single else [VMEM] * len(shapes),
            out_shape=shapes,
            compiler_params=params(),
            name=name,
        )(*args)

    def hop(value):
        return lax.ppermute(value, ("slab", "col"), pairs)

    full = jax.ShapeDtypeStruct((2 * size + 32, size), F32)
    half_map = jax.ShapeDtypeStruct((2 * size, size), BF16)
    flow = hop(flow)
    *row_map, half_row = local(
        row_map_kernel, "row_map", [half_map, half_map, state_shape, full], info, *maps
    )
    flow = local(row_kernel, "row_step", state_shape, info, own_lead, flow, *row_map)
    flow, half_row = lax.optimization_barrier((flow, half_row))
    flow = hop(flow)
    prefix, inner_map = local(
        prefix_kernel,
        "prefix_map",
        [full, full],
        info,
        *maps,
        half_row,
        first_map,
        turned,
        flow_a,
    )
    flow = local(row_kernel, "row_step", state_shape, info, own_lead, flow, *row_map)
    flow, prefix, inner_map = lax.optimization_barrier((flow, prefix, inner_map))
    flow = hop(flow)
    two_maps = [
        jax.ShapeDtypeStruct((2, 2 * size, size), BF16),
        jax.ShapeDtypeStruct((2, 2 * size, size), BF16),
        jax.ShapeDtypeStruct((2, 32, size), F32),
    ]
    entry = local(entry_map_kernel, "entry_map", two_maps, info, prefix, inner_map, turned)
    last = local(
        inflow_kernel,
        "inflow",
        jax.ShapeDtypeStruct((8, 64 + 4 * lead, size), F32),
        info,
        own_lead,
        flow,
        *entry,
        late,
    )
    rows, last = lax.optimization_barrier((rows, last))
    last = exchange(last)
    last, rows, base, extra, inject = lax.optimization_barrier((last, rows, base, extra, inject))

    shape = jax.ShapeDtypeStruct((2, 2, modes, part_rows), F32)
    left, right = local(
        state_kernel, "states", [shape, shape], place, inject, last, rows, base, extra
    )
    return jnp.transpose(left, (0, 1, 3, 2)), jnp.transpose(right, (0, 1, 3, 2))


def solution(mesh):
    placed = (
        P(("energy", "slab"), None, None, "col"),
        P(("energy", "slab"), None, None, None),
        P("energy", None, "col", None),
        P(),
        P("energy", None, None, None),
    )

    return jax.shard_map(
        on_device,
        mesh=mesh,
        in_specs=placed,
        out_specs=(
            P(("energy", "slab"), None, "col", None),
            P(("energy", "slab"), None, "col", None),
        ),
        check_vma=False,
    )
```

```python
import jax
import jax.numpy as jnp
from jax import lax
from jax.experimental import pallas as pl
from jax.experimental.pallas import tpu as pltpu
from jax.sharding import PartitionSpec as P

F32 = jnp.float32
BF16 = jnp.bfloat16
LIMIT = 24 * 1024 * 1024
LARGE = 56 * 1024 * 1024
PACK = 16
LANES = 128


def split(value):
    high = value.astype(BF16)
    return high, (value - high.astype(F32)).astype(BF16)


def mm(left, right, transposed=False):
    dims = (((1,), (1 if transposed else 0,)), ((), ()))
    return lax.dot_general(left, right, dims, preferred_element_type=F32)


def mm3(left, right, transposed=False):
    rows = left[0].shape[0]
    wide = mm(jnp.concatenate(left, axis=0), right[0], transposed)
    return wide[:rows] + (wide[rows:] + mm(left[0], right[1], transposed))


def combined(by_real, by_imag):
    half = by_real.shape[0] // 2
    return jnp.concatenate(
        [by_real[:half] - by_imag[half:], by_imag[:half] + by_real[half:]], axis=0
    )


def complex_rows(left, right):
    parts = split(left)
    return combined(mm3(parts, split(right[0])), mm3(parts, split(right[1])))


def times(left, right):
    size = right[0].shape[0] // 2
    by_real = mm3(left, (right[0][:size], right[1][:size]))
    by_imag = mm3(left, (right[0][size:], right[1][size:]))
    return combined(by_real, by_imag)


def interface_kernel(
    place_ref, inject_ref, src_ref, g0_ref, g1_ref, out_ref, high_ref, low_ref, acc_ref
):
    step = pl.program_id(0)
    slab = step // 2
    plane = step % 2
    modes = src_ref.shape[2]
    width = src_ref.shape[3]

    @pl.when(step == 0)
    def _():
        rows = lax.broadcasted_iota(jnp.int32, (width // 8, width), 0)
        cols = lax.broadcasted_iota(jnp.int32, (width // 8, width), 1)
        targets = [
            jnp.broadcast_to(inject_ref[sweep : sweep + 1, :].astype(F32), (width, modes)).T
            for sweep in range(2)
        ]
        for local in range(2):
            pieces = []
            for sweep in range(2):
                pieces.append((cols == rows * 8 + sweep).astype(F32))
                chosen = targets[sweep] == (place_ref[0] + local).astype(F32)
                for part in range(2):
                    pieces.append(jnp.where(chosen, src_ref[sweep, part], 0.0))
            high, low = split(jnp.concatenate(pieces, axis=0))
            high_ref[local] = high
            low_ref[local] = low
        acc_ref[...] = jnp.zeros_like(acc_ref)

    half = high_ref.shape[1] // 2
    lead = width // 8
    count = g0_ref.shape[2] // 8
    for sweep in range(2):
        rows = jnp.concatenate(
            [ref[0, 0, pl.ds(1 - sweep, count, stride=8), :] for ref in (g0_ref, g1_ref)], axis=1
        )
        picked = pl.ds(sweep * half, half)
        term = mm3((high_ref[slab, picked, :], low_ref[slab, picked, :]), split(rows), True)
        order = slab if sweep == 0 else 1 - slab
        rows, lanes = out_ref.shape[1] // 2, out_ref.shape[2]
        for side in range(2):
            place = (order * 2 + plane) * lead + side * rows
            place = pl.ds(pl.multiple_of(place, 8), lead)
            for member in range(4):
                out_ref[sweep * 4 + member, place, :] = term[
                    :lead, side * lanes : (side + 1) * lanes
                ]
        real, imag = term[lead : lead + modes], term[lead + modes :]

        @pl.when(plane == 0)
        def _():
            acc_ref[sweep, :modes] += real
            acc_ref[sweep, modes:] += imag

        @pl.when(plane == 1)
        def _():
            acc_ref[sweep, :modes] -= imag
            acc_ref[sweep, modes:] += real

    @pl.when(step == 3)
    def _():
        for dest in range(8):
            sweep, member = divmod(dest, 4)
            for part in range(2):
                start = part * modes + member * 16
                put(out_ref, dest, 4 * lead + part * 16, acc_ref[sweep, start : start + 16, :])


def packed_columns(place_ref, inject_ref, sweep):
    modes = inject_ref.shape[1]
    target = inject_ref[sweep : sweep + 1, :]
    own = (target == place_ref[0]) | (target == place_ref[0] + 1)
    own = jnp.broadcast_to(own.astype(F32), (PACK, modes))
    earlier = lax.broadcasted_iota(jnp.int32, (modes, modes), 0)
    later = lax.broadcasted_iota(jnp.int32, (modes, modes), 1)
    rank = mm(own.astype(BF16), (earlier < later).astype(F32).astype(BF16))
    wanted = lax.broadcasted_iota(jnp.int32, (PACK, modes), 0) + PACK * place_ref[1]
    return jnp.where(rank == wanted.astype(F32), own, 0.0)


def unpacked_rows(place_ref, inject_ref, base_ref, sweep, part):
    back = packed_columns(place_ref, inject_ref, sweep).T.astype(BF16)
    start = (2 * sweep + part) * PACK
    high, low = split(base_ref[start : start + PACK, :])
    return mm(back, high) + mm(back, low)


def select_kernel(place_ref, inject_ref, src_ref, high_ref, low_ref):
    width = src_ref.shape[3]
    rows = lax.broadcasted_iota(jnp.int32, (width // 8, width), 0)
    cols = lax.broadcasted_iota(jnp.int32, (width // 8, width), 1)
    lead = width // 8
    for slab in range(2):
        for sweep in range(2):
            span = slice(sweep * lead, (sweep + 1) * lead)
            unit = (cols == rows * 8 + sweep).astype(F32)
            high_ref[slab, span, :] = unit.astype(BF16)
            low_ref[slab, span, :] = jnp.zeros_like(unit).astype(BF16)
            here = inject_ref[sweep : sweep + 1, :] == place_ref[0] + slab
            pick = jnp.where(here, packed_columns(place_ref, inject_ref, sweep), 0.0).astype(BF16)
            for part in range(2):
                start = 2 * lead + (2 * sweep + part) * PACK
                high, low = split(src_ref[sweep, part])
                high_ref[slab, start : start + PACK, :] = mm(pick, high).astype(BF16)
                low_ref[slab, start : start + PACK, :] = mm(pick, low).astype(BF16)


def spread_kernel(high_ref, low_ref, g_ref, early_ref, late_ref, flow_ref):
    lead = g_ref.shape[3] // 8
    total = [0.0] * 4
    for slab in range(2):
        parts = (high_ref[slab], low_ref[slab])
        real = mm3(parts, split(g_ref[slab, 0]), True)
        imag = mm3(parts, split(g_ref[slab, 1]), True)
        for sweep in range(2):
            base = sweep * lead
            place = sweep * 2 * lead
            out_ref = (early_ref, late_ref)[slab]
            put(out_ref, 0, place, real[base : base + lead])
            put(out_ref, 0, place + lead, imag[base : base + lead])
            one = 2 * lead + 2 * sweep * PACK
            two, three = one + PACK, one + 2 * PACK
            total[2 * sweep] += real[one:two] - imag[two:three]
            total[2 * sweep + 1] += real[two:three] + imag[one:two]
    for item in range(4):
        flow_ref[0, item * PACK : (item + 1) * PACK, :] = total[item]


def expand_kernel(place_ref, inject_ref, base_ref, extra_ref, out_ref):
    modes = inject_ref.shape[1]
    for sweep in range(2):
        for part in range(2):
            span = slice((2 * sweep + part) * modes, (2 * sweep + part + 1) * modes)
            rows = unpacked_rows(place_ref, inject_ref, base_ref, sweep, part)
            out_ref[span, :] = extra_ref[span, :] + rows


def coupling_kernel(team_ref, c_ref, x_ref):
    left = team_ref[0] == 0
    size = c_ref.shape[3]
    for slab in range(2):
        x_ref[slab, :size] = jnp.where(left, c_ref[slab, 0].T, c_ref[slab, 0])
        x_ref[slab, size:] = jnp.where(left, c_ref[slab, 1].T, -c_ref[slab, 1])


def put(ref, dest, start, value):
    rows, lanes = ref.shape[1] // 2, ref.shape[2]
    ref[dest, start : start + value.shape[0], :] = value[:, :lanes]
    ref[dest, rows + start : rows + start + value.shape[0], :] = value[:, lanes:]


def taken(ref, source, start, count):
    rows = ref.shape[1] // 2
    halves = [ref[source, base + start : base + start + count, :] for base in (0, rows)]
    return jnp.concatenate(halves, axis=1)


def stacked(ref, start, count):
    return jnp.concatenate([taken(ref, block, start, count) for block in range(8)], axis=0)


def pair_map_kernel(
    team_ref, recv_ref, x_ref, mask_ref, top_ref, bottom_ref, qa_ref, first_ref
):
    left = team_ref[0] == 0
    size = x_ref.shape[2]
    lead = size // 8
    coupled = [(x_ref[slab, :size], x_ref[slab, size:]) for slab in range(2)]
    blocks = [
        (stacked(recv_ref, 2 * item * lead, lead), stacked(recv_ref, (2 * item + 1) * lead, lead))
        for item in range(2)
    ]
    flow = taken(recv_ref, 0, 4 * lead, 32)
    for block in range(1, 8):
        flow = flow + taken(recv_ref, block, 4 * lead, 32)
    flow_a = jnp.where(mask_ref[0] != 0, flow, 0.0)
    flow_b = jnp.where(mask_ref[1] != 0, flow, 0.0)
    qa_ref[...] = flow_a

    def pick(one, two):
        return (jnp.where(left, one[0], two[0]), jnp.where(left, one[1], two[1]))

    def product(one, two):
        return complex_rows(jnp.concatenate(one, axis=0), two)

    first = product(pick(coupled[0], blocks[0]), pick(blocks[0], coupled[1]))
    second = product(pick(coupled[1], blocks[1]), pick(blocks[1], coupled[0]))
    second = (second[:size], second[size:])
    first_ref[...] = first
    lanes = size // 2
    both = complex_rows(first, second)
    flow_a = jnp.where(left, flow_a, complex_rows(flow_a, coupled[1]))
    flow_b = jnp.where(left, flow_b, complex_rows(flow_b, coupled[0]))
    flow = complex_rows(flow_a, second) + flow_b
    for side, out_ref in enumerate((top_ref, bottom_ref)):
        span = slice(side * lanes, (side + 1) * lanes)
        out_ref[: 2 * size, :] = both[:, span]
        out_ref[2 * size :, :] = flow[:, span]


def item_of(info_ref, item):
    return jnp.where(info_ref[0] == 0, item, 3 - item)


def entry_state(info_ref, lead_ref, state_ref):
    return jnp.where(info_ref[1] == 0, lead_ref[...], state_ref[...])


def gather_kernel(info_ref, lead_ref, *refs):
    pieces, (high_ref, low_ref, flow_ref, out_ref) = refs[:8], refs[8:]
    lanes = pieces[0].shape[1]
    count = 4 * lanes
    for shift in range(4):
        place = lax.rem(info_ref[3] + shift, 4)
        for side in range(2):
            piece = pieces[2 * shift + side]
            span = slice(side * lanes, (side + 1) * lanes)
            high, low = split(piece[:count, :])
            high_ref[place, :, span] = high
            low_ref[place, :, span] = low
            flow_ref[place, :, span] = piece[count:, :]
    state = lead_ref[...]
    for item in range(4):
        index = item_of(info_ref, item)
        state = times(split(state), (high_ref[index], low_ref[index])) + flow_ref[index]
    out_ref[...] = state


def row_map_kernel(
    info_ref, high_ref, low_ref, flow_ref, row_high_ref, row_low_ref, row_flow_ref, half_ref
):
    maps, flows = [], []
    for item in range(4):
        index = item_of(info_ref, item)
        maps.append((high_ref[index], low_ref[index]))
        flows.append(flow_ref[index])
    size = high_ref.shape[2]
    early = times(maps[0], maps[1])
    early_flow = times(split(flows[0]), maps[1]) + flows[1]
    late = split(times(maps[2], maps[3]))
    late_flow = times(split(flows[2]), maps[3]) + flows[3]
    half_ref[: 2 * size, :] = early
    half_ref[2 * size :, :] = early_flow
    high, low = split(times(split(early), late))
    row_high_ref[...] = high
    row_low_ref[...] = low
    row_flow_ref[...] = times(split(early_flow), late) + late_flow


def row_kernel(info_ref, lead_ref, state_ref, high_ref, low_ref, flow_ref, out_ref):
    state = entry_state(info_ref, lead_ref, state_ref)
    out_ref[...] = times(split(state), (high_ref[...], low_ref[...])) + flow_ref[...]


def prefix_kernel(
    info_ref, high_ref, low_ref, flow_ref, half_ref, first_ref, x_ref, qa_ref, out_ref, inner_ref
):
    size = high_ref.shape[2]
    left = info_ref[0] == 0
    one, three = item_of(info_ref, 0), item_of(info_ref, 2)
    rows = lax.broadcasted_iota(jnp.int32, (2 * size + 32, size), 0)
    cols = lax.broadcasted_iota(jnp.int32, (2 * size + 32, size), 1)
    half = half_ref[...]
    third = (high_ref[three], low_ref[three])
    whole_row = times(split(half[: 2 * size]), third)
    whole_flow = times(split(half[2 * size :]), third) + flow_ref[three]
    none = (rows == cols).astype(F32)
    single = high_ref[one].astype(F32) + low_ref[one].astype(F32)
    single = jnp.concatenate([single, flow_ref[one]], axis=0)
    triple = jnp.concatenate([whole_row, whole_flow], axis=0)
    count = info_ref[2]
    low_half = jnp.where(count == 0, none, single)
    out_ref[...] = jnp.where(count < 2, low_half, jnp.where(count == 2, half, triple))
    second = split(x_ref[1])
    first = first_ref[...]
    inner_ref[: 2 * size, :] = jnp.where(left, times(split(first), second), first)
    inner_ref[2 * size :, :] = times(split(qa_ref[...]), second)


def entry_map_kernel(info_ref, prefix_ref, inner_ref, x_ref, high_ref, low_ref, flow_ref):
    size = x_ref.shape[2]
    left = info_ref[0] == 0
    prefix, flow = split(prefix_ref[: 2 * size, :]), split(prefix_ref[2 * size :, :])
    turn = split(x_ref[0])
    inner = split(inner_ref[: 2 * size, :])
    item_a = jnp.where(left, times(prefix, turn), prefix_ref[: 2 * size, :])
    flow_ref[0] = jnp.where(left, times(flow, turn), prefix_ref[2 * size :, :])
    item_b = times(prefix, inner)
    flow_ref[1] = times(flow, inner) + inner_ref[2 * size :, :]
    for item, value in enumerate((item_a, item_b)):
        high, low = split(value)
        high_ref[item] = high
        low_ref[item] = low


def inflow_kernel(
    info_ref, lead_ref, state_ref, high_ref, low_ref, flow_ref, spread_ref, out_ref
):
    rows, late = out_ref.shape[1] // 2, spread_ref.shape[1] // 2
    for side in range(2):
        out_ref[:, side * rows + 64 : (side + 1) * rows, :] = spread_ref[
            :, side * late : (side + 1) * late, :
        ]
    state = split(entry_state(info_ref, lead_ref, state_ref))
    for item in range(2):
        value = times(state, (high_ref[item], low_ref[item])) + flow_ref[item]
        for dest in range(8):
            put(out_ref, dest, 32 * item, value)


def state_kernel(
    place_ref, inject_ref, last_ref, rows_ref, base_ref, extra_ref, left_ref, right_ref
):
    modes = inject_ref.shape[1]
    width = base_ref.shape[1]
    lead = rows_ref.shape[1] // 8
    for sweep, out_ref in enumerate((left_ref, right_ref)):
        target = jnp.broadcast_to(
            inject_ref[sweep : sweep + 1, :].astype(F32), (width, modes)
        ).T
        bases = []
        for part in range(2):
            start = (2 * sweep + part) * modes
            rows = unpacked_rows(place_ref, inject_ref, base_ref, sweep, part)
            bases.append(rows + extra_ref[start : start + modes, :])
        for slab in range(2):
            item = slab if sweep == 0 else 1 - slab
            pieces = []
            for part in range(2):
                start = item * 32 + part * 16
                for member in range(4):
                    pieces.append(taken(last_ref, sweep * 4 + member, start, 16))
            parts = split(jnp.concatenate(pieces, axis=0))
            by = []
            for part in range(2):
                kind = 2 * sweep + part
                if slab == 0:
                    matrix = stacked(rows_ref, kind * lead, lead)
                else:
                    matrix = stacked(last_ref, 64 + kind * lead, lead)
                by.append(mm3(parts, split(matrix)))
            value = combined(by[0], by[1])
            chosen = target == (place_ref[0] + slab).astype(F32)
            for part in range(2):
                rows = value[part * modes : (part + 1) * modes]
                out_ref[slab, part] = jnp.where(chosen, bases[part], 0.0) + rows


def params(limit=LIMIT):
    return pltpu.CompilerParams(vmem_limit_bytes=limit)


def whole(shape):
    zeros = (0,) * len(shape)
    return pl.BlockSpec(shape, lambda *_: zeros)


SMEM = pl.BlockSpec(memory_space=pltpu.SMEM)
VMEM = pl.BlockSpec(memory_space=pltpu.VMEM)


def exchange(value):
    return lax.all_to_all(value, "col", split_axis=0, concat_axis=0, tiled=True)


def on_device(diag_inverse, couplings, sources, inject, leads):
    orbitals = diag_inverse.shape[2]
    width = diag_inverse.shape[3]
    size = couplings.shape[2]
    modes = sources.shape[3]
    lead = size // 8
    part_rows = orbitals // 8
    slabs = lax.axis_size("slab")
    slab_index = lax.axis_index("slab")
    col_index = lax.axis_index("col")
    team = col_index // 4
    member = col_index % 4
    first = slab_index * 2
    place = jnp.stack([first, jnp.zeros_like(first)]).astype(jnp.int32)
    position = jnp.where(team == 0, slab_index, slabs - 1 - slab_index)
    info = jnp.stack([team, position // 4, position % 4, slab_index % 4]).astype(jnp.int32)
    stack = 2 * (lead + 2 * modes)
    block_rows = 4 * lead + 32
    sources = jnp.transpose(sources, (0, 1, 3, 2))
    leads = jnp.transpose(leads, (0, 1, 3, 2))

    sent = pl.pallas_call(
        interface_kernel,
        grid=(4,),
        in_specs=[
            SMEM,
            whole(inject.shape),
            whole(sources.shape),
            pl.BlockSpec((1, 1, orbitals, width // 2), lambda step: (step // 2, step % 2, 0, 0)),
            pl.BlockSpec((1, 1, orbitals, width // 2), lambda step: (step // 2, step % 2, 0, 1)),
        ],
        out_specs=whole((8, 2 * block_rows, LANES)),
        out_shape=jax.ShapeDtypeStruct((8, 2 * block_rows, LANES), F32),
        scratch_shapes=[
            pltpu.VMEM((2, stack, width), BF16),
            pltpu.VMEM((2, stack, width), BF16),
            pltpu.VMEM((2, 2 * modes, size), F32),
        ],
        compiler_params=params(LARGE),
        name="interface_terms",
    )(place, inject, sources, diag_inverse, diag_inverse)
    sent, inject_after = lax.optimization_barrier((sent, inject))
    received = exchange(sent)

    def chunk_terms(place):
        terms = jax.ShapeDtypeStruct((2, 2 * lead + 4 * PACK, width), BF16)
        high, low = pl.pallas_call(
            select_kernel,
            in_specs=[SMEM, VMEM, VMEM],
            out_specs=[VMEM, VMEM],
            out_shape=[terms, terms],
            compiler_params=params(),
            name="select_terms",
        )(place, inject_after, sources)
        return pl.pallas_call(
            spread_kernel,
            grid=(8,),
            in_specs=[
                whole(terms.shape),
                whole(terms.shape),
                pl.BlockSpec((2, 2, part_rows, width), lambda step: (0, 0, step, 0)),
            ],
            out_specs=[
                pl.BlockSpec((1, 8 * lead, LANES), lambda step: (step, 0, 0)),
                pl.BlockSpec((1, 8 * lead, LANES), lambda step: (step, 0, 0)),
                pl.BlockSpec((1, 4 * PACK, part_rows), lambda step: (step, 0, 0)),
            ],
            out_shape=[
                jax.ShapeDtypeStruct((8, 8 * lead, LANES), F32),
                jax.ShapeDtypeStruct((8, 8 * lead, LANES), F32),
                jax.ShapeDtypeStruct((8, 4 * PACK, part_rows), F32),
            ],
            compiler_params=params(LARGE),
            name="spread_terms",
        )(high, low, diag_inverse)

    def summed(flows):
        return lax.psum_scatter(flows, "col", scatter_dimension=0, tiled=False)

    early, late, flows = chunk_terms(place)
    turned = pl.pallas_call(
        coupling_kernel,
        in_specs=[SMEM, VMEM],
        out_specs=VMEM,
        out_shape=jax.ShapeDtypeStruct((2, 2 * size, size), F32),
        compiler_params=params(),
        name="coupling_rows",
    )(info, couplings)
    own_inject = lax.dynamic_slice(inject, (team, member * 16), (1, 16))[0]
    own_inject = jnp.concatenate([own_inject, own_inject])
    marks = jnp.stack([own_inject == first + team, own_inject == first + 1 - team])
    marks = jnp.broadcast_to(marks.astype(F32)[:, :, None], (2, 32, size))
    own_lead = lax.dynamic_slice(leads, (team, 0, member * 16, 0), (1, 2, 16, size))
    own_lead = own_lead.reshape(32, size)
    base = summed(flows)
    owners = jnp.arange(slabs, dtype=jnp.int32)[:, None, None]
    counts = jnp.sum((inject_after[None] >> 1 == owners).astype(jnp.int32), axis=2)
    chunks = (jnp.max(counts) + PACK - 1) // PACK

    def more(chunk, extra):
        place = jnp.stack([first, chunk]).astype(jnp.int32)
        flows = chunk_terms(place)[2]
        return pl.pallas_call(
            expand_kernel,
            in_specs=[SMEM, VMEM, VMEM, VMEM],
            out_specs=VMEM,
            out_shape=jax.ShapeDtypeStruct((4 * modes, part_rows), F32),
            compiler_params=params(),
            name="expand_terms",
        )(place, inject, summed(flows), extra)

    extra = lax.fori_loop(1, chunks, more, jnp.zeros((4 * modes, part_rows), F32))
    received, turned, marks, own_lead, early, extra = lax.optimization_barrier(
        (received, turned, marks, own_lead, early, extra)
    )
    rows = exchange(early)

    top, bottom, flow_a, first_map = pl.pallas_call(
        pair_map_kernel,
        in_specs=[SMEM, VMEM, VMEM, VMEM],
        out_specs=[VMEM] * 4,
        out_shape=[
            jax.ShapeDtypeStruct((2 * size + 32, size // 2), F32),
            jax.ShapeDtypeStruct((2 * size + 32, size // 2), F32),
            jax.ShapeDtypeStruct((32, size), F32),
            jax.ShapeDtypeStruct((2 * size, size), F32),
        ],
        compiler_params=params(),
        name="pair_map",
    )(info, received, turned, marks)

    def turn(value, step):
        return lax.ppermute(
            value, "slab", [(slab, slab // 4 * 4 + (slab + step) % 4) for slab in range(slabs)]
        )

    before_top, after_bottom = turn(top, 1), turn(bottom, -1)
    before_bottom, after_top = turn(bottom, 1), turn(top, -1)
    across_top, across_bottom = turn(before_top, 1), turn(after_bottom, -1)
    pieces = (after_top, after_bottom, across_top, across_bottom, before_top, before_bottom)
    pieces, base = lax.optimization_barrier((pieces, base))
    row_maps = [
        jax.ShapeDtypeStruct((4, 2 * size, size), BF16),
        jax.ShapeDtypeStruct((4, 2 * size, size), BF16),
        jax.ShapeDtypeStruct((4, 32, size), F32),
    ]
    state_shape = jax.ShapeDtypeStruct((32, size), F32)
    *maps, flow = pl.pallas_call(
        gather_kernel,
        in_specs=[SMEM] + [VMEM] * 9,
        out_specs=[VMEM] * 4,
        out_shape=row_maps + [state_shape],
        compiler_params=params(),
        cost_estimate=pl.CostEstimate(flops=30000000000, bytes_accessed=0, transcendentals=0),
        name="gather_maps",
    )(info, own_lead, top, bottom, *pieces)

    cols = lax.axis_size("col")
    pairs = []
    for slab in range(slabs):
        for col in range(cols):
            target = (slab + (4 if col < 4 else -4)) % slabs
            pairs.append((slab * cols + col, target * cols + col))

    def local(kernel, name, shapes, *args):
        single = not isinstance(shapes, list)
        return pl.pallas_call(
            kernel,
            in_specs=[SMEM] + [VMEM] * (len(args) - 1),
            out_specs=VMEM if single else [VMEM] * len(shapes),
            out_shape=shapes,
            compiler_params=params(),
            name=name,
        )(*args)

    def hop(value):
        return lax.ppermute(value, ("slab", "col"), pairs)

    full = jax.ShapeDtypeStruct((2 * size + 32, size), F32)
    half_map = jax.ShapeDtypeStruct((2 * size, size), BF16)
    flow = hop(flow)
    *row_map, half_row = local(
        row_map_kernel, "row_map", [half_map, half_map, state_shape, full], info, *maps
    )
    flow = local(row_kernel, "row_step", state_shape, info, own_lead, flow, *row_map)
    flow, half_row = lax.optimization_barrier((flow, half_row))
    flow = hop(flow)
    prefix, inner_map = local(
        prefix_kernel,
        "prefix_map",
        [full, full],
        info,
        *maps,
        half_row,
        first_map,
        turned,
        flow_a,
    )
    flow = local(row_kernel, "row_step", state_shape, info, own_lead, flow, *row_map)
    flow, prefix, inner_map = lax.optimization_barrier((flow, prefix, inner_map))
    flow = hop(flow)
    two_maps = [
        jax.ShapeDtypeStruct((2, 2 * size, size), BF16),
        jax.ShapeDtypeStruct((2, 2 * size, size), BF16),
        jax.ShapeDtypeStruct((2, 32, size), F32),
    ]
    entry = local(entry_map_kernel, "entry_map", two_maps, info, prefix, inner_map, turned)
    last = local(
        inflow_kernel,
        "inflow",
        jax.ShapeDtypeStruct((8, 2 * (64 + 4 * lead), LANES), F32),
        info,
        own_lead,
        flow,
        *entry,
        late,
    )
    rows, last = lax.optimization_barrier((rows, last))
    last = exchange(last)
    last, rows, base, extra, inject = lax.optimization_barrier((last, rows, base, extra, inject))

    shape = jax.ShapeDtypeStruct((2, 2, modes, part_rows), F32)
    left, right = local(
        state_kernel, "states", [shape, shape], place, inject, last, rows, base, extra
    )
    return jnp.transpose(left, (0, 1, 3, 2)), jnp.transpose(right, (0, 1, 3, 2))


def solution(mesh):
    placed = (
        P(("energy", "slab"), None, None, "col"),
        P(("energy", "slab"), None, None, None),
        P("energy", None, "col", None),
        P(),
        P("energy", None, None, None),
    )

    return jax.shard_map(
        on_device,
        mesh=mesh,
        in_specs=placed,
        out_specs=(
            P(("energy", "slab"), None, "col", None),
            P(("energy", "slab"), None, "col", None),
        ),
        check_vma=False,
    )
```

```python
import jax
import jax.numpy as jnp
from jax import lax
from jax.experimental import pallas as pl
from jax.experimental.pallas import tpu as pltpu
from jax.sharding import PartitionSpec as P

F32 = jnp.float32
BF16 = jnp.bfloat16
LIMIT = 24 * 1024 * 1024
LARGE = 56 * 1024 * 1024
PACK = 16
LANES = 128


def split(value):
    high = value.astype(BF16)
    return high, (value - high.astype(F32)).astype(BF16)


def mm(left, right, transposed=False):
    dims = (((1,), (1 if transposed else 0,)), ((), ()))
    return lax.dot_general(left, right, dims, preferred_element_type=F32)


def mm3(left, right, transposed=False):
    rows = left[0].shape[0]
    wide = mm(jnp.concatenate(left, axis=0), right[0], transposed)
    return wide[:rows] + (wide[rows:] + mm(left[0], right[1], transposed))


def combined(by_real, by_imag):
    half = by_real.shape[0] // 2
    return jnp.concatenate(
        [by_real[:half] - by_imag[half:], by_imag[:half] + by_real[half:]], axis=0
    )


def complex_rows(left, right):
    parts = split(left)
    return combined(mm3(parts, split(right[0])), mm3(parts, split(right[1])))


def times(left, right):
    size = right[0].shape[0] // 2
    by_real = mm3(left, (right[0][:size], right[1][:size]))
    by_imag = mm3(left, (right[0][size:], right[1][size:]))
    return combined(by_real, by_imag)


def interface_kernel(
    place_ref, inject_ref, src_ref, g0_ref, g1_ref, out_ref, high_ref, low_ref, acc_ref
):
    step = pl.program_id(0)
    slab = step // 2
    plane = step % 2
    modes = src_ref.shape[2]
    width = src_ref.shape[3]

    @pl.when(step == 0)
    def _():
        rows = lax.broadcasted_iota(jnp.int32, (width // 8, width), 0)
        cols = lax.broadcasted_iota(jnp.int32, (width // 8, width), 1)
        targets = [
            jnp.broadcast_to(inject_ref[sweep : sweep + 1, :].astype(F32), (width, modes)).T
            for sweep in range(2)
        ]
        for local in range(2):
            pieces = []
            for sweep in range(2):
                pieces.append((cols == rows * 8 + sweep).astype(F32))
                chosen = targets[sweep] == (place_ref[0] + local).astype(F32)
                for part in range(2):
                    pieces.append(jnp.where(chosen, src_ref[sweep, part], 0.0))
            high, low = split(jnp.concatenate(pieces, axis=0))
            high_ref[local] = high
            low_ref[local] = low
        acc_ref[...] = jnp.zeros_like(acc_ref)

    half = high_ref.shape[1] // 2
    lead = width // 8
    count = g0_ref.shape[2] // 8
    for sweep in range(2):
        rows = jnp.concatenate(
            [ref[0, 0, pl.ds(1 - sweep, count, stride=8), :] for ref in (g0_ref, g1_ref)], axis=1
        )
        picked = pl.ds(sweep * half, half)
        term = mm3((high_ref[slab, picked, :], low_ref[slab, picked, :]), split(rows), True)
        order = slab if sweep == 0 else 1 - slab
        rows, lanes = out_ref.shape[1] // 2, out_ref.shape[2]
        for side in range(2):
            place = (order * 2 + plane) * lead + side * rows
            place = pl.ds(pl.multiple_of(place, 8), lead)
            for member in range(4):
                out_ref[sweep * 4 + member, place, :] = term[
                    :lead, side * lanes : (side + 1) * lanes
                ]
        real, imag = term[lead : lead + modes], term[lead + modes :]

        @pl.when(plane == 0)
        def _():
            acc_ref[sweep, :modes] += real
            acc_ref[sweep, modes:] += imag

        @pl.when(plane == 1)
        def _():
            acc_ref[sweep, :modes] -= imag
            acc_ref[sweep, modes:] += real

    @pl.when(step == 3)
    def _():
        for dest in range(8):
            sweep, member = divmod(dest, 4)
            for part in range(2):
                start = part * modes + member * 16
                put(out_ref, dest, 4 * lead + part * 16, acc_ref[sweep, start : start + 16, :])


def packed_columns(place_ref, inject_ref, sweep):
    modes = inject_ref.shape[1]
    target = inject_ref[sweep : sweep + 1, :]
    own = (target == place_ref[0]) | (target == place_ref[0] + 1)
    own = jnp.broadcast_to(own.astype(F32), (PACK, modes))
    earlier = lax.broadcasted_iota(jnp.int32, (modes, modes), 0)
    later = lax.broadcasted_iota(jnp.int32, (modes, modes), 1)
    rank = mm(own.astype(BF16), (earlier < later).astype(F32).astype(BF16))
    wanted = lax.broadcasted_iota(jnp.int32, (PACK, modes), 0) + PACK * place_ref[1]
    return jnp.where(rank == wanted.astype(F32), own, 0.0)


def unpacked_rows(place_ref, inject_ref, base_ref, sweep, part):
    back = packed_columns(place_ref, inject_ref, sweep).T.astype(BF16)
    start = (2 * sweep + part) * PACK
    high, low = split(base_ref[start : start + PACK, :])
    return mm(back, high) + mm(back, low)


def select_kernel(place_ref, inject_ref, src_ref, high_ref, low_ref):
    width = src_ref.shape[3]
    rows = lax.broadcasted_iota(jnp.int32, (width // 8, width), 0)
    cols = lax.broadcasted_iota(jnp.int32, (width // 8, width), 1)
    lead = width // 8
    for slab in range(2):
        for sweep in range(2):
            span = slice(sweep * lead, (sweep + 1) * lead)
            unit = (cols == rows * 8 + sweep).astype(F32)
            high_ref[slab, span, :] = unit.astype(BF16)
            low_ref[slab, span, :] = jnp.zeros_like(unit).astype(BF16)
            here = inject_ref[sweep : sweep + 1, :] == place_ref[0] + slab
            pick = jnp.where(here, packed_columns(place_ref, inject_ref, sweep), 0.0).astype(BF16)
            for part in range(2):
                start = 2 * lead + (2 * sweep + part) * PACK
                high, low = split(src_ref[sweep, part])
                high_ref[slab, start : start + PACK, :] = mm(pick, high).astype(BF16)
                low_ref[slab, start : start + PACK, :] = mm(pick, low).astype(BF16)


def spread_kernel(high_ref, low_ref, g_ref, out_ref, flow_ref):
    lead = g_ref.shape[3] // 8
    total = [0.0] * 4
    for slab in range(2):
        parts = (high_ref[slab], low_ref[slab])
        real = mm3(parts, split(g_ref[slab, 0]), True)
        imag = mm3(parts, split(g_ref[slab, 1]), True)
        for sweep in range(2):
            base = sweep * lead
            place = slab * 4 * lead + sweep * 2 * lead
            put(out_ref, 0, place, real[base : base + lead])
            put(out_ref, 0, place + lead, imag[base : base + lead])
            one = 2 * lead + 2 * sweep * PACK
            two, three = one + PACK, one + 2 * PACK
            total[2 * sweep] += real[one:two] - imag[two:three]
            total[2 * sweep + 1] += real[two:three] + imag[one:two]
    for item in range(4):
        flow_ref[0, item * PACK : (item + 1) * PACK, :] = total[item]


def expand_kernel(place_ref, inject_ref, base_ref, extra_ref, out_ref):
    modes = inject_ref.shape[1]
    for sweep in range(2):
        for part in range(2):
            span = slice((2 * sweep + part) * modes, (2 * sweep + part + 1) * modes)
            rows = unpacked_rows(place_ref, inject_ref, base_ref, sweep, part)
            out_ref[span, :] = extra_ref[span, :] + rows


def coupling_kernel(team_ref, c_ref, x_ref):
    left = team_ref[0] == 0
    size = c_ref.shape[3]
    for slab in range(2):
        x_ref[slab, :size] = jnp.where(left, c_ref[slab, 0].T, c_ref[slab, 0])
        x_ref[slab, size:] = jnp.where(left, c_ref[slab, 1].T, -c_ref[slab, 1])


def put(ref, dest, start, value):
    rows, lanes = ref.shape[1] // 2, ref.shape[2]
    ref[dest, start : start + value.shape[0], :] = value[:, :lanes]
    ref[dest, rows + start : rows + start + value.shape[0], :] = value[:, lanes:]


def taken(ref, source, start, count):
    rows = ref.shape[1] // 2
    halves = [ref[source, base + start : base + start + count, :] for base in (0, rows)]
    return jnp.concatenate(halves, axis=1)


def stacked(ref, start, count):
    return jnp.concatenate([taken(ref, block, start, count) for block in range(8)], axis=0)


def pair_map_kernel(
    team_ref, recv_ref, x_ref, mask_ref, top_ref, bottom_ref, qa_ref, first_ref
):
    left = team_ref[0] == 0
    size = x_ref.shape[2]
    lead = size // 8
    coupled = [(x_ref[slab, :size], x_ref[slab, size:]) for slab in range(2)]
    blocks = [
        (stacked(recv_ref, 2 * item * lead, lead), stacked(recv_ref, (2 * item + 1) * lead, lead))
        for item in range(2)
    ]
    flow = taken(recv_ref, 0, 4 * lead, 32)
    for block in range(1, 8):
        flow = flow + taken(recv_ref, block, 4 * lead, 32)
    flow_a = jnp.where(mask_ref[0] != 0, flow, 0.0)
    flow_b = jnp.where(mask_ref[1] != 0, flow, 0.0)
    qa_ref[...] = flow_a

    def pick(one, two):
        return (jnp.where(left, one[0], two[0]), jnp.where(left, one[1], two[1]))

    def product(one, two):
        return complex_rows(jnp.concatenate(one, axis=0), two)

    first = product(pick(coupled[0], blocks[0]), pick(blocks[0], coupled[1]))
    second = product(pick(coupled[1], blocks[1]), pick(blocks[1], coupled[0]))
    second = (second[:size], second[size:])
    first_ref[...] = first
    lanes = size // 2
    both = complex_rows(first, second)
    flow_a = jnp.where(left, flow_a, complex_rows(flow_a, coupled[1]))
    flow_b = jnp.where(left, flow_b, complex_rows(flow_b, coupled[0]))
    flow = complex_rows(flow_a, second) + flow_b
    for side, out_ref in enumerate((top_ref, bottom_ref)):
        span = slice(side * lanes, (side + 1) * lanes)
        out_ref[: 2 * size, :] = both[:, span]
        out_ref[2 * size :, :] = flow[:, span]


def item_of(info_ref, item):
    return jnp.where(info_ref[0] == 0, item, 3 - item)


def entry_state(info_ref, lead_ref, state_ref):
    return jnp.where(info_ref[1] == 0, lead_ref[...], state_ref[...])


def gather_kernel(info_ref, lead_ref, *refs):
    pieces, (high_ref, low_ref, flow_ref, out_ref) = refs[:8], refs[8:]
    lanes = pieces[0].shape[1]
    count = 4 * lanes
    for shift in range(4):
        place = lax.rem(info_ref[3] + shift, 4)
        for side in range(2):
            piece = pieces[2 * shift + side]
            span = slice(side * lanes, (side + 1) * lanes)
            high, low = split(piece[:count, :])
            high_ref[place, :, span] = high
            low_ref[place, :, span] = low
            flow_ref[place, :, span] = piece[count:, :]
    state = lead_ref[...]
    for item in range(4):
        index = item_of(info_ref, item)
        state = times(split(state), (high_ref[index], low_ref[index])) + flow_ref[index]
    out_ref[...] = state


def row_map_kernel(
    info_ref, high_ref, low_ref, flow_ref, row_high_ref, row_low_ref, row_flow_ref, half_ref
):
    maps, flows = [], []
    for item in range(4):
        index = item_of(info_ref, item)
        maps.append((high_ref[index], low_ref[index]))
        flows.append(flow_ref[index])
    size = high_ref.shape[2]
    early = times(maps[0], maps[1])
    early_flow = times(split(flows[0]), maps[1]) + flows[1]
    late = split(times(maps[2], maps[3]))
    late_flow = times(split(flows[2]), maps[3]) + flows[3]
    half_ref[: 2 * size, :] = early
    half_ref[2 * size :, :] = early_flow
    high, low = split(times(split(early), late))
    row_high_ref[...] = high
    row_low_ref[...] = low
    row_flow_ref[...] = times(split(early_flow), late) + late_flow


def row_kernel(info_ref, lead_ref, state_ref, high_ref, low_ref, flow_ref, out_ref):
    state = entry_state(info_ref, lead_ref, state_ref)
    out_ref[...] = times(split(state), (high_ref[...], low_ref[...])) + flow_ref[...]


def prefix_kernel(
    info_ref, high_ref, low_ref, flow_ref, half_ref, first_ref, x_ref, qa_ref, out_ref, inner_ref
):
    size = high_ref.shape[2]
    left = info_ref[0] == 0
    one, three = item_of(info_ref, 0), item_of(info_ref, 2)
    rows = lax.broadcasted_iota(jnp.int32, (2 * size + 32, size), 0)
    cols = lax.broadcasted_iota(jnp.int32, (2 * size + 32, size), 1)
    half = half_ref[...]
    third = (high_ref[three], low_ref[three])
    whole_row = times(split(half[: 2 * size]), third)
    whole_flow = times(split(half[2 * size :]), third) + flow_ref[three]
    none = (rows == cols).astype(F32)
    single = high_ref[one].astype(F32) + low_ref[one].astype(F32)
    single = jnp.concatenate([single, flow_ref[one]], axis=0)
    triple = jnp.concatenate([whole_row, whole_flow], axis=0)
    count = info_ref[2]
    low_half = jnp.where(count == 0, none, single)
    out_ref[...] = jnp.where(count < 2, low_half, jnp.where(count == 2, half, triple))
    second = split(x_ref[1])
    first = first_ref[...]
    inner_ref[: 2 * size, :] = jnp.where(left, times(split(first), second), first)
    inner_ref[2 * size :, :] = times(split(qa_ref[...]), second)


def entry_map_kernel(info_ref, prefix_ref, inner_ref, x_ref, high_ref, low_ref, flow_ref):
    size = x_ref.shape[2]
    left = info_ref[0] == 0
    prefix, flow = split(prefix_ref[: 2 * size, :]), split(prefix_ref[2 * size :, :])
    turn = split(x_ref[0])
    inner = split(inner_ref[: 2 * size, :])
    item_a = jnp.where(left, times(prefix, turn), prefix_ref[: 2 * size, :])
    flow_ref[0] = jnp.where(left, times(flow, turn), prefix_ref[2 * size :, :])
    item_b = times(prefix, inner)
    flow_ref[1] = times(flow, inner) + inner_ref[2 * size :, :]
    for item, value in enumerate((item_a, item_b)):
        high, low = split(value)
        high_ref[item] = high
        low_ref[item] = low


def inflow_kernel(info_ref, lead_ref, state_ref, high_ref, low_ref, flow_ref, out_ref):
    state = split(entry_state(info_ref, lead_ref, state_ref))
    for item in range(2):
        value = times(state, (high_ref[item], low_ref[item])) + flow_ref[item]
        for dest in range(8):
            put(out_ref, dest, 32 * item, value)


def arrange_kernel(
    place_ref, inject_ref, recv_ref, base_ref, extra_ref, high_ref, low_ref, out_ref
):
    lead = recv_ref.shape[1] // 16
    modes = inject_ref.shape[1]
    width = base_ref.shape[1]
    for slab in range(2):
        for kind in range(4):
            high, low = split(stacked(recv_ref, (slab * 4 + kind) * lead, lead))
            sweep, part = divmod(kind, 2)
            high_ref[slab, sweep, part] = high
            low_ref[slab, sweep, part] = low
    for sweep in range(2):
        target = jnp.broadcast_to(
            inject_ref[sweep : sweep + 1, :].astype(F32), (width, modes)
        ).T
        for part in range(2):
            start = (2 * sweep + part) * modes
            rows = unpacked_rows(place_ref, inject_ref, base_ref, sweep, part)
            rows = rows + extra_ref[start : start + modes, :]
            for slab in range(2):
                chosen = target == (place_ref[0] + slab).astype(F32)
                out_ref[sweep, slab, part] = jnp.where(chosen, rows, 0.0)


def state_kernel(last_ref, high_ref, low_ref, base_ref, left_ref, right_ref):
    modes = base_ref.shape[3]
    for sweep, out_ref in enumerate((left_ref, right_ref)):
        for slab in range(2):
            item = slab if sweep == 0 else 1 - slab
            pieces = []
            for part in range(2):
                start = item * 32 + part * 16
                for member in range(4):
                    pieces.append(taken(last_ref, sweep * 4 + member, start, 16))
            parts = split(jnp.concatenate(pieces, axis=0))
            by = [
                mm3(parts, (high_ref[slab, sweep, part], low_ref[slab, sweep, part]))
                for part in range(2)
            ]
            value = combined(by[0], by[1])
            for part in range(2):
                rows = value[part * modes : (part + 1) * modes]
                out_ref[slab, part] = base_ref[sweep, slab, part] + rows


def params(limit=LIMIT):
    return pltpu.CompilerParams(vmem_limit_bytes=limit)


def whole(shape):
    zeros = (0,) * len(shape)
    return pl.BlockSpec(shape, lambda *_: zeros)


SMEM = pl.BlockSpec(memory_space=pltpu.SMEM)
VMEM = pl.BlockSpec(memory_space=pltpu.VMEM)


def exchange(value):
    return lax.all_to_all(value, "col", split_axis=0, concat_axis=0, tiled=True)


def on_device(diag_inverse, couplings, sources, inject, leads):
    orbitals = diag_inverse.shape[2]
    width = diag_inverse.shape[3]
    size = couplings.shape[2]
    modes = sources.shape[3]
    lead = size // 8
    part_rows = orbitals // 8
    slabs = lax.axis_size("slab")
    slab_index = lax.axis_index("slab")
    col_index = lax.axis_index("col")
    team = col_index // 4
    member = col_index % 4
    first = slab_index * 2
    place = jnp.stack([first, jnp.zeros_like(first)]).astype(jnp.int32)
    position = jnp.where(team == 0, slab_index, slabs - 1 - slab_index)
    info = jnp.stack([team, position // 4, position % 4, slab_index % 4]).astype(jnp.int32)
    stack = 2 * (lead + 2 * modes)
    block_rows = 4 * lead + 32
    sources = jnp.transpose(sources, (0, 1, 3, 2))
    leads = jnp.transpose(leads, (0, 1, 3, 2))

    sent = pl.pallas_call(
        interface_kernel,
        grid=(4,),
        in_specs=[
            SMEM,
            whole(inject.shape),
            whole(sources.shape),
            pl.BlockSpec((1, 1, orbitals, width // 2), lambda step: (step // 2, step % 2, 0, 0)),
            pl.BlockSpec((1, 1, orbitals, width // 2), lambda step: (step // 2, step % 2, 0, 1)),
        ],
        out_specs=whole((8, 2 * block_rows, LANES)),
        out_shape=jax.ShapeDtypeStruct((8, 2 * block_rows, LANES), F32),
        scratch_shapes=[
            pltpu.VMEM((2, stack, width), BF16),
            pltpu.VMEM((2, stack, width), BF16),
            pltpu.VMEM((2, 2 * modes, size), F32),
        ],
        compiler_params=params(LARGE),
        name="interface_terms",
    )(place, inject, sources, diag_inverse, diag_inverse)
    sent, inject_after = lax.optimization_barrier((sent, inject))
    received = exchange(sent)

    def chunk_terms(place):
        terms = jax.ShapeDtypeStruct((2, 2 * lead + 4 * PACK, width), BF16)
        high, low = pl.pallas_call(
            select_kernel,
            in_specs=[SMEM, VMEM, VMEM],
            out_specs=[VMEM, VMEM],
            out_shape=[terms, terms],
            compiler_params=params(),
            name="select_terms",
        )(place, inject_after, sources)
        return pl.pallas_call(
            spread_kernel,
            grid=(8,),
            in_specs=[
                whole(terms.shape),
                whole(terms.shape),
                pl.BlockSpec((2, 2, part_rows, width), lambda step: (0, 0, step, 0)),
            ],
            out_specs=[
                pl.BlockSpec((1, 16 * lead, LANES), lambda step: (step, 0, 0)),
                pl.BlockSpec((1, 4 * PACK, part_rows), lambda step: (step, 0, 0)),
            ],
            out_shape=[
                jax.ShapeDtypeStruct((8, 16 * lead, LANES), F32),
                jax.ShapeDtypeStruct((8, 4 * PACK, part_rows), F32),
            ],
            compiler_params=params(LARGE),
            name="spread_terms",
        )(high, low, diag_inverse)

    def summed(flows):
        return lax.psum_scatter(flows, "col", scatter_dimension=0, tiled=False)

    spread, flows = chunk_terms(place)
    turned = pl.pallas_call(
        coupling_kernel,
        in_specs=[SMEM, VMEM],
        out_specs=VMEM,
        out_shape=jax.ShapeDtypeStruct((2, 2 * size, size), F32),
        compiler_params=params(),
        name="coupling_rows",
    )(info, couplings)
    own_inject = lax.dynamic_slice(inject, (team, member * 16), (1, 16))[0]
    own_inject = jnp.concatenate([own_inject, own_inject])
    marks = jnp.stack([own_inject == first + team, own_inject == first + 1 - team])
    marks = jnp.broadcast_to(marks.astype(F32)[:, :, None], (2, 32, size))
    own_lead = lax.dynamic_slice(leads, (team, 0, member * 16, 0), (1, 2, 16, size))
    own_lead = own_lead.reshape(32, size)
    base = summed(flows)
    owners = jnp.arange(slabs, dtype=jnp.int32)[:, None, None]
    counts = jnp.sum((inject_after[None] >> 1 == owners).astype(jnp.int32), axis=2)
    chunks = (jnp.max(counts) + PACK - 1) // PACK

    def more(chunk, extra):
        place = jnp.stack([first, chunk]).astype(jnp.int32)
        flows = chunk_terms(place)[1]
        return pl.pallas_call(
            expand_kernel,
            in_specs=[SMEM, VMEM, VMEM, VMEM],
            out_specs=VMEM,
            out_shape=jax.ShapeDtypeStruct((4 * modes, part_rows), F32),
            compiler_params=params(),
            name="expand_terms",
        )(place, inject, summed(flows), extra)

    extra = lax.fori_loop(1, chunks, more, jnp.zeros((4 * modes, part_rows), F32))
    received, turned, marks, own_lead, spread, extra = lax.optimization_barrier(
        (received, turned, marks, own_lead, spread, extra)
    )
    rows = exchange(spread)

    top, bottom, flow_a, first_map = pl.pallas_call(
        pair_map_kernel,
        in_specs=[SMEM, VMEM, VMEM, VMEM],
        out_specs=[VMEM] * 4,
        out_shape=[
            jax.ShapeDtypeStruct((2 * size + 32, size // 2), F32),
            jax.ShapeDtypeStruct((2 * size + 32, size // 2), F32),
            jax.ShapeDtypeStruct((32, size), F32),
            jax.ShapeDtypeStruct((2 * size, size), F32),
        ],
        compiler_params=params(),
        name="pair_map",
    )(info, received, turned, marks)

    def turn(value, step):
        return lax.ppermute(
            value, "slab", [(slab, slab // 4 * 4 + (slab + step) % 4) for slab in range(slabs)]
        )

    before_top, after_bottom = turn(top, 1), turn(bottom, -1)
    before_bottom, after_top = turn(bottom, 1), turn(top, -1)
    across_top, across_bottom = turn(before_top, 1), turn(after_bottom, -1)
    pieces = (after_top, after_bottom, across_top, across_bottom, before_top, before_bottom)
    row_maps = [
        jax.ShapeDtypeStruct((4, 2 * size, size), BF16),
        jax.ShapeDtypeStruct((4, 2 * size, size), BF16),
        jax.ShapeDtypeStruct((4, 32, size), F32),
    ]
    state_shape = jax.ShapeDtypeStruct((32, size), F32)
    *maps, flow = pl.pallas_call(
        gather_kernel,
        in_specs=[SMEM] + [VMEM] * 9,
        out_specs=[VMEM] * 4,
        out_shape=row_maps + [state_shape],
        compiler_params=params(),
        name="gather_maps",
    )(info, own_lead, top, bottom, *pieces)

    cols = lax.axis_size("col")
    pairs = []
    for slab in range(slabs):
        for col in range(cols):
            target = (slab + (4 if col < 4 else -4)) % slabs
            pairs.append((slab * cols + col, target * cols + col))

    def local(kernel, name, shapes, *args):
        single = not isinstance(shapes, list)
        return pl.pallas_call(
            kernel,
            in_specs=[SMEM] + [VMEM] * (len(args) - 1),
            out_specs=VMEM if single else [VMEM] * len(shapes),
            out_shape=shapes,
            compiler_params=params(),
            name=name,
        )(*args)

    def hop(value):
        return lax.ppermute(value, ("slab", "col"), pairs)

    full = jax.ShapeDtypeStruct((2 * size + 32, size), F32)
    half_map = jax.ShapeDtypeStruct((2 * size, size), BF16)
    flow = hop(flow)
    *row_map, half_row = local(
        row_map_kernel, "row_map", [half_map, half_map, state_shape, full], info, *maps
    )
    flow = local(row_kernel, "row_step", state_shape, info, own_lead, flow, *row_map)
    flow, half_row = lax.optimization_barrier((flow, half_row))
    flow = hop(flow)
    prefix, inner_map = local(
        prefix_kernel,
        "prefix_map",
        [full, full],
        info,
        *maps,
        half_row,
        first_map,
        turned,
        flow_a,
    )
    flow = local(row_kernel, "row_step", state_shape, info, own_lead, flow, *row_map)
    flow, prefix, inner_map = lax.optimization_barrier((flow, prefix, inner_map))
    flow = hop(flow)
    two_maps = [
        jax.ShapeDtypeStruct((2, 2 * size, size), BF16),
        jax.ShapeDtypeStruct((2, 2 * size, size), BF16),
        jax.ShapeDtypeStruct((2, 32, size), F32),
    ]
    entry = local(entry_map_kernel, "entry_map", two_maps, info, prefix, inner_map, turned)
    last = local(
        inflow_kernel,
        "inflow",
        jax.ShapeDtypeStruct((8, 2 * 64, LANES), F32),
        info,
        own_lead,
        flow,
        *entry,
    )
    rows, base, last = lax.optimization_barrier((rows, base, last))
    last = exchange(last)
    arranged = [
        jax.ShapeDtypeStruct((2, 2, 2, size, part_rows), BF16),
        jax.ShapeDtypeStruct((2, 2, 2, size, part_rows), BF16),
        jax.ShapeDtypeStruct((2, 2, 2, modes, part_rows), F32),
    ]
    arranged = local(
        arrange_kernel, "arrange_rows", arranged, place, inject, rows, base, extra
    )

    shape = jax.ShapeDtypeStruct((2, 2, modes, part_rows), F32)
    left, right = pl.pallas_call(
        state_kernel,
        in_specs=[VMEM] * 4,
        out_specs=[VMEM, VMEM],
        out_shape=[shape, shape],
        compiler_params=params(),
        name="states",
    )(last, *arranged)
    return jnp.transpose(left, (0, 1, 3, 2)), jnp.transpose(right, (0, 1, 3, 2))


def solution(mesh):
    placed = (
        P(("energy", "slab"), None, None, "col"),
        P(("energy", "slab"), None, None, None),
        P("energy", None, "col", None),
        P(),
        P("energy", None, None, None),
    )

    return jax.shard_map(
        on_device,
        mesh=mesh,
        in_specs=placed,
        out_specs=(
            P(("energy", "slab"), None, "col", None),
            P(("energy", "slab"), None, "col", None),
        ),
        check_vma=False,
    )
```

```python
import jax
import jax.numpy as jnp
from jax import lax
from jax.experimental import pallas as pl
from jax.experimental.pallas import tpu as pltpu
from jax.sharding import PartitionSpec as P

F32 = jnp.float32
BF16 = jnp.bfloat16
LIMIT = 24 * 1024 * 1024
LARGE = 56 * 1024 * 1024
PACK = 16
LANES = 128
SHARE = 32


def split(value):
    high = value.astype(BF16)
    return high, (value - high.astype(F32)).astype(BF16)


def mm(left, right, transposed=False):
    dims = (((1,), (1 if transposed else 0,)), ((), ()))
    return lax.dot_general(left, right, dims, preferred_element_type=F32)


def mm3(left, right, transposed=False):
    rows = left[0].shape[0]
    wide = mm(jnp.concatenate(left, axis=0), right[0], transposed)
    return wide[:rows] + (wide[rows:] + mm(left[0], right[1], transposed))


def combined(by_real, by_imag):
    half = by_real.shape[0] // 2
    return jnp.concatenate(
        [by_real[:half] - by_imag[half:], by_imag[:half] + by_real[half:]], axis=0
    )


def complex_rows(left, right):
    parts = split(left)
    return combined(mm3(parts, split(right[0])), mm3(parts, split(right[1])))


def times(left, right):
    size = right[0].shape[0] // 2
    by_real = mm3(left, (right[0][:size], right[1][:size]))
    by_imag = mm3(left, (right[0][size:], right[1][size:]))
    return combined(by_real, by_imag)


def interface_kernel(
    place_ref, inject_ref, src_ref, g0_ref, g1_ref, *refs
):
    out_refs, (high_ref, low_ref, acc_ref, columns_ref) = refs[:4], refs[4:]
    step = pl.program_id(0)
    slab = step // 2
    plane = step % 2
    modes = src_ref.shape[2]
    width = src_ref.shape[3]

    @pl.when(step == 0)
    def _():
        rows = lax.broadcasted_iota(jnp.int32, (width // 8, width), 0)
        cols = lax.broadcasted_iota(jnp.int32, (width // 8, width), 1)
        targets = [
            jnp.broadcast_to(inject_ref[sweep : sweep + 1, :].astype(F32), (width, modes)).T
            for sweep in range(2)
        ]
        for local in range(2):
            pieces = []
            for sweep in range(2):
                pieces.append((cols == rows * 8 + sweep).astype(F32))
                chosen = targets[sweep] == (place_ref[0] + local).astype(F32)
                for part in range(2):
                    pieces.append(jnp.where(chosen, src_ref[sweep, part], 0.0))
            high, low = split(jnp.concatenate(pieces, axis=0))
            high_ref[local] = high
            low_ref[local] = low
        acc_ref[...] = jnp.zeros_like(acc_ref)

    half = high_ref.shape[1] // 2
    lead = width // 8
    count = g0_ref.shape[2] // 8
    for sweep in range(2):
        rows = jnp.concatenate(
            [ref[0, 0, pl.ds(1 - sweep, count, stride=8), :] for ref in (g0_ref, g1_ref)], axis=1
        )
        picked = pl.ds(sweep * half, half)
        term = mm3((high_ref[slab, picked, :], low_ref[slab, picked, :]), split(rows), True)
        order = slab if sweep == 0 else 1 - slab
        span = pl.ds(pl.multiple_of((order * 2 + plane) * lead, lead), lead)
        columns_ref[sweep, span, :] = term[:lead]
        real, imag = term[lead : lead + modes], term[lead + modes :]

        @pl.when(plane == 0)
        def _():
            acc_ref[sweep, :modes] += real
            acc_ref[sweep, modes:] += imag

        @pl.when(plane == 1)
        def _():
            acc_ref[sweep, :modes] -= imag
            acc_ref[sweep, modes:] += real

    @pl.when(step == 3)
    def _():
        for turn, out_ref in enumerate(out_refs):
            worker = lax.rem((place_ref[2] + 1) // 2 + turn, 4)
            sweep, half = lax.rem(worker, 2), worker // 2
            out_ref[: 4 * lead, :] = columns_ref[sweep]
            for part in range(2):
                start = pl.multiple_of(part * modes + half * SHARE, 8)
                place = 4 * lead + part * SHARE
                out_ref[place : place + SHARE, :] = acc_ref[sweep, pl.ds(start, SHARE), :]


def packed_columns(place_ref, inject_ref, sweep):
    modes = inject_ref.shape[1]
    target = inject_ref[sweep : sweep + 1, :]
    own = (target == place_ref[0]) | (target == place_ref[0] + 1)
    own = jnp.broadcast_to(own.astype(F32), (PACK, modes))
    earlier = lax.broadcasted_iota(jnp.int32, (modes, modes), 0)
    later = lax.broadcasted_iota(jnp.int32, (modes, modes), 1)
    rank = mm(own.astype(BF16), (earlier < later).astype(F32).astype(BF16))
    wanted = lax.broadcasted_iota(jnp.int32, (PACK, modes), 0) + PACK * place_ref[1]
    return jnp.where(rank == wanted.astype(F32), own, 0.0)


def unpacked_rows(place_ref, inject_ref, base_ref, sweep, part):
    back = packed_columns(place_ref, inject_ref, sweep).T.astype(BF16)
    start = (2 * sweep + part) * PACK
    high, low = split(base_ref[start : start + PACK, :])
    return mm(back, high) + mm(back, low)


def select_kernel(place_ref, inject_ref, src_ref, high_ref, low_ref):
    width = src_ref.shape[3]
    rows = lax.broadcasted_iota(jnp.int32, (width // 8, width), 0)
    cols = lax.broadcasted_iota(jnp.int32, (width // 8, width), 1)
    lead = width // 8
    for slab in range(2):
        for sweep in range(2):
            span = slice(sweep * lead, (sweep + 1) * lead)
            unit = (cols == rows * 8 + sweep).astype(F32)
            high_ref[slab, span, :] = unit.astype(BF16)
            low_ref[slab, span, :] = jnp.zeros_like(unit).astype(BF16)
            here = inject_ref[sweep : sweep + 1, :] == place_ref[0] + slab
            pick = jnp.where(here, packed_columns(place_ref, inject_ref, sweep), 0.0).astype(BF16)
            for part in range(2):
                start = 2 * lead + (2 * sweep + part) * PACK
                high, low = split(src_ref[sweep, part])
                high_ref[slab, start : start + PACK, :] = mm(pick, high).astype(BF16)
                low_ref[slab, start : start + PACK, :] = mm(pick, low).astype(BF16)


def spread_kernel(high_ref, low_ref, g_ref, out_ref, flow_ref):
    lead = g_ref.shape[3] // 8
    total = [0.0] * 4
    for slab in range(2):
        parts = (high_ref[slab], low_ref[slab])
        real = mm3(parts, split(g_ref[slab, 0]), True)
        imag = mm3(parts, split(g_ref[slab, 1]), True)
        for sweep in range(2):
            base = sweep * lead
            place = slab * 4 * lead + sweep * 2 * lead
            put(out_ref, 0, place, real[base : base + lead])
            put(out_ref, 0, place + lead, imag[base : base + lead])
            one = 2 * lead + 2 * sweep * PACK
            two, three = one + PACK, one + 2 * PACK
            total[2 * sweep] += real[one:two] - imag[two:three]
            total[2 * sweep + 1] += real[two:three] + imag[one:two]
    for item in range(4):
        flow_ref[0, item * PACK : (item + 1) * PACK, :] = total[item]


def expand_kernel(place_ref, inject_ref, base_ref, extra_ref, out_ref):
    modes = inject_ref.shape[1]
    for sweep in range(2):
        for part in range(2):
            span = slice((2 * sweep + part) * modes, (2 * sweep + part + 1) * modes)
            rows = unpacked_rows(place_ref, inject_ref, base_ref, sweep, part)
            out_ref[span, :] = extra_ref[span, :] + rows


def coupling_kernel(team_ref, c_ref, x_ref):
    left = team_ref[0] == 0
    size = c_ref.shape[3]
    for slab in range(2):
        x_ref[slab, :size] = jnp.where(left, c_ref[slab, 0].T, c_ref[slab, 0])
        x_ref[slab, size:] = jnp.where(left, c_ref[slab, 1].T, -c_ref[slab, 1])


def put(ref, dest, start, value):
    rows, lanes = ref.shape[1] // 2, ref.shape[2]
    ref[dest, start : start + value.shape[0], :] = value[:, :lanes]
    ref[dest, rows + start : rows + start + value.shape[0], :] = value[:, lanes:]


def taken(ref, source, start, count):
    rows = ref.shape[1] // 2
    halves = [ref[source, base + start : base + start + count, :] for base in (0, rows)]
    return jnp.concatenate(halves, axis=1)


def stacked(ref, start, count):
    return jnp.concatenate([taken(ref, block, start, count) for block in range(8)], axis=0)


def pair_map_kernel(info_ref, x_ref, mask_ref, *refs):
    recv_refs, (top_ref, bottom_ref, qa_ref, first_ref, block_ref) = refs[:8], refs[8:]
    left = info_ref[0] == 0
    size = x_ref.shape[2]
    lead = size // 8
    coupled = [(x_ref[slab, :size], x_ref[slab, size:]) for slab in range(2)]
    flow = 0.0
    for away, recv_ref in enumerate(recv_refs):
        source = lax.rem(info_ref[4] + 8 - away, 8)
        span = pl.ds(pl.multiple_of(source * lead, lead), lead)
        for item in range(4):
            block_ref[item, span, :] = recv_ref[item * lead : (item + 1) * lead, :]
        flow = flow + recv_ref[4 * lead :, :]
    blocks = [(block_ref[2 * item], block_ref[2 * item + 1]) for item in range(2)]
    flow_a = jnp.where(mask_ref[0] != 0, flow, 0.0)
    flow_b = jnp.where(mask_ref[1] != 0, flow, 0.0)
    qa_ref[...] = flow_a

    def pick(one, two):
        return (jnp.where(left, one[0], two[0]), jnp.where(left, one[1], two[1]))

    def product(one, two):
        return complex_rows(jnp.concatenate(one, axis=0), two)

    first = product(pick(coupled[0], blocks[0]), pick(blocks[0], coupled[1]))
    second = product(pick(coupled[1], blocks[1]), pick(blocks[1], coupled[0]))
    second = (second[:size], second[size:])
    first_ref[...] = first
    lanes = size // 2
    both = complex_rows(first, second)
    flow_a = jnp.where(left, flow_a, complex_rows(flow_a, coupled[1]))
    flow_b = jnp.where(left, flow_b, complex_rows(flow_b, coupled[0]))
    flow = complex_rows(flow_a, second) + flow_b
    for side, out_ref in enumerate((top_ref, bottom_ref)):
        span = slice(side * lanes, (side + 1) * lanes)
        out_ref[: 2 * size, :] = both[:, span]
        out_ref[2 * size :, :] = flow[:, span]


def item_of(info_ref, item):
    return jnp.where(info_ref[0] == 0, item, 3 - item)


def entry_state(info_ref, lead_ref, state_ref):
    return jnp.where(info_ref[1] == 0, lead_ref[...], state_ref[...])


def gather_kernel(info_ref, lead_ref, *refs):
    pieces, (high_ref, low_ref, flow_ref, out_ref) = refs[:8], refs[8:]
    lanes = pieces[0].shape[1]
    count = 4 * lanes
    for shift in range(4):
        place = lax.rem(info_ref[3] + shift, 4)
        for side in range(2):
            piece = pieces[2 * shift + side]
            span = slice(side * lanes, (side + 1) * lanes)
            high, low = split(piece[:count, :])
            high_ref[place, :, span] = high
            low_ref[place, :, span] = low
            flow_ref[place, :, span] = piece[count:, :]
    state = lead_ref[...]
    for item in range(4):
        index = item_of(info_ref, item)
        state = times(split(state), (high_ref[index], low_ref[index])) + flow_ref[index]
    out_ref[...] = state


def row_map_kernel(
    info_ref, high_ref, low_ref, flow_ref, row_high_ref, row_low_ref, row_flow_ref, half_ref
):
    maps, flows = [], []
    for item in range(4):
        index = item_of(info_ref, item)
        maps.append((high_ref[index], low_ref[index]))
        flows.append(flow_ref[index])
    size = high_ref.shape[2]
    early = times(maps[0], maps[1])
    early_flow = times(split(flows[0]), maps[1]) + flows[1]
    late = split(times(maps[2], maps[3]))
    late_flow = times(split(flows[2]), maps[3]) + flows[3]
    half_ref[: 2 * size, :] = early
    half_ref[2 * size :, :] = early_flow
    high, low = split(times(split(early), late))
    row_high_ref[...] = high
    row_low_ref[...] = low
    row_flow_ref[...] = times(split(early_flow), late) + late_flow


def row_kernel(info_ref, lead_ref, state_ref, high_ref, low_ref, flow_ref, out_ref):
    state = entry_state(info_ref, lead_ref, state_ref)
    out_ref[...] = times(split(state), (high_ref[...], low_ref[...])) + flow_ref[...]


def prefix_kernel(
    info_ref, high_ref, low_ref, flow_ref, half_ref, first_ref, x_ref, qa_ref, out_ref, inner_ref
):
    size = high_ref.shape[2]
    left = info_ref[0] == 0
    one, three = item_of(info_ref, 0), item_of(info_ref, 2)
    rows = lax.broadcasted_iota(jnp.int32, (2 * size + 2 * SHARE, size), 0)
    cols = lax.broadcasted_iota(jnp.int32, (2 * size + 2 * SHARE, size), 1)
    half = half_ref[...]
    third = (high_ref[three], low_ref[three])
    whole_row = times(split(half[: 2 * size]), third)
    whole_flow = times(split(half[2 * size :]), third) + flow_ref[three]
    none = (rows == cols).astype(F32)
    single = high_ref[one].astype(F32) + low_ref[one].astype(F32)
    single = jnp.concatenate([single, flow_ref[one]], axis=0)
    triple = jnp.concatenate([whole_row, whole_flow], axis=0)
    count = info_ref[2]
    low_half = jnp.where(count == 0, none, single)
    out_ref[...] = jnp.where(count < 2, low_half, jnp.where(count == 2, half, triple))
    second = split(x_ref[1])
    first = first_ref[...]
    inner_ref[: 2 * size, :] = jnp.where(left, times(split(first), second), first)
    inner_ref[2 * size :, :] = times(split(qa_ref[...]), second)


def entry_map_kernel(info_ref, prefix_ref, inner_ref, x_ref, high_ref, low_ref, flow_ref):
    size = x_ref.shape[2]
    left = info_ref[0] == 0
    prefix, flow = split(prefix_ref[: 2 * size, :]), split(prefix_ref[2 * size :, :])
    turn = split(x_ref[0])
    inner = split(inner_ref[: 2 * size, :])
    item_a = jnp.where(left, times(prefix, turn), prefix_ref[: 2 * size, :])
    flow_ref[0] = jnp.where(left, times(flow, turn), prefix_ref[2 * size :, :])
    item_b = times(prefix, inner)
    flow_ref[1] = times(flow, inner) + inner_ref[2 * size :, :]
    for item, value in enumerate((item_a, item_b)):
        high, low = split(value)
        high_ref[item] = high
        low_ref[item] = low


def inflow_kernel(info_ref, lead_ref, state_ref, high_ref, low_ref, flow_ref, out_ref):
    state = split(entry_state(info_ref, lead_ref, state_ref))
    for item in range(2):
        value = times(state, (high_ref[item], low_ref[item])) + flow_ref[item]
        out_ref[2 * SHARE * item : 2 * SHARE * (item + 1), :] = value


def arrange_kernel(
    place_ref, inject_ref, recv_ref, base_ref, extra_ref, high_ref, low_ref, out_ref
):
    lead = recv_ref.shape[1] // 16
    modes = inject_ref.shape[1]
    width = base_ref.shape[1]
    for slab in range(2):
        for kind in range(4):
            high, low = split(stacked(recv_ref, (slab * 4 + kind) * lead, lead))
            sweep, part = divmod(kind, 2)
            high_ref[slab, sweep, part] = high
            low_ref[slab, sweep, part] = low
    for sweep in range(2):
        target = jnp.broadcast_to(
            inject_ref[sweep : sweep + 1, :].astype(F32), (width, modes)
        ).T
        for part in range(2):
            start = (2 * sweep + part) * modes
            rows = unpacked_rows(place_ref, inject_ref, base_ref, sweep, part)
            rows = rows + extra_ref[start : start + modes, :]
            for slab in range(2):
                chosen = target == (place_ref[0] + slab).astype(F32)
                out_ref[sweep, slab, part] = jnp.where(chosen, rows, 0.0)


def state_kernel(place_ref, high_ref, low_ref, base_ref, *refs):
    recv_refs, (left_ref, right_ref, inner_ref) = refs[:8], refs[8:]
    modes = base_ref.shape[3]
    for away, recv_ref in enumerate(recv_refs):
        source = lax.rem(place_ref[2] + 8 - away, 8)

        @pl.when(lax.rem(source, 2) == 0)
        def _(source=source, recv_ref=recv_ref):
            inner_ref[source // 2] = recv_ref[...]

    for sweep, out_ref in enumerate((left_ref, right_ref)):
        for slab in range(2):
            item = slab if sweep == 0 else 1 - slab
            pieces = []
            for part in range(2):
                start = (item * 2 + part) * SHARE
                for half in range(2):
                    pieces.append(inner_ref[sweep + 2 * half, start : start + SHARE, :])
            parts = split(jnp.concatenate(pieces, axis=0))
            by = [
                mm3(parts, (high_ref[slab, sweep, part], low_ref[slab, sweep, part]))
                for part in range(2)
            ]
            value = combined(by[0], by[1])
            for part in range(2):
                rows = value[part * modes : (part + 1) * modes]
                out_ref[slab, part] = base_ref[sweep, slab, part] + rows


def params(limit=LIMIT):
    return pltpu.CompilerParams(vmem_limit_bytes=limit)


def whole(shape):
    zeros = (0,) * len(shape)
    return pl.BlockSpec(shape, lambda *_: zeros)


SMEM = pl.BlockSpec(memory_space=pltpu.SMEM)
VMEM = pl.BlockSpec(memory_space=pltpu.VMEM)


def exchange(value):
    return lax.all_to_all(value, "col", split_axis=0, concat_axis=0, tiled=True)


def on_device(diag_inverse, couplings, sources, inject, leads):
    orbitals = diag_inverse.shape[2]
    width = diag_inverse.shape[3]
    size = couplings.shape[2]
    modes = sources.shape[3]
    lead = size // 8
    part_rows = orbitals // 8
    slabs = lax.axis_size("slab")
    slab_index = lax.axis_index("slab")
    col_index = lax.axis_index("col")
    team = col_index // 2 % 2
    member = col_index // 4
    first = slab_index * 2
    place = jnp.stack([first, jnp.zeros_like(first), col_index]).astype(jnp.int32)
    position = jnp.where(team == 0, slab_index, slabs - 1 - slab_index)
    info = [team, position // 4, position % 4, slab_index % 4, col_index]
    info = jnp.stack(info).astype(jnp.int32)
    stack = 2 * (lead + 2 * modes)
    block = jax.ShapeDtypeStruct((4 * lead + 2 * SHARE, size), F32)
    sources = jnp.transpose(sources, (0, 1, 3, 2))
    leads = jnp.transpose(leads, (0, 1, 3, 2))

    sent = pl.pallas_call(
        interface_kernel,
        grid=(4,),
        in_specs=[
            SMEM,
            whole(inject.shape),
            whole(sources.shape),
            pl.BlockSpec((1, 1, orbitals, width // 2), lambda step: (step // 2, step % 2, 0, 0)),
            pl.BlockSpec((1, 1, orbitals, width // 2), lambda step: (step // 2, step % 2, 0, 1)),
        ],
        out_specs=[whole(block.shape)] * 4,
        out_shape=[block] * 4,
        scratch_shapes=[
            pltpu.VMEM((2, stack, width), BF16),
            pltpu.VMEM((2, stack, width), BF16),
            pltpu.VMEM((2, 2 * modes, size), F32),
            pltpu.VMEM((2, 4 * lead, size), F32),
        ],
        compiler_params=params(LARGE),
        name="interface_terms",
    )(place, inject, sources, diag_inverse, diag_inverse)
    received = [sent[0]] + [
        lax.ppermute(
            sent[away // 2],
            "col",
            [(col, (col + away) % 8) for col in range(8) if (col + away) % 2 == 0],
        )
        for away in range(1, 8)
    ]
    received[1], received[7], inject_after = lax.optimization_barrier(
        (received[1], received[7], inject)
    )

    def chunk_terms(place):
        terms = jax.ShapeDtypeStruct((2, 2 * lead + 4 * PACK, width), BF16)
        high, low = pl.pallas_call(
            select_kernel,
            in_specs=[SMEM, VMEM, VMEM],
            out_specs=[VMEM, VMEM],
            out_shape=[terms, terms],
            compiler_params=params(),
            name="select_terms",
        )(place, inject_after, sources)
        return pl.pallas_call(
            spread_kernel,
            grid=(8,),
            in_specs=[
                whole(terms.shape),
                whole(terms.shape),
                pl.BlockSpec((2, 2, part_rows, width), lambda step: (0, 0, step, 0)),
            ],
            out_specs=[
                pl.BlockSpec((1, 16 * lead, LANES), lambda step: (step, 0, 0)),
                pl.BlockSpec((1, 4 * PACK, part_rows), lambda step: (step, 0, 0)),
            ],
            out_shape=[
                jax.ShapeDtypeStruct((8, 16 * lead, LANES), F32),
                jax.ShapeDtypeStruct((8, 4 * PACK, part_rows), F32),
            ],
            compiler_params=params(LARGE),
            name="spread_terms",
        )(high, low, diag_inverse)

    def summed(flows):
        return lax.psum_scatter(flows, "col", scatter_dimension=0, tiled=False)

    spread, flows = chunk_terms(place)
    turned = pl.pallas_call(
        coupling_kernel,
        in_specs=[SMEM, VMEM],
        out_specs=VMEM,
        out_shape=jax.ShapeDtypeStruct((2, 2 * size, size), F32),
        compiler_params=params(),
        name="coupling_rows",
    )(info, couplings)
    own_inject = lax.dynamic_slice(inject, (team, member * SHARE), (1, SHARE))[0]
    own_inject = jnp.concatenate([own_inject, own_inject])
    marks = jnp.stack([own_inject == first + team, own_inject == first + 1 - team])
    marks = jnp.broadcast_to(marks.astype(F32)[:, :, None], (2, 2 * SHARE, size))
    own_lead = lax.dynamic_slice(leads, (team, 0, member * SHARE, 0), (1, 2, SHARE, size))
    own_lead = own_lead.reshape(2 * SHARE, size)
    base = summed(flows)
    owners = jnp.arange(slabs, dtype=jnp.int32)[:, None, None]
    counts = jnp.sum((inject_after[None] >> 1 == owners).astype(jnp.int32), axis=2)
    chunks = (jnp.max(counts) + PACK - 1) // PACK

    def more(chunk, extra):
        place = jnp.stack([first, chunk]).astype(jnp.int32)
        flows = chunk_terms(place)[1]
        return pl.pallas_call(
            expand_kernel,
            in_specs=[SMEM, VMEM, VMEM, VMEM],
            out_specs=VMEM,
            out_shape=jax.ShapeDtypeStruct((4 * modes, part_rows), F32),
            compiler_params=params(),
            name="expand_terms",
        )(place, inject, summed(flows), extra)

    extra = lax.fori_loop(1, chunks, more, jnp.zeros((4 * modes, part_rows), F32))
    received, turned, marks, own_lead, spread, extra = lax.optimization_barrier(
        (received, turned, marks, own_lead, spread, extra)
    )
    rows = exchange(spread)

    top, bottom, flow_a, first_map = pl.pallas_call(
        pair_map_kernel,
        in_specs=[SMEM] + [VMEM] * 10,
        out_specs=[VMEM] * 4,
        out_shape=[
            jax.ShapeDtypeStruct((2 * size + 2 * SHARE, size // 2), F32),
            jax.ShapeDtypeStruct((2 * size + 2 * SHARE, size // 2), F32),
            jax.ShapeDtypeStruct((2 * SHARE, size), F32),
            jax.ShapeDtypeStruct((2 * size, size), F32),
        ],
        scratch_shapes=[pltpu.VMEM((4, size, size), F32)],
        compiler_params=params(),
        name="pair_map",
    )(info, turned, marks, *received)

    def turn(value, step):
        return lax.ppermute(
            value, "slab", [(slab, slab // 4 * 4 + (slab + step) % 4) for slab in range(slabs)]
        )

    before_top, after_bottom = turn(top, 1), turn(bottom, -1)
    before_bottom, after_top = turn(bottom, 1), turn(top, -1)
    across_top, across_bottom = turn(before_top, 1), turn(after_bottom, -1)
    pieces = (after_top, after_bottom, across_top, across_bottom, before_top, before_bottom)
    row_maps = [
        jax.ShapeDtypeStruct((4, 2 * size, size), BF16),
        jax.ShapeDtypeStruct((4, 2 * size, size), BF16),
        jax.ShapeDtypeStruct((4, 2 * SHARE, size), F32),
    ]
    state_shape = jax.ShapeDtypeStruct((2 * SHARE, size), F32)
    *maps, flow = pl.pallas_call(
        gather_kernel,
        in_specs=[SMEM] + [VMEM] * 9,
        out_specs=[VMEM] * 4,
        out_shape=row_maps + [state_shape],
        compiler_params=params(),
        name="gather_maps",
    )(info, own_lead, top, bottom, *pieces)

    cols = lax.axis_size("col")
    pairs = []
    for slab in range(slabs):
        for col in range(cols):
            target = (slab + (4 if col // 2 % 2 == 0 else -4)) % slabs
            pairs.append((slab * cols + col, target * cols + col))

    def local(kernel, name, shapes, *args):
        single = not isinstance(shapes, list)
        return pl.pallas_call(
            kernel,
            in_specs=[SMEM] + [VMEM] * (len(args) - 1),
            out_specs=VMEM if single else [VMEM] * len(shapes),
            out_shape=shapes,
            compiler_params=params(),
            name=name,
        )(*args)

    def hop(value):
        return lax.ppermute(value, ("slab", "col"), pairs)

    full = jax.ShapeDtypeStruct((2 * size + 2 * SHARE, size), F32)
    half_map = jax.ShapeDtypeStruct((2 * size, size), BF16)
    flow = hop(flow)
    *row_map, half_row = local(
        row_map_kernel, "row_map", [half_map, half_map, state_shape, full], info, *maps
    )
    flow = local(row_kernel, "row_step", state_shape, info, own_lead, flow, *row_map)
    flow, half_row = lax.optimization_barrier((flow, half_row))
    flow = hop(flow)
    prefix, inner_map = local(
        prefix_kernel,
        "prefix_map",
        [full, full],
        info,
        *maps,
        half_row,
        first_map,
        turned,
        flow_a,
    )
    flow = local(row_kernel, "row_step", state_shape, info, own_lead, flow, *row_map)
    flow, prefix, inner_map = lax.optimization_barrier((flow, prefix, inner_map))
    flow = hop(flow)
    two_maps = [
        jax.ShapeDtypeStruct((2, 2 * size, size), BF16),
        jax.ShapeDtypeStruct((2, 2 * size, size), BF16),
        jax.ShapeDtypeStruct((2, 2 * SHARE, size), F32),
    ]
    entry = local(entry_map_kernel, "entry_map", two_maps, info, prefix, inner_map, turned)
    last = local(
        inflow_kernel,
        "inflow",
        jax.ShapeDtypeStruct((4 * SHARE, size), F32),
        info,
        own_lead,
        flow,
        *entry,
    )
    rows, base, last = lax.optimization_barrier((rows, base, last))
    last = [last] + [
        lax.ppermute(last, "col", [(col, (col + away) % 8) for col in range(0, 8, 2)])
        for away in range(1, 8)
    ]
    arranged = [
        jax.ShapeDtypeStruct((2, 2, 2, size, part_rows), BF16),
        jax.ShapeDtypeStruct((2, 2, 2, size, part_rows), BF16),
        jax.ShapeDtypeStruct((2, 2, 2, modes, part_rows), F32),
    ]
    arranged = local(
        arrange_kernel, "arrange_rows", arranged, place, inject, rows, base, extra
    )

    shape = jax.ShapeDtypeStruct((2, 2, modes, part_rows), F32)
    left, right = pl.pallas_call(
        state_kernel,
        in_specs=[SMEM] + [VMEM] * 11,
        out_specs=[VMEM, VMEM],
        out_shape=[shape, shape],
        scratch_shapes=[pltpu.VMEM((4, 4 * SHARE, size), F32)],
        compiler_params=params(),
        name="states",
    )(place, *arranged, *last)
    return jnp.transpose(left, (0, 1, 3, 2)), jnp.transpose(right, (0, 1, 3, 2))


def solution(mesh):
    placed = (
        P(("energy", "slab"), None, None, "col"),
        P(("energy", "slab"), None, None, None),
        P("energy", None, "col", None),
        P(),
        P("energy", None, None, None),
    )

    return jax.shard_map(
        on_device,
        mesh=mesh,
        in_specs=placed,
        out_specs=(
            P(("energy", "slab"), None, "col", None),
            P(("energy", "slab"), None, "col", None),
        ),
        check_vma=False,
    )
```

```python
import jax
import jax.numpy as jnp
from jax import lax
from jax.experimental import pallas as pl
from jax.experimental.pallas import tpu as pltpu
from jax.sharding import PartitionSpec as P

F32 = jnp.float32
BF16 = jnp.bfloat16
LIMIT = 24 * 1024 * 1024
LARGE = 56 * 1024 * 1024
PACK = 16
LANES = 128


def split(value):
    high = value.astype(BF16)
    return high, (value - high.astype(F32)).astype(BF16)


def mm(left, right, transposed=False):
    dims = (((1,), (1 if transposed else 0,)), ((), ()))
    return lax.dot_general(left, right, dims, preferred_element_type=F32)


def mm3(left, right, transposed=False):
    rows = left[0].shape[0]
    wide = mm(jnp.concatenate(left, axis=0), right[0], transposed)
    return wide[:rows] + (wide[rows:] + mm(left[0], right[1], transposed))


def combined(by_real, by_imag):
    half = by_real.shape[0] // 2
    return jnp.concatenate(
        [by_real[:half] - by_imag[half:], by_imag[:half] + by_real[half:]], axis=0
    )


def complex_rows(left, right):
    parts = split(left)
    return combined(mm3(parts, split(right[0])), mm3(parts, split(right[1])))


def times(left, right):
    size = right[0].shape[0] // 2
    by_real = mm3(left, (right[0][:size], right[1][:size]))
    by_imag = mm3(left, (right[0][size:], right[1][size:]))
    return combined(by_real, by_imag)


def interface_kernel(inject_ref, src_hbm, g_hbm, out_ref, g_ref, src_ref, sems, src_sem):
    first = lax.axis_index("slab") * 2
    modes, width = src_ref.shape[2], src_ref.shape[3]
    lanes = width // 2
    lead = width // 8
    fetch_src = pltpu.make_async_copy(src_hbm, src_ref, src_sem)
    fetch_src.start()
    fetches = {}
    for slab in range(2):
        for plane in range(2):
            for side in range(2):
                fetch = pltpu.make_async_copy(
                    g_hbm.at[slab, plane, :, side * lanes : (side + 1) * lanes],
                    g_ref.at[slab, plane, side],
                    sems.at[slab, plane, side],
                )
                fetch.start()
                fetches[slab, plane, side] = fetch
    rows = lax.broadcasted_iota(jnp.int32, (lead, width), 0)
    cols = lax.broadcasted_iota(jnp.int32, (lead, width), 1)
    targets = [
        jnp.broadcast_to(inject_ref[sweep : sweep + 1, :].astype(F32), (width, modes)).T
        for sweep in range(2)
    ]
    fetch_src.wait()
    count = g_ref.shape[3] // 8
    total = [0.0] * 4
    for slab in range(2):
        chosen = [target == (first + slab).astype(F32) for target in targets]
        left = []
        for sweep in range(2):
            unit = (cols == rows * 8 + sweep).astype(F32)
            source = [jnp.where(chosen[sweep], src_ref[sweep, part], 0.0) for part in range(2)]
            left.append(split(jnp.concatenate([unit] + source, axis=0)))
        for plane in range(2):
            for side in range(2):
                fetches[slab, plane, side].wait()
            for sweep in range(2):
                picked = jnp.concatenate(
                    [
                        g_ref[slab, plane, side, pl.ds(1 - sweep, count, stride=8), :]
                        for side in range(2)
                    ],
                    axis=1,
                )
                term = mm3(left[sweep], split(picked), True)
                order = slab if sweep == 0 else 1 - slab
                for member in range(4):
                    put(out_ref, sweep * 4 + member, (order * 2 + plane) * lead, term[:lead])
                real, imag = term[lead : lead + modes], term[lead + modes :]
                if plane == 0:
                    total[2 * sweep] += real
                    total[2 * sweep + 1] += imag
                else:
                    total[2 * sweep] -= imag
                    total[2 * sweep + 1] += real
    for dest in range(8):
        sweep, member = divmod(dest, 4)
        for part in range(2):
            piece = total[2 * sweep + part][member * 16 : (member + 1) * 16]
            put(out_ref, dest, 4 * lead + part * 16, piece)


def packed_columns(place_ref, inject_ref, sweep):
    modes = inject_ref.shape[1]
    target = inject_ref[sweep : sweep + 1, :]
    own = (target == place_ref[0]) | (target == place_ref[0] + 1)
    own = jnp.broadcast_to(own.astype(F32), (PACK, modes))
    earlier = lax.broadcasted_iota(jnp.int32, (modes, modes), 0)
    later = lax.broadcasted_iota(jnp.int32, (modes, modes), 1)
    rank = mm(own.astype(BF16), (earlier < later).astype(F32).astype(BF16))
    wanted = lax.broadcasted_iota(jnp.int32, (PACK, modes), 0) + PACK * place_ref[1]
    return jnp.where(rank == wanted.astype(F32), own, 0.0)


def unpacked_rows(place_ref, inject_ref, base_ref, sweep, part):
    back = packed_columns(place_ref, inject_ref, sweep).T.astype(BF16)
    start = (2 * sweep + part) * PACK
    high, low = split(base_ref[start : start + PACK, :])
    return mm(back, high) + mm(back, low)


def select_kernel(place_ref, inject_ref, src_ref, high_ref, low_ref):
    width = src_ref.shape[3]
    rows = lax.broadcasted_iota(jnp.int32, (width // 8, width), 0)
    cols = lax.broadcasted_iota(jnp.int32, (width // 8, width), 1)
    lead = width // 8
    for slab in range(2):
        for sweep in range(2):
            span = slice(sweep * lead, (sweep + 1) * lead)
            unit = (cols == rows * 8 + sweep).astype(F32)
            high_ref[slab, span, :] = unit.astype(BF16)
            low_ref[slab, span, :] = jnp.zeros_like(unit).astype(BF16)
            here = inject_ref[sweep : sweep + 1, :] == place_ref[0] + slab
            pick = jnp.where(here, packed_columns(place_ref, inject_ref, sweep), 0.0).astype(BF16)
            for part in range(2):
                start = 2 * lead + (2 * sweep + part) * PACK
                high, low = split(src_ref[sweep, part])
                high_ref[slab, start : start + PACK, :] = mm(pick, high).astype(BF16)
                low_ref[slab, start : start + PACK, :] = mm(pick, low).astype(BF16)


def spread_kernel(high_ref, low_ref, g_ref, out_ref, flow_ref):
    lead = g_ref.shape[3] // 8
    total = [0.0] * 4
    for slab in range(2):
        parts = (high_ref[slab], low_ref[slab])
        real = mm3(parts, split(g_ref[slab, 0]), True)
        imag = mm3(parts, split(g_ref[slab, 1]), True)
        for sweep in range(2):
            base = sweep * lead
            place = slab * 4 * lead + sweep * 2 * lead
            put(out_ref, 0, place, real[base : base + lead])
            put(out_ref, 0, place + lead, imag[base : base + lead])
            one = 2 * lead + 2 * sweep * PACK
            two, three = one + PACK, one + 2 * PACK
            total[2 * sweep] += real[one:two] - imag[two:three]
            total[2 * sweep + 1] += real[two:three] + imag[one:two]
    for item in range(4):
        flow_ref[0, item * PACK : (item + 1) * PACK, :] = total[item]


def expand_kernel(place_ref, inject_ref, base_ref, extra_ref, out_ref):
    modes = inject_ref.shape[1]
    for sweep in range(2):
        for part in range(2):
            span = slice((2 * sweep + part) * modes, (2 * sweep + part + 1) * modes)
            rows = unpacked_rows(place_ref, inject_ref, base_ref, sweep, part)
            out_ref[span, :] = extra_ref[span, :] + rows


def coupling_kernel(team_ref, c_ref, x_ref):
    left = team_ref[0] == 0
    size = c_ref.shape[3]
    for slab in range(2):
        x_ref[slab, :size] = jnp.where(left, c_ref[slab, 0].T, c_ref[slab, 0])
        x_ref[slab, size:] = jnp.where(left, c_ref[slab, 1].T, -c_ref[slab, 1])


def put(ref, dest, start, value):
    rows, lanes = ref.shape[1] // 2, ref.shape[2]
    ref[dest, start : start + value.shape[0], :] = value[:, :lanes]
    ref[dest, rows + start : rows + start + value.shape[0], :] = value[:, lanes:]


def taken(ref, source, start, count):
    rows = ref.shape[1] // 2
    halves = [ref[source, base + start : base + start + count, :] for base in (0, rows)]
    return jnp.concatenate(halves, axis=1)


def stacked(ref, start, count):
    return jnp.concatenate([taken(ref, block, start, count) for block in range(8)], axis=0)


def pair_map_kernel(
    team_ref, recv_ref, x_ref, mask_ref, top_ref, bottom_ref, qa_ref, first_ref
):
    left = team_ref[0] == 0
    size = x_ref.shape[2]
    lead = size // 8
    coupled = [(x_ref[slab, :size], x_ref[slab, size:]) for slab in range(2)]
    blocks = [
        (stacked(recv_ref, 2 * item * lead, lead), stacked(recv_ref, (2 * item + 1) * lead, lead))
        for item in range(2)
    ]
    flow = taken(recv_ref, 0, 4 * lead, 32)
    for block in range(1, 8):
        flow = flow + taken(recv_ref, block, 4 * lead, 32)
    flow_a = jnp.where(mask_ref[0] != 0, flow, 0.0)
    flow_b = jnp.where(mask_ref[1] != 0, flow, 0.0)
    qa_ref[...] = flow_a

    def pick(one, two):
        return (jnp.where(left, one[0], two[0]), jnp.where(left, one[1], two[1]))

    def product(one, two):
        return complex_rows(jnp.concatenate(one, axis=0), two)

    first = product(pick(coupled[0], blocks[0]), pick(blocks[0], coupled[1]))
    second = product(pick(coupled[1], blocks[1]), pick(blocks[1], coupled[0]))
    second = (second[:size], second[size:])
    first_ref[...] = first
    lanes = size // 2
    both = complex_rows(first, second)
    flow_a = jnp.where(left, flow_a, complex_rows(flow_a, coupled[1]))
    flow_b = jnp.where(left, flow_b, complex_rows(flow_b, coupled[0]))
    flow = complex_rows(flow_a, second) + flow_b
    for side, out_ref in enumerate((top_ref, bottom_ref)):
        span = slice(side * lanes, (side + 1) * lanes)
        out_ref[: 2 * size, :] = both[:, span]
        out_ref[2 * size :, :] = flow[:, span]


def item_of(info_ref, item):
    return jnp.where(info_ref[0] == 0, item, 3 - item)


def entry_state(info_ref, lead_ref, state_ref):
    return jnp.where(info_ref[1] == 0, lead_ref[...], state_ref[...])


def gather_kernel(info_ref, lead_ref, *refs):
    pieces, (high_ref, low_ref, flow_ref, out_ref) = refs[:8], refs[8:]
    lanes = pieces[0].shape[1]
    count = 4 * lanes
    for shift in range(4):
        place = lax.rem(info_ref[3] + shift, 4)
        for side in range(2):
            piece = pieces[2 * shift + side]
            span = slice(side * lanes, (side + 1) * lanes)
            high, low = split(piece[:count, :])
            high_ref[place, :, span] = high
            low_ref[place, :, span] = low
            flow_ref[place, :, span] = piece[count:, :]
    state = lead_ref[...]
    for item in range(4):
        index = item_of(info_ref, item)
        state = times(split(state), (high_ref[index], low_ref[index])) + flow_ref[index]
    out_ref[...] = state


def row_map_kernel(
    info_ref, high_ref, low_ref, flow_ref, row_high_ref, row_low_ref, row_flow_ref, half_ref
):
    maps, flows = [], []
    for item in range(4):
        index = item_of(info_ref, item)
        maps.append((high_ref[index], low_ref[index]))
        flows.append(flow_ref[index])
    size = high_ref.shape[2]
    early = times(maps[0], maps[1])
    early_flow = times(split(flows[0]), maps[1]) + flows[1]
    late = split(times(maps[2], maps[3]))
    late_flow = times(split(flows[2]), maps[3]) + flows[3]
    half_ref[: 2 * size, :] = early
    half_ref[2 * size :, :] = early_flow
    high, low = split(times(split(early), late))
    row_high_ref[...] = high
    row_low_ref[...] = low
    row_flow_ref[...] = times(split(early_flow), late) + late_flow


def row_kernel(info_ref, lead_ref, state_ref, high_ref, low_ref, flow_ref, out_ref):
    state = entry_state(info_ref, lead_ref, state_ref)
    out_ref[...] = times(split(state), (high_ref[...], low_ref[...])) + flow_ref[...]


def prefix_kernel(
    info_ref, high_ref, low_ref, flow_ref, half_ref, first_ref, x_ref, qa_ref, out_ref, inner_ref
):
    size = high_ref.shape[2]
    left = info_ref[0] == 0
    one, three = item_of(info_ref, 0), item_of(info_ref, 2)
    rows = lax.broadcasted_iota(jnp.int32, (2 * size + 32, size), 0)
    cols = lax.broadcasted_iota(jnp.int32, (2 * size + 32, size), 1)
    half = half_ref[...]
    third = (high_ref[three], low_ref[three])
    whole_row = times(split(half[: 2 * size]), third)
    whole_flow = times(split(half[2 * size :]), third) + flow_ref[three]
    none = (rows == cols).astype(F32)
    single = high_ref[one].astype(F32) + low_ref[one].astype(F32)
    single = jnp.concatenate([single, flow_ref[one]], axis=0)
    triple = jnp.concatenate([whole_row, whole_flow], axis=0)
    count = info_ref[2]
    low_half = jnp.where(count == 0, none, single)
    out_ref[...] = jnp.where(count < 2, low_half, jnp.where(count == 2, half, triple))
    second = split(x_ref[1])
    first = first_ref[...]
    inner_ref[: 2 * size, :] = jnp.where(left, times(split(first), second), first)
    inner_ref[2 * size :, :] = times(split(qa_ref[...]), second)


def entry_map_kernel(info_ref, prefix_ref, inner_ref, x_ref, high_ref, low_ref, flow_ref):
    size = x_ref.shape[2]
    left = info_ref[0] == 0
    prefix, flow = split(prefix_ref[: 2 * size, :]), split(prefix_ref[2 * size :, :])
    turn = split(x_ref[0])
    inner = split(inner_ref[: 2 * size, :])
    item_a = jnp.where(left, times(prefix, turn), prefix_ref[: 2 * size, :])
    flow_ref[0] = jnp.where(left, times(flow, turn), prefix_ref[2 * size :, :])
    item_b = times(prefix, inner)
    flow_ref[1] = times(flow, inner) + inner_ref[2 * size :, :]
    for item, value in enumerate((item_a, item_b)):
        high, low = split(value)
        high_ref[item] = high
        low_ref[item] = low


def inflow_kernel(info_ref, lead_ref, state_ref, high_ref, low_ref, flow_ref, out_ref):
    state = split(entry_state(info_ref, lead_ref, state_ref))
    for item in range(2):
        value = times(state, (high_ref[item], low_ref[item])) + flow_ref[item]
        for dest in range(8):
            put(out_ref, dest, 32 * item, value)


def arrange_kernel(
    place_ref, inject_ref, recv_ref, base_ref, extra_ref, high_ref, low_ref, out_ref
):
    lead = recv_ref.shape[1] // 16
    modes = inject_ref.shape[1]
    width = base_ref.shape[1]
    for slab in range(2):
        for kind in range(4):
            high, low = split(stacked(recv_ref, (slab * 4 + kind) * lead, lead))
            sweep, part = divmod(kind, 2)
            high_ref[slab, sweep, part] = high
            low_ref[slab, sweep, part] = low
    for sweep in range(2):
        target = jnp.broadcast_to(
            inject_ref[sweep : sweep + 1, :].astype(F32), (width, modes)
        ).T
        for part in range(2):
            start = (2 * sweep + part) * modes
            rows = unpacked_rows(place_ref, inject_ref, base_ref, sweep, part)
            rows = rows + extra_ref[start : start + modes, :]
            for slab in range(2):
                chosen = target == (place_ref[0] + slab).astype(F32)
                out_ref[sweep, slab, part] = jnp.where(chosen, rows, 0.0)


def state_kernel(last_ref, high_ref, low_ref, base_ref, left_ref, right_ref):
    modes = base_ref.shape[3]
    for sweep, out_ref in enumerate((left_ref, right_ref)):
        for slab in range(2):
            item = slab if sweep == 0 else 1 - slab
            pieces = []
            for part in range(2):
                start = item * 32 + part * 16
                for member in range(4):
                    pieces.append(taken(last_ref, sweep * 4 + member, start, 16))
            parts = split(jnp.concatenate(pieces, axis=0))
            by = [
                mm3(parts, (high_ref[slab, sweep, part], low_ref[slab, sweep, part]))
                for part in range(2)
            ]
            value = combined(by[0], by[1])
            for part in range(2):
                rows = value[part * modes : (part + 1) * modes]
                out_ref[slab, part] = base_ref[sweep, slab, part] + rows


def params(limit=LIMIT):
    return pltpu.CompilerParams(vmem_limit_bytes=limit)


def whole(shape):
    zeros = (0,) * len(shape)
    return pl.BlockSpec(shape, lambda *_: zeros)


SMEM = pl.BlockSpec(memory_space=pltpu.SMEM)
VMEM = pl.BlockSpec(memory_space=pltpu.VMEM)
ANY = pl.BlockSpec(memory_space=pl.ANY)


def exchange(value):
    return lax.all_to_all(value, "col", split_axis=0, concat_axis=0, tiled=True)


def on_device(diag_inverse, couplings, sources, inject, leads):
    orbitals = diag_inverse.shape[2]
    width = diag_inverse.shape[3]
    size = couplings.shape[2]
    modes = sources.shape[3]
    lead = size // 8
    part_rows = orbitals // 8
    slabs = lax.axis_size("slab")
    slab_index = lax.axis_index("slab")
    col_index = lax.axis_index("col")
    team = col_index // 4
    member = col_index % 4
    first = slab_index * 2
    place = jnp.stack([first, jnp.zeros_like(first)]).astype(jnp.int32)
    position = jnp.where(team == 0, slab_index, slabs - 1 - slab_index)
    info = jnp.stack([team, position // 4, position % 4, slab_index % 4]).astype(jnp.int32)
    block_rows = 4 * lead + 32
    sources = jnp.transpose(sources, (0, 1, 3, 2))
    leads = jnp.transpose(leads, (0, 1, 3, 2))

    sent = pl.pallas_call(
        interface_kernel,
        grid=(1,),
        in_specs=[whole(inject.shape), ANY, ANY],
        out_specs=whole((8, 2 * block_rows, LANES)),
        out_shape=jax.ShapeDtypeStruct((8, 2 * block_rows, LANES), F32),
        scratch_shapes=[
            pltpu.VMEM((2, 2, 2, orbitals, width // 2), F32),
            pltpu.VMEM(sources.shape, F32),
            pltpu.SemaphoreType.DMA((2, 2, 2)),
            pltpu.SemaphoreType.DMA,
        ],
        compiler_params=params(LARGE),
        name="interface_terms",
    )(inject, sources, diag_inverse)
    sent, inject_after = lax.optimization_barrier((sent, inject))
    received = exchange(sent)

    def chunk_terms(place):
        terms = jax.ShapeDtypeStruct((2, 2 * lead + 4 * PACK, width), BF16)
        high, low = pl.pallas_call(
            select_kernel,
            in_specs=[SMEM, VMEM, VMEM],
            out_specs=[VMEM, VMEM],
            out_shape=[terms, terms],
            compiler_params=params(),
            name="select_terms",
        )(place, inject_after, sources)
        return pl.pallas_call(
            spread_kernel,
            grid=(8,),
            in_specs=[
                whole(terms.shape),
                whole(terms.shape),
                pl.BlockSpec((2, 2, part_rows, width), lambda step: (0, 0, step, 0)),
            ],
            out_specs=[
                pl.BlockSpec((1, 16 * lead, LANES), lambda step: (step, 0, 0)),
                pl.BlockSpec((1, 4 * PACK, part_rows), lambda step: (step, 0, 0)),
            ],
            out_shape=[
                jax.ShapeDtypeStruct((8, 16 * lead, LANES), F32),
                jax.ShapeDtypeStruct((8, 4 * PACK, part_rows), F32),
            ],
            compiler_params=params(LARGE),
            name="spread_terms",
        )(high, low, diag_inverse)

    def summed(flows):
        return lax.psum_scatter(flows, "col", scatter_dimension=0, tiled=False)

    spread, flows = chunk_terms(place)
    turned = pl.pallas_call(
        coupling_kernel,
        in_specs=[SMEM, VMEM],
        out_specs=VMEM,
        out_shape=jax.ShapeDtypeStruct((2, 2 * size, size), F32),
        compiler_params=params(),
        name="coupling_rows",
    )(info, couplings)
    own_inject = lax.dynamic_slice(inject, (team, member * 16), (1, 16))[0]
    own_inject = jnp.concatenate([own_inject, own_inject])
    marks = jnp.stack([own_inject == first + team, own_inject == first + 1 - team])
    marks = jnp.broadcast_to(marks.astype(F32)[:, :, None], (2, 32, size))
    own_lead = lax.dynamic_slice(leads, (team, 0, member * 16, 0), (1, 2, 16, size))
    own_lead = own_lead.reshape(32, size)
    base = summed(flows)
    owners = jnp.arange(slabs, dtype=jnp.int32)[:, None, None]
    counts = jnp.sum((inject_after[None] >> 1 == owners).astype(jnp.int32), axis=2)
    chunks = (jnp.max(counts) + PACK - 1) // PACK

    def more(chunk, extra):
        place = jnp.stack([first, chunk]).astype(jnp.int32)
        flows = chunk_terms(place)[1]
        return pl.pallas_call(
            expand_kernel,
            in_specs=[SMEM, VMEM, VMEM, VMEM],
            out_specs=VMEM,
            out_shape=jax.ShapeDtypeStruct((4 * modes, part_rows), F32),
            compiler_params=params(),
            name="expand_terms",
        )(place, inject, summed(flows), extra)

    extra = lax.fori_loop(1, chunks, more, jnp.zeros((4 * modes, part_rows), F32))
    received, turned, marks, own_lead, spread, extra = lax.optimization_barrier(
        (received, turned, marks, own_lead, spread, extra)
    )
    rows = exchange(spread)

    top, bottom, flow_a, first_map = pl.pallas_call(
        pair_map_kernel,
        in_specs=[SMEM, VMEM, VMEM, VMEM],
        out_specs=[VMEM] * 4,
        out_shape=[
            jax.ShapeDtypeStruct((2 * size + 32, size // 2), F32),
            jax.ShapeDtypeStruct((2 * size + 32, size // 2), F32),
            jax.ShapeDtypeStruct((32, size), F32),
            jax.ShapeDtypeStruct((2 * size, size), F32),
        ],
        compiler_params=params(),
        name="pair_map",
    )(info, received, turned, marks)

    def turn(value, step):
        return lax.ppermute(
            value, "slab", [(slab, slab // 4 * 4 + (slab + step) % 4) for slab in range(slabs)]
        )

    before_top, after_bottom = turn(top, 1), turn(bottom, -1)
    before_bottom, after_top = turn(bottom, 1), turn(top, -1)
    across_top, across_bottom = turn(before_top, 1), turn(after_bottom, -1)
    pieces = (after_top, after_bottom, across_top, across_bottom, before_top, before_bottom)
    row_maps = [
        jax.ShapeDtypeStruct((4, 2 * size, size), BF16),
        jax.ShapeDtypeStruct((4, 2 * size, size), BF16),
        jax.ShapeDtypeStruct((4, 32, size), F32),
    ]
    state_shape = jax.ShapeDtypeStruct((32, size), F32)
    *maps, flow = pl.pallas_call(
        gather_kernel,
        in_specs=[SMEM] + [VMEM] * 9,
        out_specs=[VMEM] * 4,
        out_shape=row_maps + [state_shape],
        compiler_params=params(),
        name="gather_maps",
    )(info, own_lead, top, bottom, *pieces)

    cols = lax.axis_size("col")
    pairs = []
    for slab in range(slabs):
        for col in range(cols):
            target = (slab + (4 if col < 4 else -4)) % slabs
            pairs.append((slab * cols + col, target * cols + col))

    def local(kernel, name, shapes, *args):
        single = not isinstance(shapes, list)
        return pl.pallas_call(
            kernel,
            in_specs=[SMEM] + [VMEM] * (len(args) - 1),
            out_specs=VMEM if single else [VMEM] * len(shapes),
            out_shape=shapes,
            compiler_params=params(),
            name=name,
        )(*args)

    def hop(value):
        return lax.ppermute(value, ("slab", "col"), pairs)

    full = jax.ShapeDtypeStruct((2 * size + 32, size), F32)
    half_map = jax.ShapeDtypeStruct((2 * size, size), BF16)
    flow = hop(flow)
    *row_map, half_row = local(
        row_map_kernel, "row_map", [half_map, half_map, state_shape, full], info, *maps
    )
    flow = local(row_kernel, "row_step", state_shape, info, own_lead, flow, *row_map)
    flow, half_row = lax.optimization_barrier((flow, half_row))
    flow = hop(flow)
    prefix, inner_map = local(
        prefix_kernel,
        "prefix_map",
        [full, full],
        info,
        *maps,
        half_row,
        first_map,
        turned,
        flow_a,
    )
    flow = local(row_kernel, "row_step", state_shape, info, own_lead, flow, *row_map)
    flow, prefix, inner_map = lax.optimization_barrier((flow, prefix, inner_map))
    flow = hop(flow)
    two_maps = [
        jax.ShapeDtypeStruct((2, 2 * size, size), BF16),
        jax.ShapeDtypeStruct((2, 2 * size, size), BF16),
        jax.ShapeDtypeStruct((2, 32, size), F32),
    ]
    entry = local(entry_map_kernel, "entry_map", two_maps, info, prefix, inner_map, turned)
    last = local(
        inflow_kernel,
        "inflow",
        jax.ShapeDtypeStruct((8, 2 * 64, LANES), F32),
        info,
        own_lead,
        flow,
        *entry,
    )
    rows, base, last = lax.optimization_barrier((rows, base, last))
    last = exchange(last)
    arranged = [
        jax.ShapeDtypeStruct((2, 2, 2, size, part_rows), BF16),
        jax.ShapeDtypeStruct((2, 2, 2, size, part_rows), BF16),
        jax.ShapeDtypeStruct((2, 2, 2, modes, part_rows), F32),
    ]
    arranged = local(
        arrange_kernel, "arrange_rows", arranged, place, inject, rows, base, extra
    )

    shape = jax.ShapeDtypeStruct((2, 2, modes, part_rows), F32)
    left, right = pl.pallas_call(
        state_kernel,
        in_specs=[VMEM] * 4,
        out_specs=[VMEM, VMEM],
        out_shape=[shape, shape],
        compiler_params=params(),
        name="states",
    )(last, *arranged)
    return jnp.transpose(left, (0, 1, 3, 2)), jnp.transpose(right, (0, 1, 3, 2))


def solution(mesh):
    placed = (
        P(("energy", "slab"), None, None, "col"),
        P(("energy", "slab"), None, None, None),
        P("energy", None, "col", None),
        P(),
        P("energy", None, None, None),
    )

    return jax.shard_map(
        on_device,
        mesh=mesh,
        in_specs=placed,
        out_specs=(
            P(("energy", "slab"), None, "col", None),
            P(("energy", "slab"), None, "col", None),
        ),
        check_vma=False,
    )
```

```python
import jax
import jax.numpy as jnp
from jax import lax
from jax.experimental import pallas as pl
from jax.experimental.pallas import tpu as pltpu
from jax.sharding import PartitionSpec as P

F32 = jnp.float32
BF16 = jnp.bfloat16
LIMIT = 24 * 1024 * 1024
LARGE = 56 * 1024 * 1024
PACK = 16
LANES = 128


def split(value):
    high = value.astype(BF16)
    return high, (value - high.astype(F32)).astype(BF16)


def mm(left, right, transposed=False):
    dims = (((1,), (1 if transposed else 0,)), ((), ()))
    return lax.dot_general(left, right, dims, preferred_element_type=F32)


def mm3(left, right, transposed=False):
    rows = left[0].shape[0]
    wide = mm(jnp.concatenate(left, axis=0), right[0], transposed)
    return wide[:rows] + (wide[rows:] + mm(left[0], right[1], transposed))


def combined(by_real, by_imag):
    half = by_real.shape[0] // 2
    return jnp.concatenate(
        [by_real[:half] - by_imag[half:], by_imag[:half] + by_real[half:]], axis=0
    )


def complex_rows(left, right):
    parts = split(left)
    return combined(mm3(parts, split(right[0])), mm3(parts, split(right[1])))


def times(left, right):
    size = right[0].shape[0] // 2
    by_real = mm3(left, (right[0][:size], right[1][:size]))
    by_imag = mm3(left, (right[0][size:], right[1][size:]))
    return combined(by_real, by_imag)


def interface_kernel(inject_ref, src_hbm, g_hbm, out_ref, g_ref, src_ref, sems, src_sem):
    first = lax.axis_index("slab") * 2
    modes, width = src_ref.shape[2], src_ref.shape[3]
    lanes = width // 2
    lead = width // 8
    fetch_src = pltpu.make_async_copy(src_hbm, src_ref, src_sem)
    fetch_src.start()
    fetches = {}
    for slab in range(2):
        for plane in range(2):
            for side in range(2):
                fetch = pltpu.make_async_copy(
                    g_hbm.at[slab, plane, :, side * lanes : (side + 1) * lanes],
                    g_ref.at[slab, plane, side],
                    sems.at[slab, plane, side],
                )
                fetch.start()
                fetches[slab, plane, side] = fetch
    rows = lax.broadcasted_iota(jnp.int32, (width, lead), 0)
    cols = lax.broadcasted_iota(jnp.int32, (width, lead), 1)
    fetch_src.wait()
    columns = [
        jnp.concatenate([src_ref[sweep, part] for part in range(2)], axis=0).T
        for sweep in range(2)
    ]
    count = g_ref.shape[3] // 8
    sums = [[0.0, 0.0], [0.0, 0.0]]
    picks = [{}, {}]
    for slab in range(2):
        right = []
        for sweep in range(2):
            target = inject_ref[sweep : sweep + 1, :]
            chosen = jnp.concatenate([target, target], axis=1) == first + slab
            unit = (rows == cols * 8 + sweep).astype(F32)
            source = jnp.where(chosen, columns[sweep], 0.0)
            right.append(split(jnp.concatenate([source, unit], axis=1)))
        for plane in range(2):
            for side in range(2):
                fetches[slab, plane, side].wait()
            for sweep in range(2):
                picked = jnp.concatenate(
                    [
                        g_ref[slab, plane, side, pl.ds(1 - sweep, count, stride=8), :]
                        for side in range(2)
                    ],
                    axis=1,
                )
                term = mm3(split(picked), right[sweep])
                sums[sweep][plane] += term[:, : 2 * modes]
                picks[sweep][slab, plane] = term[:, 2 * modes :]
    for sweep in range(2):
        slabs = (0, 1) if sweep == 0 else (1, 0)
        block = [picks[sweep][slab, plane] for slab in slabs for plane in range(2)]
        block = jnp.concatenate(block, axis=1).T
        by_real, by_imag = sums[sweep][0].T, sums[sweep][1].T
        total = (by_real[:modes] - by_imag[modes:], by_real[modes:] + by_imag[:modes])
        for member in range(4):
            dest = sweep * 4 + member
            put(out_ref, dest, 0, block)
            for part in range(2):
                piece = total[part][member * 16 : (member + 1) * 16]
                put(out_ref, dest, 4 * lead + part * 16, piece)


def packed_columns(place_ref, inject_ref, sweep):
    modes = inject_ref.shape[1]
    target = inject_ref[sweep : sweep + 1, :]
    own = (target == place_ref[0]) | (target == place_ref[0] + 1)
    own = jnp.broadcast_to(own.astype(F32), (PACK, modes))
    earlier = lax.broadcasted_iota(jnp.int32, (modes, modes), 0)
    later = lax.broadcasted_iota(jnp.int32, (modes, modes), 1)
    rank = mm(own.astype(BF16), (earlier < later).astype(F32).astype(BF16))
    wanted = lax.broadcasted_iota(jnp.int32, (PACK, modes), 0) + PACK * place_ref[1]
    return jnp.where(rank == wanted.astype(F32), own, 0.0)


def unpacked_rows(place_ref, inject_ref, base_ref, sweep, part):
    back = packed_columns(place_ref, inject_ref, sweep).T.astype(BF16)
    start = (2 * sweep + part) * PACK
    high, low = split(base_ref[start : start + PACK, :])
    return mm(back, high) + mm(back, low)


def select_kernel(place_ref, inject_ref, src_ref, high_ref, low_ref):
    width = src_ref.shape[3]
    rows = lax.broadcasted_iota(jnp.int32, (width // 8, width), 0)
    cols = lax.broadcasted_iota(jnp.int32, (width // 8, width), 1)
    lead = width // 8
    for slab in range(2):
        for sweep in range(2):
            span = slice(sweep * lead, (sweep + 1) * lead)
            unit = (cols == rows * 8 + sweep).astype(F32)
            high_ref[slab, span, :] = unit.astype(BF16)
            low_ref[slab, span, :] = jnp.zeros_like(unit).astype(BF16)
            here = inject_ref[sweep : sweep + 1, :] == place_ref[0] + slab
            pick = jnp.where(here, packed_columns(place_ref, inject_ref, sweep), 0.0).astype(BF16)
            for part in range(2):
                start = 2 * lead + (2 * sweep + part) * PACK
                high, low = split(src_ref[sweep, part])
                high_ref[slab, start : start + PACK, :] = mm(pick, high).astype(BF16)
                low_ref[slab, start : start + PACK, :] = mm(pick, low).astype(BF16)


def spread_kernel(high_ref, low_ref, g_ref, out_ref, flow_ref):
    lead = g_ref.shape[3] // 8
    total = [0.0] * 4
    for slab in range(2):
        parts = (high_ref[slab], low_ref[slab])
        real = mm3(parts, split(g_ref[slab, 0]), True)
        imag = mm3(parts, split(g_ref[slab, 1]), True)
        for sweep in range(2):
            base = sweep * lead
            place = slab * 4 * lead + sweep * 2 * lead
            put(out_ref, 0, place, real[base : base + lead])
            put(out_ref, 0, place + lead, imag[base : base + lead])
            one = 2 * lead + 2 * sweep * PACK
            two, three = one + PACK, one + 2 * PACK
            total[2 * sweep] += real[one:two] - imag[two:three]
            total[2 * sweep + 1] += real[two:three] + imag[one:two]
    for item in range(4):
        flow_ref[0, item * PACK : (item + 1) * PACK, :] = total[item]


def expand_kernel(place_ref, inject_ref, base_ref, extra_ref, out_ref):
    modes = inject_ref.shape[1]
    for sweep in range(2):
        for part in range(2):
            span = slice((2 * sweep + part) * modes, (2 * sweep + part + 1) * modes)
            rows = unpacked_rows(place_ref, inject_ref, base_ref, sweep, part)
            out_ref[span, :] = extra_ref[span, :] + rows


def coupling_kernel(team_ref, c_ref, x_ref):
    left = team_ref[0] == 0
    size = c_ref.shape[3]
    for slab in range(2):
        x_ref[slab, :size] = jnp.where(left, c_ref[slab, 0].T, c_ref[slab, 0])
        x_ref[slab, size:] = jnp.where(left, c_ref[slab, 1].T, -c_ref[slab, 1])


def put(ref, dest, start, value):
    rows, lanes = ref.shape[1] // 2, ref.shape[2]
    ref[dest, start : start + value.shape[0], :] = value[:, :lanes]
    ref[dest, rows + start : rows + start + value.shape[0], :] = value[:, lanes:]


def taken(ref, source, start, count):
    rows = ref.shape[1] // 2
    halves = [ref[source, base + start : base + start + count, :] for base in (0, rows)]
    return jnp.concatenate(halves, axis=1)


def stacked(ref, start, count):
    return jnp.concatenate([taken(ref, block, start, count) for block in range(8)], axis=0)


def pair_map_kernel(
    team_ref, recv_ref, x_ref, mask_ref, top_ref, bottom_ref, qa_ref, first_ref
):
    left = team_ref[0] == 0
    size = x_ref.shape[2]
    lead = size // 8
    coupled = [(x_ref[slab, :size], x_ref[slab, size:]) for slab in range(2)]
    blocks = [
        (stacked(recv_ref, 2 * item * lead, lead), stacked(recv_ref, (2 * item + 1) * lead, lead))
        for item in range(2)
    ]
    flow = taken(recv_ref, 0, 4 * lead, 32)
    for block in range(1, 8):
        flow = flow + taken(recv_ref, block, 4 * lead, 32)
    flow_a = jnp.where(mask_ref[0] != 0, flow, 0.0)
    flow_b = jnp.where(mask_ref[1] != 0, flow, 0.0)
    qa_ref[...] = flow_a

    def pick(one, two):
        return (jnp.where(left, one[0], two[0]), jnp.where(left, one[1], two[1]))

    def product(one, two):
        return complex_rows(jnp.concatenate(one, axis=0), two)

    first = product(pick(coupled[0], blocks[0]), pick(blocks[0], coupled[1]))
    second = product(pick(coupled[1], blocks[1]), pick(blocks[1], coupled[0]))
    second = (second[:size], second[size:])
    first_ref[...] = first
    lanes = size // 2
    both = complex_rows(first, second)
    flow_a = jnp.where(left, flow_a, complex_rows(flow_a, coupled[1]))
    flow_b = jnp.where(left, flow_b, complex_rows(flow_b, coupled[0]))
    flow = complex_rows(flow_a, second) + flow_b
    for side, out_ref in enumerate((top_ref, bottom_ref)):
        span = slice(side * lanes, (side + 1) * lanes)
        out_ref[: 2 * size, :] = both[:, span]
        out_ref[2 * size :, :] = flow[:, span]


def item_of(info_ref, item):
    return jnp.where(info_ref[0] == 0, item, 3 - item)


def entry_state(info_ref, lead_ref, state_ref):
    return jnp.where(info_ref[1] == 0, lead_ref[...], state_ref[...])


def gather_kernel(info_ref, lead_ref, *refs):
    pieces, (high_ref, low_ref, flow_ref, out_ref) = refs[:8], refs[8:]
    lanes = pieces[0].shape[1]
    count = 4 * lanes
    for shift in range(4):
        place = lax.rem(info_ref[3] + shift, 4)
        for side in range(2):
            piece = pieces[2 * shift + side]
            span = slice(side * lanes, (side + 1) * lanes)
            high, low = split(piece[:count, :])
            high_ref[place, :, span] = high
            low_ref[place, :, span] = low
            flow_ref[place, :, span] = piece[count:, :]
    state = lead_ref[...]
    for item in range(4):
        index = item_of(info_ref, item)
        state = times(split(state), (high_ref[index], low_ref[index])) + flow_ref[index]
    out_ref[...] = state


def row_map_kernel(
    info_ref, high_ref, low_ref, flow_ref, row_high_ref, row_low_ref, row_flow_ref, half_ref
):
    maps, flows = [], []
    for item in range(4):
        index = item_of(info_ref, item)
        maps.append((high_ref[index], low_ref[index]))
        flows.append(flow_ref[index])
    size = high_ref.shape[2]
    early = times(maps[0], maps[1])
    early_flow = times(split(flows[0]), maps[1]) + flows[1]
    late = split(times(maps[2], maps[3]))
    late_flow = times(split(flows[2]), maps[3]) + flows[3]
    half_ref[: 2 * size, :] = early
    half_ref[2 * size :, :] = early_flow
    high, low = split(times(split(early), late))
    row_high_ref[...] = high
    row_low_ref[...] = low
    row_flow_ref[...] = times(split(early_flow), late) + late_flow


def row_kernel(info_ref, lead_ref, state_ref, high_ref, low_ref, flow_ref, out_ref):
    state = entry_state(info_ref, lead_ref, state_ref)
    out_ref[...] = times(split(state), (high_ref[...], low_ref[...])) + flow_ref[...]


def prefix_kernel(
    info_ref, high_ref, low_ref, flow_ref, half_ref, first_ref, x_ref, qa_ref, out_ref, inner_ref
):
    size = high_ref.shape[2]
    left = info_ref[0] == 0
    one, three = item_of(info_ref, 0), item_of(info_ref, 2)
    rows = lax.broadcasted_iota(jnp.int32, (2 * size + 32, size), 0)
    cols = lax.broadcasted_iota(jnp.int32, (2 * size + 32, size), 1)
    half = half_ref[...]
    third = (high_ref[three], low_ref[three])
    whole_row = times(split(half[: 2 * size]), third)
    whole_flow = times(split(half[2 * size :]), third) + flow_ref[three]
    none = (rows == cols).astype(F32)
    single = high_ref[one].astype(F32) + low_ref[one].astype(F32)
    single = jnp.concatenate([single, flow_ref[one]], axis=0)
    triple = jnp.concatenate([whole_row, whole_flow], axis=0)
    count = info_ref[2]
    low_half = jnp.where(count == 0, none, single)
    out_ref[...] = jnp.where(count < 2, low_half, jnp.where(count == 2, half, triple))
    second = split(x_ref[1])
    first = first_ref[...]
    inner_ref[: 2 * size, :] = jnp.where(left, times(split(first), second), first)
    inner_ref[2 * size :, :] = times(split(qa_ref[...]), second)


def entry_map_kernel(info_ref, prefix_ref, inner_ref, x_ref, high_ref, low_ref, flow_ref):
    size = x_ref.shape[2]
    left = info_ref[0] == 0
    prefix, flow = split(prefix_ref[: 2 * size, :]), split(prefix_ref[2 * size :, :])
    turn = split(x_ref[0])
    inner = split(inner_ref[: 2 * size, :])
    item_a = jnp.where(left, times(prefix, turn), prefix_ref[: 2 * size, :])
    flow_ref[0] = jnp.where(left, times(flow, turn), prefix_ref[2 * size :, :])
    item_b = times(prefix, inner)
    flow_ref[1] = times(flow, inner) + inner_ref[2 * size :, :]
    for item, value in enumerate((item_a, item_b)):
        high, low = split(value)
        high_ref[item] = high
        low_ref[item] = low


def inflow_kernel(info_ref, lead_ref, state_ref, high_ref, low_ref, flow_ref, out_ref):
    state = split(entry_state(info_ref, lead_ref, state_ref))
    for item in range(2):
        value = times(state, (high_ref[item], low_ref[item])) + flow_ref[item]
        for dest in range(8):
            put(out_ref, dest, 32 * item, value)


def arrange_kernel(
    place_ref, inject_ref, recv_ref, base_ref, extra_ref, high_ref, low_ref, out_ref
):
    lead = recv_ref.shape[1] // 16
    modes = inject_ref.shape[1]
    width = base_ref.shape[1]
    for slab in range(2):
        for kind in range(4):
            high, low = split(stacked(recv_ref, (slab * 4 + kind) * lead, lead))
            sweep, part = divmod(kind, 2)
            high_ref[slab, sweep, part] = high
            low_ref[slab, sweep, part] = low
    for sweep in range(2):
        target = jnp.broadcast_to(
            inject_ref[sweep : sweep + 1, :].astype(F32), (width, modes)
        ).T
        for part in range(2):
            start = (2 * sweep + part) * modes
            rows = unpacked_rows(place_ref, inject_ref, base_ref, sweep, part)
            rows = rows + extra_ref[start : start + modes, :]
            for slab in range(2):
                chosen = target == (place_ref[0] + slab).astype(F32)
                out_ref[sweep, slab, part] = jnp.where(chosen, rows, 0.0)


def state_kernel(last_ref, high_ref, low_ref, base_ref, left_ref, right_ref):
    modes = base_ref.shape[3]
    for sweep, out_ref in enumerate((left_ref, right_ref)):
        for slab in range(2):
            item = slab if sweep == 0 else 1 - slab
            pieces = []
            for part in range(2):
                start = item * 32 + part * 16
                for member in range(4):
                    pieces.append(taken(last_ref, sweep * 4 + member, start, 16))
            parts = split(jnp.concatenate(pieces, axis=0))
            by = [
                mm3(parts, (high_ref[slab, sweep, part], low_ref[slab, sweep, part]))
                for part in range(2)
            ]
            value = combined(by[0], by[1])
            for part in range(2):
                rows = value[part * modes : (part + 1) * modes]
                out_ref[slab, part] = base_ref[sweep, slab, part] + rows


def params(limit=LIMIT):
    return pltpu.CompilerParams(vmem_limit_bytes=limit)


def whole(shape):
    zeros = (0,) * len(shape)
    return pl.BlockSpec(shape, lambda *_: zeros)


SMEM = pl.BlockSpec(memory_space=pltpu.SMEM)
VMEM = pl.BlockSpec(memory_space=pltpu.VMEM)
ANY = pl.BlockSpec(memory_space=pl.ANY)


def exchange(value):
    return lax.all_to_all(value, "col", split_axis=0, concat_axis=0, tiled=True)


def on_device(diag_inverse, couplings, sources, inject, leads):
    orbitals = diag_inverse.shape[2]
    width = diag_inverse.shape[3]
    size = couplings.shape[2]
    modes = sources.shape[3]
    lead = size // 8
    part_rows = orbitals // 8
    slabs = lax.axis_size("slab")
    slab_index = lax.axis_index("slab")
    col_index = lax.axis_index("col")
    team = col_index // 4
    member = col_index % 4
    first = slab_index * 2
    place = jnp.stack([first, jnp.zeros_like(first)]).astype(jnp.int32)
    position = jnp.where(team == 0, slab_index, slabs - 1 - slab_index)
    info = jnp.stack([team, position // 4, position % 4, slab_index % 4]).astype(jnp.int32)
    block_rows = 4 * lead + 32
    sources = jnp.transpose(sources, (0, 1, 3, 2))
    leads = jnp.transpose(leads, (0, 1, 3, 2))

    sent = pl.pallas_call(
        interface_kernel,
        grid=(1,),
        in_specs=[whole(inject.shape), ANY, ANY],
        out_specs=whole((8, 2 * block_rows, LANES)),
        out_shape=jax.ShapeDtypeStruct((8, 2 * block_rows, LANES), F32),
        scratch_shapes=[
            pltpu.VMEM((2, 2, 2, orbitals, width // 2), F32),
            pltpu.VMEM(sources.shape, F32),
            pltpu.SemaphoreType.DMA((2, 2, 2)),
            pltpu.SemaphoreType.DMA,
        ],
        compiler_params=params(LARGE),
        name="interface_terms",
    )(inject, sources, diag_inverse)
    sent, inject_after = lax.optimization_barrier((sent, inject))
    received = exchange(sent)

    def chunk_terms(place):
        terms = jax.ShapeDtypeStruct((2, 2 * lead + 4 * PACK, width), BF16)
        high, low = pl.pallas_call(
            select_kernel,
            in_specs=[SMEM, VMEM, VMEM],
            out_specs=[VMEM, VMEM],
            out_shape=[terms, terms],
            compiler_params=params(),
            name="select_terms",
        )(place, inject_after, sources)
        return pl.pallas_call(
            spread_kernel,
            grid=(8,),
            in_specs=[
                whole(terms.shape),
                whole(terms.shape),
                pl.BlockSpec((2, 2, part_rows, width), lambda step: (0, 0, step, 0)),
            ],
            out_specs=[
                pl.BlockSpec((1, 16 * lead, LANES), lambda step: (step, 0, 0)),
                pl.BlockSpec((1, 4 * PACK, part_rows), lambda step: (step, 0, 0)),
            ],
            out_shape=[
                jax.ShapeDtypeStruct((8, 16 * lead, LANES), F32),
                jax.ShapeDtypeStruct((8, 4 * PACK, part_rows), F32),
            ],
            compiler_params=params(LARGE),
            name="spread_terms",
        )(high, low, diag_inverse)

    def summed(flows):
        return lax.psum_scatter(flows, "col", scatter_dimension=0, tiled=False)

    spread, flows = chunk_terms(place)
    turned = pl.pallas_call(
        coupling_kernel,
        in_specs=[SMEM, VMEM],
        out_specs=VMEM,
        out_shape=jax.ShapeDtypeStruct((2, 2 * size, size), F32),
        compiler_params=params(),
        name="coupling_rows",
    )(info, couplings)
    own_inject = lax.dynamic_slice(inject, (team, member * 16), (1, 16))[0]
    own_inject = jnp.concatenate([own_inject, own_inject])
    marks = jnp.stack([own_inject == first + team, own_inject == first + 1 - team])
    marks = jnp.broadcast_to(marks.astype(F32)[:, :, None], (2, 32, size))
    own_lead = lax.dynamic_slice(leads, (team, 0, member * 16, 0), (1, 2, 16, size))
    own_lead = own_lead.reshape(32, size)
    base = summed(flows)
    owners = jnp.arange(slabs, dtype=jnp.int32)[:, None, None]
    counts = jnp.sum((inject_after[None] >> 1 == owners).astype(jnp.int32), axis=2)
    chunks = (jnp.max(counts) + PACK - 1) // PACK

    def more(chunk, extra):
        place = jnp.stack([first, chunk]).astype(jnp.int32)
        flows = chunk_terms(place)[1]
        return pl.pallas_call(
            expand_kernel,
            in_specs=[SMEM, VMEM, VMEM, VMEM],
            out_specs=VMEM,
            out_shape=jax.ShapeDtypeStruct((4 * modes, part_rows), F32),
            compiler_params=params(),
            name="expand_terms",
        )(place, inject, summed(flows), extra)

    extra = lax.fori_loop(1, chunks, more, jnp.zeros((4 * modes, part_rows), F32))
    received, turned, marks, own_lead, spread, extra = lax.optimization_barrier(
        (received, turned, marks, own_lead, spread, extra)
    )
    rows = exchange(spread)

    top, bottom, flow_a, first_map = pl.pallas_call(
        pair_map_kernel,
        in_specs=[SMEM, VMEM, VMEM, VMEM],
        out_specs=[VMEM] * 4,
        out_shape=[
            jax.ShapeDtypeStruct((2 * size + 32, size // 2), F32),
            jax.ShapeDtypeStruct((2 * size + 32, size // 2), F32),
            jax.ShapeDtypeStruct((32, size), F32),
            jax.ShapeDtypeStruct((2 * size, size), F32),
        ],
        compiler_params=params(),
        name="pair_map",
    )(info, received, turned, marks)

    def turn(value, step):
        return lax.ppermute(
            value, "slab", [(slab, slab // 4 * 4 + (slab + step) % 4) for slab in range(slabs)]
        )

    before_top, after_bottom = turn(top, 1), turn(bottom, -1)
    before_bottom, after_top = turn(bottom, 1), turn(top, -1)
    across_top, across_bottom = turn(before_top, 1), turn(after_bottom, -1)
    pieces = (after_top, after_bottom, across_top, across_bottom, before_top, before_bottom)
    row_maps = [
        jax.ShapeDtypeStruct((4, 2 * size, size), BF16),
        jax.ShapeDtypeStruct((4, 2 * size, size), BF16),
        jax.ShapeDtypeStruct((4, 32, size), F32),
    ]
    state_shape = jax.ShapeDtypeStruct((32, size), F32)
    *maps, flow = pl.pallas_call(
        gather_kernel,
        in_specs=[SMEM] + [VMEM] * 9,
        out_specs=[VMEM] * 4,
        out_shape=row_maps + [state_shape],
        compiler_params=params(),
        name="gather_maps",
    )(info, own_lead, top, bottom, *pieces)

    cols = lax.axis_size("col")
    pairs = []
    for slab in range(slabs):
        for col in range(cols):
            target = (slab + (4 if col < 4 else -4)) % slabs
            pairs.append((slab * cols + col, target * cols + col))

    def local(kernel, name, shapes, *args):
        single = not isinstance(shapes, list)
        return pl.pallas_call(
            kernel,
            in_specs=[SMEM] + [VMEM] * (len(args) - 1),
            out_specs=VMEM if single else [VMEM] * len(shapes),
            out_shape=shapes,
            compiler_params=params(),
            name=name,
        )(*args)

    def hop(value):
        return lax.ppermute(value, ("slab", "col"), pairs)

    full = jax.ShapeDtypeStruct((2 * size + 32, size), F32)
    half_map = jax.ShapeDtypeStruct((2 * size, size), BF16)
    flow = hop(flow)
    *row_map, half_row = local(
        row_map_kernel, "row_map", [half_map, half_map, state_shape, full], info, *maps
    )
    flow = local(row_kernel, "row_step", state_shape, info, own_lead, flow, *row_map)
    flow, half_row = lax.optimization_barrier((flow, half_row))
    flow = hop(flow)
    prefix, inner_map = local(
        prefix_kernel,
        "prefix_map",
        [full, full],
        info,
        *maps,
        half_row,
        first_map,
        turned,
        flow_a,
    )
    flow = local(row_kernel, "row_step", state_shape, info, own_lead, flow, *row_map)
    flow, prefix, inner_map = lax.optimization_barrier((flow, prefix, inner_map))
    flow = hop(flow)
    two_maps = [
        jax.ShapeDtypeStruct((2, 2 * size, size), BF16),
        jax.ShapeDtypeStruct((2, 2 * size, size), BF16),
        jax.ShapeDtypeStruct((2, 32, size), F32),
    ]
    entry = local(entry_map_kernel, "entry_map", two_maps, info, prefix, inner_map, turned)
    last = local(
        inflow_kernel,
        "inflow",
        jax.ShapeDtypeStruct((8, 2 * 64, LANES), F32),
        info,
        own_lead,
        flow,
        *entry,
    )
    rows, base, last = lax.optimization_barrier((rows, base, last))
    last = exchange(last)
    arranged = [
        jax.ShapeDtypeStruct((2, 2, 2, size, part_rows), BF16),
        jax.ShapeDtypeStruct((2, 2, 2, size, part_rows), BF16),
        jax.ShapeDtypeStruct((2, 2, 2, modes, part_rows), F32),
    ]
    arranged = local(
        arrange_kernel, "arrange_rows", arranged, place, inject, rows, base, extra
    )

    shape = jax.ShapeDtypeStruct((2, 2, modes, part_rows), F32)
    left, right = pl.pallas_call(
        state_kernel,
        in_specs=[VMEM] * 4,
        out_specs=[VMEM, VMEM],
        out_shape=[shape, shape],
        compiler_params=params(),
        name="states",
    )(last, *arranged)
    return jnp.transpose(left, (0, 1, 3, 2)), jnp.transpose(right, (0, 1, 3, 2))


def solution(mesh):
    placed = (
        P(("energy", "slab"), None, None, "col"),
        P(("energy", "slab"), None, None, None),
        P("energy", None, "col", None),
        P(),
        P("energy", None, None, None),
    )

    return jax.shard_map(
        on_device,
        mesh=mesh,
        in_specs=placed,
        out_specs=(
            P(("energy", "slab"), None, "col", None),
            P(("energy", "slab"), None, "col", None),
        ),
        check_vma=False,
    )
```

```python
import jax
import jax.numpy as jnp
from jax import lax
from jax.experimental import pallas as pl
from jax.experimental.pallas import tpu as pltpu
from jax.sharding import PartitionSpec as P

F32 = jnp.float32
BF16 = jnp.bfloat16
LIMIT = 24 * 1024 * 1024
LARGE = 56 * 1024 * 1024
PACK = 16
LANES = 128


def split(value):
    high = value.astype(BF16)
    return high, (value - high.astype(F32)).astype(BF16)


def mm(left, right, transposed=False):
    dims = (((1,), (1 if transposed else 0,)), ((), ()))
    return lax.dot_general(left, right, dims, preferred_element_type=F32)


def mm3(left, right, transposed=False):
    rows = left[0].shape[0]
    wide = mm(jnp.concatenate(left, axis=0), right[0], transposed)
    return wide[:rows] + (wide[rows:] + mm(left[0], right[1], transposed))


def combined(by_real, by_imag):
    half = by_real.shape[0] // 2
    return jnp.concatenate(
        [by_real[:half] - by_imag[half:], by_imag[:half] + by_real[half:]], axis=0
    )


def complex_rows(left, right):
    parts = split(left)
    return combined(mm3(parts, split(right[0])), mm3(parts, split(right[1])))


def times(left, right):
    size = right[0].shape[0] // 2
    by_real = mm3(left, (right[0][:size], right[1][:size]))
    by_imag = mm3(left, (right[0][size:], right[1][size:]))
    return combined(by_real, by_imag)


def interface_kernel(inject_ref, src_hbm, g_hbm, out_ref, g_ref, src_ref, sems, src_sem):
    first = lax.axis_index("slab") * 2
    modes, width = src_ref.shape[2], src_ref.shape[3]
    lead = width // 8
    fetch_src = pltpu.make_async_copy(src_hbm, src_ref, src_sem)
    fetch_src.start()
    fetches = {}
    for slab in range(2):
        for plane in range(2):
            for sweep in range(2):
                fetch = pltpu.make_async_copy(
                    g_hbm.at[slab, plane, :, 1 - sweep, :],
                    g_ref.at[slab, plane, sweep],
                    sems.at[slab, plane, sweep],
                )
                fetch.start()
                fetches[slab, plane, sweep] = fetch
    rows = lax.broadcasted_iota(jnp.int32, (width, lead), 0)
    cols = lax.broadcasted_iota(jnp.int32, (width, lead), 1)
    fetch_src.wait()
    columns = [
        jnp.concatenate([src_ref[sweep, part] for part in range(2)], axis=0).T
        for sweep in range(2)
    ]
    sums = [[0.0, 0.0], [0.0, 0.0]]
    picks = [{}, {}]
    for slab in range(2):
        right = []
        for sweep in range(2):
            target = inject_ref[sweep : sweep + 1, :]
            chosen = jnp.concatenate([target, target], axis=1) == first + slab
            unit = (rows == cols * 8 + sweep).astype(F32)
            source = jnp.where(chosen, columns[sweep], 0.0)
            right.append(split(jnp.concatenate([source, unit], axis=1)))
        for plane in range(2):
            for sweep in range(2):
                fetches[slab, plane, sweep].wait()
                term = mm3(split(g_ref[slab, plane, sweep]), right[sweep])
                sums[sweep][plane] += term[:, : 2 * modes]
                picks[sweep][slab, plane] = term[:, 2 * modes :]
    for sweep in range(2):
        slabs = (0, 1) if sweep == 0 else (1, 0)
        block = [picks[sweep][slab, plane] for slab in slabs for plane in range(2)]
        block = jnp.concatenate(block, axis=1).T
        by_real, by_imag = sums[sweep][0].T, sums[sweep][1].T
        total = (by_real[:modes] - by_imag[modes:], by_real[modes:] + by_imag[:modes])
        for member in range(4):
            dest = sweep * 4 + member
            put(out_ref, dest, 0, block)
            for part in range(2):
                piece = total[part][member * 16 : (member + 1) * 16]
                put(out_ref, dest, 4 * lead + part * 16, piece)


def packed_columns(place_ref, inject_ref, sweep):
    modes = inject_ref.shape[1]
    target = inject_ref[sweep : sweep + 1, :]
    own = (target == place_ref[0]) | (target == place_ref[0] + 1)
    own = jnp.broadcast_to(own.astype(F32), (PACK, modes))
    earlier = lax.broadcasted_iota(jnp.int32, (modes, modes), 0)
    later = lax.broadcasted_iota(jnp.int32, (modes, modes), 1)
    rank = mm(own.astype(BF16), (earlier < later).astype(F32).astype(BF16))
    wanted = lax.broadcasted_iota(jnp.int32, (PACK, modes), 0) + PACK * place_ref[1]
    return jnp.where(rank == wanted.astype(F32), own, 0.0)


def unpacked_rows(place_ref, inject_ref, base_ref, sweep, part):
    back = packed_columns(place_ref, inject_ref, sweep).T.astype(BF16)
    start = (2 * sweep + part) * PACK
    high, low = split(base_ref[start : start + PACK, :])
    return mm(back, high) + mm(back, low)


def select_kernel(place_ref, inject_ref, src_ref, high_ref, low_ref):
    width = src_ref.shape[3]
    rows = lax.broadcasted_iota(jnp.int32, (width // 8, width), 0)
    cols = lax.broadcasted_iota(jnp.int32, (width // 8, width), 1)
    lead = width // 8
    for slab in range(2):
        for sweep in range(2):
            span = slice(sweep * lead, (sweep + 1) * lead)
            unit = (cols == rows * 8 + sweep).astype(F32)
            high_ref[slab, span, :] = unit.astype(BF16)
            low_ref[slab, span, :] = jnp.zeros_like(unit).astype(BF16)
            here = inject_ref[sweep : sweep + 1, :] == place_ref[0] + slab
            pick = jnp.where(here, packed_columns(place_ref, inject_ref, sweep), 0.0).astype(BF16)
            for part in range(2):
                start = 2 * lead + (2 * sweep + part) * PACK
                high, low = split(src_ref[sweep, part])
                high_ref[slab, start : start + PACK, :] = mm(pick, high).astype(BF16)
                low_ref[slab, start : start + PACK, :] = mm(pick, low).astype(BF16)


def spread_kernel(high_ref, low_ref, g_ref, out_ref, flow_ref):
    lead = g_ref.shape[3] // 8
    total = [0.0] * 4
    for slab in range(2):
        parts = (high_ref[slab], low_ref[slab])
        real = mm3(parts, split(g_ref[slab, 0]), True)
        imag = mm3(parts, split(g_ref[slab, 1]), True)
        for sweep in range(2):
            base = sweep * lead
            place = slab * 4 * lead + sweep * 2 * lead
            put(out_ref, 0, place, real[base : base + lead])
            put(out_ref, 0, place + lead, imag[base : base + lead])
            one = 2 * lead + 2 * sweep * PACK
            two, three = one + PACK, one + 2 * PACK
            total[2 * sweep] += real[one:two] - imag[two:three]
            total[2 * sweep + 1] += real[two:three] + imag[one:two]
    for item in range(4):
        flow_ref[0, item * PACK : (item + 1) * PACK, :] = total[item]


def expand_kernel(place_ref, inject_ref, base_ref, extra_ref, out_ref):
    modes = inject_ref.shape[1]
    for sweep in range(2):
        for part in range(2):
            span = slice((2 * sweep + part) * modes, (2 * sweep + part + 1) * modes)
            rows = unpacked_rows(place_ref, inject_ref, base_ref, sweep, part)
            out_ref[span, :] = extra_ref[span, :] + rows


def coupling_kernel(team_ref, c_ref, x_ref):
    left = team_ref[0] == 0
    size = c_ref.shape[3]
    for slab in range(2):
        x_ref[slab, :size] = jnp.where(left, c_ref[slab, 0].T, c_ref[slab, 0])
        x_ref[slab, size:] = jnp.where(left, c_ref[slab, 1].T, -c_ref[slab, 1])


def put(ref, dest, start, value):
    rows, lanes = ref.shape[1] // 2, ref.shape[2]
    ref[dest, start : start + value.shape[0], :] = value[:, :lanes]
    ref[dest, rows + start : rows + start + value.shape[0], :] = value[:, lanes:]


def taken(ref, source, start, count):
    rows = ref.shape[1] // 2
    halves = [ref[source, base + start : base + start + count, :] for base in (0, rows)]
    return jnp.concatenate(halves, axis=1)


def stacked(ref, start, count):
    return jnp.concatenate([taken(ref, block, start, count) for block in range(8)], axis=0)


def pair_map_kernel(
    team_ref, recv_ref, x_ref, mask_ref, top_ref, bottom_ref, qa_ref, first_ref
):
    left = team_ref[0] == 0
    size = x_ref.shape[2]
    lead = size // 8
    coupled = [(x_ref[slab, :size], x_ref[slab, size:]) for slab in range(2)]
    blocks = [
        (stacked(recv_ref, 2 * item * lead, lead), stacked(recv_ref, (2 * item + 1) * lead, lead))
        for item in range(2)
    ]
    flow = taken(recv_ref, 0, 4 * lead, 32)
    for block in range(1, 8):
        flow = flow + taken(recv_ref, block, 4 * lead, 32)
    flow_a = jnp.where(mask_ref[0] != 0, flow, 0.0)
    flow_b = jnp.where(mask_ref[1] != 0, flow, 0.0)
    qa_ref[...] = flow_a

    def pick(one, two):
        return (jnp.where(left, one[0], two[0]), jnp.where(left, one[1], two[1]))

    def product(one, two):
        return complex_rows(jnp.concatenate(one, axis=0), two)

    first = product(pick(coupled[0], blocks[0]), pick(blocks[0], coupled[1]))
    second = product(pick(coupled[1], blocks[1]), pick(blocks[1], coupled[0]))
    second = (second[:size], second[size:])
    first_ref[...] = first
    lanes = size // 2
    both = complex_rows(first, second)
    flow_a = jnp.where(left, flow_a, complex_rows(flow_a, coupled[1]))
    flow_b = jnp.where(left, flow_b, complex_rows(flow_b, coupled[0]))
    flow = complex_rows(flow_a, second) + flow_b
    for side, out_ref in enumerate((top_ref, bottom_ref)):
        span = slice(side * lanes, (side + 1) * lanes)
        out_ref[: 2 * size, :] = both[:, span]
        out_ref[2 * size :, :] = flow[:, span]


def item_of(info_ref, item):
    return jnp.where(info_ref[0] == 0, item, 3 - item)


def entry_state(info_ref, lead_ref, state_ref):
    return jnp.where(info_ref[1] == 0, lead_ref[...], state_ref[...])


def gather_kernel(info_ref, lead_ref, *refs):
    pieces, (high_ref, low_ref, flow_ref, out_ref) = refs[:8], refs[8:]
    lanes = pieces[0].shape[1]
    count = 4 * lanes
    for shift in range(4):
        place = lax.rem(info_ref[3] + shift, 4)
        for side in range(2):
            piece = pieces[2 * shift + side]
            span = slice(side * lanes, (side + 1) * lanes)
            high, low = split(piece[:count, :])
            high_ref[place, :, span] = high
            low_ref[place, :, span] = low
            flow_ref[place, :, span] = piece[count:, :]
    state = lead_ref[...]
    for item in range(4):
        index = item_of(info_ref, item)
        state = times(split(state), (high_ref[index], low_ref[index])) + flow_ref[index]
    out_ref[...] = state


def row_map_kernel(
    info_ref, high_ref, low_ref, flow_ref, row_high_ref, row_low_ref, row_flow_ref, half_ref
):
    maps, flows = [], []
    for item in range(4):
        index = item_of(info_ref, item)
        maps.append((high_ref[index], low_ref[index]))
        flows.append(flow_ref[index])
    size = high_ref.shape[2]
    early = times(maps[0], maps[1])
    early_flow = times(split(flows[0]), maps[1]) + flows[1]
    late = split(times(maps[2], maps[3]))
    late_flow = times(split(flows[2]), maps[3]) + flows[3]
    half_ref[: 2 * size, :] = early
    half_ref[2 * size :, :] = early_flow
    high, low = split(times(split(early), late))
    row_high_ref[...] = high
    row_low_ref[...] = low
    row_flow_ref[...] = times(split(early_flow), late) + late_flow


def row_kernel(info_ref, lead_ref, state_ref, high_ref, low_ref, flow_ref, out_ref):
    state = entry_state(info_ref, lead_ref, state_ref)
    out_ref[...] = times(split(state), (high_ref[...], low_ref[...])) + flow_ref[...]


def prefix_kernel(
    info_ref, high_ref, low_ref, flow_ref, half_ref, first_ref, x_ref, qa_ref, out_ref, inner_ref
):
    size = high_ref.shape[2]
    left = info_ref[0] == 0
    one, three = item_of(info_ref, 0), item_of(info_ref, 2)
    rows = lax.broadcasted_iota(jnp.int32, (2 * size + 32, size), 0)
    cols = lax.broadcasted_iota(jnp.int32, (2 * size + 32, size), 1)
    half = half_ref[...]
    third = (high_ref[three], low_ref[three])
    whole_row = times(split(half[: 2 * size]), third)
    whole_flow = times(split(half[2 * size :]), third) + flow_ref[three]
    none = (rows == cols).astype(F32)
    single = high_ref[one].astype(F32) + low_ref[one].astype(F32)
    single = jnp.concatenate([single, flow_ref[one]], axis=0)
    triple = jnp.concatenate([whole_row, whole_flow], axis=0)
    count = info_ref[2]
    low_half = jnp.where(count == 0, none, single)
    out_ref[...] = jnp.where(count < 2, low_half, jnp.where(count == 2, half, triple))
    second = split(x_ref[1])
    first = first_ref[...]
    inner_ref[: 2 * size, :] = jnp.where(left, times(split(first), second), first)
    inner_ref[2 * size :, :] = times(split(qa_ref[...]), second)


def entry_map_kernel(info_ref, prefix_ref, inner_ref, x_ref, high_ref, low_ref, flow_ref):
    size = x_ref.shape[2]
    left = info_ref[0] == 0
    prefix, flow = split(prefix_ref[: 2 * size, :]), split(prefix_ref[2 * size :, :])
    turn = split(x_ref[0])
    inner = split(inner_ref[: 2 * size, :])
    item_a = jnp.where(left, times(prefix, turn), prefix_ref[: 2 * size, :])
    flow_ref[0] = jnp.where(left, times(flow, turn), prefix_ref[2 * size :, :])
    item_b = times(prefix, inner)
    flow_ref[1] = times(flow, inner) + inner_ref[2 * size :, :]
    for item, value in enumerate((item_a, item_b)):
        high, low = split(value)
        high_ref[item] = high
        low_ref[item] = low


def inflow_kernel(info_ref, lead_ref, state_ref, high_ref, low_ref, flow_ref, out_ref):
    state = split(entry_state(info_ref, lead_ref, state_ref))
    for item in range(2):
        value = times(state, (high_ref[item], low_ref[item])) + flow_ref[item]
        for dest in range(8):
            put(out_ref, dest, 32 * item, value)


def arrange_kernel(
    place_ref, inject_ref, recv_ref, base_ref, extra_ref, high_ref, low_ref, out_ref
):
    lead = recv_ref.shape[1] // 16
    modes = inject_ref.shape[1]
    width = base_ref.shape[1]
    for slab in range(2):
        for kind in range(4):
            high, low = split(stacked(recv_ref, (slab * 4 + kind) * lead, lead))
            sweep, part = divmod(kind, 2)
            high_ref[slab, sweep, part] = high
            low_ref[slab, sweep, part] = low
    for sweep in range(2):
        target = jnp.broadcast_to(
            inject_ref[sweep : sweep + 1, :].astype(F32), (width, modes)
        ).T
        for part in range(2):
            start = (2 * sweep + part) * modes
            rows = unpacked_rows(place_ref, inject_ref, base_ref, sweep, part)
            rows = rows + extra_ref[start : start + modes, :]
            for slab in range(2):
                chosen = target == (place_ref[0] + slab).astype(F32)
                out_ref[sweep, slab, part] = jnp.where(chosen, rows, 0.0)


def state_kernel(last_ref, high_ref, low_ref, base_ref, left_ref, right_ref):
    modes = base_ref.shape[3]
    for sweep, out_ref in enumerate((left_ref, right_ref)):
        for slab in range(2):
            item = slab if sweep == 0 else 1 - slab
            pieces = []
            for part in range(2):
                start = item * 32 + part * 16
                for member in range(4):
                    pieces.append(taken(last_ref, sweep * 4 + member, start, 16))
            parts = split(jnp.concatenate(pieces, axis=0))
            by = [
                mm3(parts, (high_ref[slab, sweep, part], low_ref[slab, sweep, part]))
                for part in range(2)
            ]
            value = combined(by[0], by[1])
            for part in range(2):
                rows = value[part * modes : (part + 1) * modes]
                out_ref[slab, part] = base_ref[sweep, slab, part] + rows


def params(limit=LIMIT):
    return pltpu.CompilerParams(vmem_limit_bytes=limit)


def whole(shape):
    zeros = (0,) * len(shape)
    return pl.BlockSpec(shape, lambda *_: zeros)


SMEM = pl.BlockSpec(memory_space=pltpu.SMEM)
VMEM = pl.BlockSpec(memory_space=pltpu.VMEM)
ANY = pl.BlockSpec(memory_space=pl.ANY)


def exchange(value):
    return lax.all_to_all(value, "col", split_axis=0, concat_axis=0, tiled=True)


def on_device(diag_inverse, couplings, sources, inject, leads):
    orbitals = diag_inverse.shape[2]
    width = diag_inverse.shape[3]
    size = couplings.shape[2]
    modes = sources.shape[3]
    lead = size // 8
    part_rows = orbitals // 8
    slabs = lax.axis_size("slab")
    slab_index = lax.axis_index("slab")
    col_index = lax.axis_index("col")
    team = col_index // 4
    member = col_index % 4
    first = slab_index * 2
    place = jnp.stack([first, jnp.zeros_like(first)]).astype(jnp.int32)
    position = jnp.where(team == 0, slab_index, slabs - 1 - slab_index)
    info = jnp.stack([team, position // 4, position % 4, slab_index % 4]).astype(jnp.int32)
    block_rows = 4 * lead + 32
    sources = jnp.transpose(sources, (0, 1, 3, 2))
    leads = jnp.transpose(leads, (0, 1, 3, 2))

    sent = pl.pallas_call(
        interface_kernel,
        grid=(1,),
        in_specs=[whole(inject.shape), ANY, ANY],
        out_specs=whole((8, 2 * block_rows, LANES)),
        out_shape=jax.ShapeDtypeStruct((8, 2 * block_rows, LANES), F32),
        scratch_shapes=[
            pltpu.VMEM((2, 2, 2, size, width), F32),
            pltpu.VMEM(sources.shape, F32),
            pltpu.SemaphoreType.DMA((2, 2, 2)),
            pltpu.SemaphoreType.DMA,
        ],
        compiler_params=params(LARGE),
        name="interface_terms",
    )(inject, sources, diag_inverse.reshape(2, 2, size, orbitals // size, width))
    sent, inject_after = lax.optimization_barrier((sent, inject))
    received = exchange(sent)

    def chunk_terms(place):
        terms = jax.ShapeDtypeStruct((2, 2 * lead + 4 * PACK, width), BF16)
        high, low = pl.pallas_call(
            select_kernel,
            in_specs=[SMEM, VMEM, VMEM],
            out_specs=[VMEM, VMEM],
            out_shape=[terms, terms],
            compiler_params=params(),
            name="select_terms",
        )(place, inject_after, sources)
        return pl.pallas_call(
            spread_kernel,
            grid=(8,),
            in_specs=[
                whole(terms.shape),
                whole(terms.shape),
                pl.BlockSpec((2, 2, part_rows, width), lambda step: (0, 0, step, 0)),
            ],
            out_specs=[
                pl.BlockSpec((1, 16 * lead, LANES), lambda step: (step, 0, 0)),
                pl.BlockSpec((1, 4 * PACK, part_rows), lambda step: (step, 0, 0)),
            ],
            out_shape=[
                jax.ShapeDtypeStruct((8, 16 * lead, LANES), F32),
                jax.ShapeDtypeStruct((8, 4 * PACK, part_rows), F32),
            ],
            compiler_params=params(LARGE),
            name="spread_terms",
        )(high, low, diag_inverse)

    def summed(flows):
        return lax.psum_scatter(flows, "col", scatter_dimension=0, tiled=False)

    spread, flows = chunk_terms(place)
    turned = pl.pallas_call(
        coupling_kernel,
        in_specs=[SMEM, VMEM],
        out_specs=VMEM,
        out_shape=jax.ShapeDtypeStruct((2, 2 * size, size), F32),
        compiler_params=params(),
        name="coupling_rows",
    )(info, couplings)
    own_inject = lax.dynamic_slice(inject, (team, member * 16), (1, 16))[0]
    own_inject = jnp.concatenate([own_inject, own_inject])
    marks = jnp.stack([own_inject == first + team, own_inject == first + 1 - team])
    marks = jnp.broadcast_to(marks.astype(F32)[:, :, None], (2, 32, size))
    own_lead = lax.dynamic_slice(leads, (team, 0, member * 16, 0), (1, 2, 16, size))
    own_lead = own_lead.reshape(32, size)
    base = summed(flows)
    owners = jnp.arange(slabs, dtype=jnp.int32)[:, None, None]
    counts = jnp.sum((inject_after[None] >> 1 == owners).astype(jnp.int32), axis=2)
    chunks = (jnp.max(counts) + PACK - 1) // PACK

    def more(chunk, extra):
        place = jnp.stack([first, chunk]).astype(jnp.int32)
        flows = chunk_terms(place)[1]
        return pl.pallas_call(
            expand_kernel,
            in_specs=[SMEM, VMEM, VMEM, VMEM],
            out_specs=VMEM,
            out_shape=jax.ShapeDtypeStruct((4 * modes, part_rows), F32),
            compiler_params=params(),
            name="expand_terms",
        )(place, inject, summed(flows), extra)

    extra = lax.fori_loop(1, chunks, more, jnp.zeros((4 * modes, part_rows), F32))
    received, turned, marks, own_lead, spread, extra = lax.optimization_barrier(
        (received, turned, marks, own_lead, spread, extra)
    )
    rows = exchange(spread)

    top, bottom, flow_a, first_map = pl.pallas_call(
        pair_map_kernel,
        in_specs=[SMEM, VMEM, VMEM, VMEM],
        out_specs=[VMEM] * 4,
        out_shape=[
            jax.ShapeDtypeStruct((2 * size + 32, size // 2), F32),
            jax.ShapeDtypeStruct((2 * size + 32, size // 2), F32),
            jax.ShapeDtypeStruct((32, size), F32),
            jax.ShapeDtypeStruct((2 * size, size), F32),
        ],
        compiler_params=params(),
        name="pair_map",
    )(info, received, turned, marks)

    def turn(value, step):
        return lax.ppermute(
            value, "slab", [(slab, slab // 4 * 4 + (slab + step) % 4) for slab in range(slabs)]
        )

    before_top, after_bottom = turn(top, 1), turn(bottom, -1)
    before_bottom, after_top = turn(bottom, 1), turn(top, -1)
    across_top, across_bottom = turn(before_top, 1), turn(after_bottom, -1)
    pieces = (after_top, after_bottom, across_top, across_bottom, before_top, before_bottom)
    row_maps = [
        jax.ShapeDtypeStruct((4, 2 * size, size), BF16),
        jax.ShapeDtypeStruct((4, 2 * size, size), BF16),
        jax.ShapeDtypeStruct((4, 32, size), F32),
    ]
    state_shape = jax.ShapeDtypeStruct((32, size), F32)
    *maps, flow = pl.pallas_call(
        gather_kernel,
        in_specs=[SMEM] + [VMEM] * 9,
        out_specs=[VMEM] * 4,
        out_shape=row_maps + [state_shape],
        compiler_params=params(),
        name="gather_maps",
    )(info, own_lead, top, bottom, *pieces)

    cols = lax.axis_size("col")
    pairs = []
    for slab in range(slabs):
        for col in range(cols):
            target = (slab + (4 if col < 4 else -4)) % slabs
            pairs.append((slab * cols + col, target * cols + col))

    def local(kernel, name, shapes, *args):
        single = not isinstance(shapes, list)
        return pl.pallas_call(
            kernel,
            in_specs=[SMEM] + [VMEM] * (len(args) - 1),
            out_specs=VMEM if single else [VMEM] * len(shapes),
            out_shape=shapes,
            compiler_params=params(),
            name=name,
        )(*args)

    def hop(value):
        return lax.ppermute(value, ("slab", "col"), pairs)

    full = jax.ShapeDtypeStruct((2 * size + 32, size), F32)
    half_map = jax.ShapeDtypeStruct((2 * size, size), BF16)
    flow = hop(flow)
    *row_map, half_row = local(
        row_map_kernel, "row_map", [half_map, half_map, state_shape, full], info, *maps
    )
    flow = local(row_kernel, "row_step", state_shape, info, own_lead, flow, *row_map)
    flow, half_row = lax.optimization_barrier((flow, half_row))
    flow = hop(flow)
    prefix, inner_map = local(
        prefix_kernel,
        "prefix_map",
        [full, full],
        info,
        *maps,
        half_row,
        first_map,
        turned,
        flow_a,
    )
    flow = local(row_kernel, "row_step", state_shape, info, own_lead, flow, *row_map)
    flow, prefix, inner_map = lax.optimization_barrier((flow, prefix, inner_map))
    flow = hop(flow)
    two_maps = [
        jax.ShapeDtypeStruct((2, 2 * size, size), BF16),
        jax.ShapeDtypeStruct((2, 2 * size, size), BF16),
        jax.ShapeDtypeStruct((2, 32, size), F32),
    ]
    entry = local(entry_map_kernel, "entry_map", two_maps, info, prefix, inner_map, turned)
    last = local(
        inflow_kernel,
        "inflow",
        jax.ShapeDtypeStruct((8, 2 * 64, LANES), F32),
        info,
        own_lead,
        flow,
        *entry,
    )
    rows, base, last = lax.optimization_barrier((rows, base, last))
    last = exchange(last)
    arranged = [
        jax.ShapeDtypeStruct((2, 2, 2, size, part_rows), BF16),
        jax.ShapeDtypeStruct((2, 2, 2, size, part_rows), BF16),
        jax.ShapeDtypeStruct((2, 2, 2, modes, part_rows), F32),
    ]
    arranged = local(
        arrange_kernel, "arrange_rows", arranged, place, inject, rows, base, extra
    )

    shape = jax.ShapeDtypeStruct((2, 2, modes, part_rows), F32)
    left, right = pl.pallas_call(
        state_kernel,
        in_specs=[VMEM] * 4,
        out_specs=[VMEM, VMEM],
        out_shape=[shape, shape],
        compiler_params=params(),
        name="states",
    )(last, *arranged)
    return jnp.transpose(left, (0, 1, 3, 2)), jnp.transpose(right, (0, 1, 3, 2))


def solution(mesh):
    placed = (
        P(("energy", "slab"), None, None, "col"),
        P(("energy", "slab"), None, None, None),
        P("energy", None, "col", None),
        P(),
        P("energy", None, None, None),
    )

    return jax.shard_map(
        on_device,
        mesh=mesh,
        in_specs=placed,
        out_specs=(
            P(("energy", "slab"), None, "col", None),
            P(("energy", "slab"), None, "col", None),
        ),
        check_vma=False,
    )
```

```python
import jax
import jax.numpy as jnp
from jax import lax
from jax.experimental import pallas as pl
from jax.experimental.pallas import tpu as pltpu
from jax.sharding import PartitionSpec as P

F32 = jnp.float32
BF16 = jnp.bfloat16
LIMIT = 24 * 1024 * 1024
LARGE = 56 * 1024 * 1024
PACK = 16
LANES = 128


def split(value):
    high = value.astype(BF16)
    return high, (value - high.astype(F32)).astype(BF16)


def mm(left, right, transposed=False):
    dims = (((1,), (1 if transposed else 0,)), ((), ()))
    return lax.dot_general(left, right, dims, preferred_element_type=F32)


def mm3(left, right, transposed=False):
    rows = left[0].shape[0]
    wide = mm(jnp.concatenate(left, axis=0), right[0], transposed)
    return wide[:rows] + (wide[rows:] + mm(left[0], right[1], transposed))


def combined(by_real, by_imag):
    half = by_real.shape[0] // 2
    return jnp.concatenate(
        [by_real[:half] - by_imag[half:], by_imag[:half] + by_real[half:]], axis=0
    )


def complex_rows(left, right):
    parts = split(left)
    return combined(mm3(parts, split(right[0])), mm3(parts, split(right[1])))


def times(left, right):
    size = right[0].shape[0] // 2
    by_real = mm3(left, (right[0][:size], right[1][:size]))
    by_imag = mm3(left, (right[0][size:], right[1][size:]))
    return combined(by_real, by_imag)


def interface_kernel(inject_ref, src_hbm, g_hbm, out_ref, g_ref, src_ref, sems, src_sem):
    first = lax.axis_index("slab") * 2
    modes, width = src_ref.shape[2], src_ref.shape[3]
    lead = width // 8
    fetch_src = pltpu.make_async_copy(src_hbm, src_ref, src_sem)
    fetch_src.start()
    fetches = {}
    for slab in range(2):
        for plane in range(2):
            for sweep in range(2):
                fetch = pltpu.make_async_copy(
                    g_hbm.at[slab, plane, :, 1 - sweep, :],
                    g_ref.at[slab, plane, sweep],
                    sems.at[slab, plane, sweep],
                )
                fetch.start()
                fetches[slab, plane, sweep] = fetch
    rows = lax.broadcasted_iota(jnp.int32, (lead, width), 0)
    cols = lax.broadcasted_iota(jnp.int32, (lead, width), 1)
    targets = [
        jnp.broadcast_to(inject_ref[sweep : sweep + 1, :].astype(F32), (width, modes)).T
        for sweep in range(2)
    ]
    fetch_src.wait()
    total = [0.0] * 4
    for slab in range(2):
        chosen = [target == (first + slab).astype(F32) for target in targets]
        left = []
        for sweep in range(2):
            unit = (cols == rows * 8 + sweep).astype(F32)
            source = [jnp.where(chosen[sweep], src_ref[sweep, part], 0.0) for part in range(2)]
            left.append(split(jnp.concatenate([unit] + source, axis=0)))
        for plane in range(2):
            for sweep in range(2):
                fetches[slab, plane, sweep].wait()
                term = mm3(left[sweep], split(g_ref[slab, plane, sweep]), True)
                order = slab if sweep == 0 else 1 - slab
                for member in range(4):
                    put(out_ref, sweep * 4 + member, (order * 2 + plane) * lead, term[:lead])
                real, imag = term[lead : lead + modes], term[lead + modes :]
                if plane == 0:
                    total[2 * sweep] += real
                    total[2 * sweep + 1] += imag
                else:
                    total[2 * sweep] -= imag
                    total[2 * sweep + 1] += real
    for dest in range(8):
        sweep, member = divmod(dest, 4)
        for part in range(2):
            piece = total[2 * sweep + part][member * 16 : (member + 1) * 16]
            put(out_ref, dest, 4 * lead + part * 16, piece)


def packed_columns(place_ref, inject_ref, sweep):
    modes = inject_ref.shape[1]
    target = inject_ref[sweep : sweep + 1, :]
    own = (target == place_ref[0]) | (target == place_ref[0] + 1)
    own = jnp.broadcast_to(own.astype(F32), (PACK, modes))
    earlier = lax.broadcasted_iota(jnp.int32, (modes, modes), 0)
    later = lax.broadcasted_iota(jnp.int32, (modes, modes), 1)
    rank = mm(own.astype(BF16), (earlier < later).astype(F32).astype(BF16))
    wanted = lax.broadcasted_iota(jnp.int32, (PACK, modes), 0) + PACK * place_ref[1]
    return jnp.where(rank == wanted.astype(F32), own, 0.0)


def unpacked_rows(place_ref, inject_ref, base_ref, sweep, part):
    back = packed_columns(place_ref, inject_ref, sweep).T.astype(BF16)
    start = (2 * sweep + part) * PACK
    high, low = split(base_ref[start : start + PACK, :])
    return mm(back, high) + mm(back, low)


def select_kernel(place_ref, inject_ref, src_ref, high_ref, low_ref):
    width = src_ref.shape[3]
    rows = lax.broadcasted_iota(jnp.int32, (width // 8, width), 0)
    cols = lax.broadcasted_iota(jnp.int32, (width // 8, width), 1)
    lead = width // 8
    for slab in range(2):
        for sweep in range(2):
            span = slice(sweep * lead, (sweep + 1) * lead)
            unit = (cols == rows * 8 + sweep).astype(F32)
            high_ref[slab, span, :] = unit.astype(BF16)
            low_ref[slab, span, :] = jnp.zeros_like(unit).astype(BF16)
            here = inject_ref[sweep : sweep + 1, :] == place_ref[0] + slab
            pick = jnp.where(here, packed_columns(place_ref, inject_ref, sweep), 0.0).astype(BF16)
            for part in range(2):
                start = 2 * lead + (2 * sweep + part) * PACK
                high, low = split(src_ref[sweep, part])
                high_ref[slab, start : start + PACK, :] = mm(pick, high).astype(BF16)
                low_ref[slab, start : start + PACK, :] = mm(pick, low).astype(BF16)


def spread_kernel(high_ref, low_ref, g_ref, out_ref, flow_ref):
    lead = g_ref.shape[3] // 8
    total = [0.0] * 4
    for slab in range(2):
        parts = (high_ref[slab], low_ref[slab])
        real = mm3(parts, split(g_ref[slab, 0]), True)
        imag = mm3(parts, split(g_ref[slab, 1]), True)
        for sweep in range(2):
            base = sweep * lead
            place = slab * 4 * lead + sweep * 2 * lead
            put(out_ref, 0, place, real[base : base + lead])
            put(out_ref, 0, place + lead, imag[base : base + lead])
            one = 2 * lead + 2 * sweep * PACK
            two, three = one + PACK, one + 2 * PACK
            total[2 * sweep] += real[one:two] - imag[two:three]
            total[2 * sweep + 1] += real[two:three] + imag[one:two]
    for item in range(4):
        flow_ref[0, item * PACK : (item + 1) * PACK, :] = total[item]


def expand_kernel(place_ref, inject_ref, base_ref, extra_ref, out_ref):
    modes = inject_ref.shape[1]
    for sweep in range(2):
        for part in range(2):
            span = slice((2 * sweep + part) * modes, (2 * sweep + part + 1) * modes)
            rows = unpacked_rows(place_ref, inject_ref, base_ref, sweep, part)
            out_ref[span, :] = extra_ref[span, :] + rows


def coupling_kernel(team_ref, c_ref, x_ref):
    left = team_ref[0] == 0
    size = c_ref.shape[3]
    for slab in range(2):
        x_ref[slab, :size] = jnp.where(left, c_ref[slab, 0].T, c_ref[slab, 0])
        x_ref[slab, size:] = jnp.where(left, c_ref[slab, 1].T, -c_ref[slab, 1])


def put(ref, dest, start, value):
    rows, lanes = ref.shape[1] // 2, ref.shape[2]
    ref[dest, start : start + value.shape[0], :] = value[:, :lanes]
    ref[dest, rows + start : rows + start + value.shape[0], :] = value[:, lanes:]


def taken(ref, source, start, count):
    rows = ref.shape[1] // 2
    halves = [ref[source, base + start : base + start + count, :] for base in (0, rows)]
    return jnp.concatenate(halves, axis=1)


def stacked(ref, start, count):
    return jnp.concatenate([taken(ref, block, start, count) for block in range(8)], axis=0)


def pair_map_kernel(
    team_ref, recv_ref, x_ref, mask_ref, top_ref, bottom_ref, qa_ref, first_ref
):
    left = team_ref[0] == 0
    size = x_ref.shape[2]
    lead = size // 8
    coupled = [(x_ref[slab, :size], x_ref[slab, size:]) for slab in range(2)]
    blocks = [
        (stacked(recv_ref, 2 * item * lead, lead), stacked(recv_ref, (2 * item + 1) * lead, lead))
        for item in range(2)
    ]
    flow = taken(recv_ref, 0, 4 * lead, 32)
    for block in range(1, 8):
        flow = flow + taken(recv_ref, block, 4 * lead, 32)
    flow_a = jnp.where(mask_ref[0] != 0, flow, 0.0)
    flow_b = jnp.where(mask_ref[1] != 0, flow, 0.0)
    qa_ref[...] = flow_a

    def pick(one, two):
        return (jnp.where(left, one[0], two[0]), jnp.where(left, one[1], two[1]))

    def product(one, two):
        return complex_rows(jnp.concatenate(one, axis=0), two)

    first = product(pick(coupled[0], blocks[0]), pick(blocks[0], coupled[1]))
    second = product(pick(coupled[1], blocks[1]), pick(blocks[1], coupled[0]))
    second = (second[:size], second[size:])
    first_ref[...] = first
    lanes = size // 2
    both = complex_rows(first, second)
    flow_a = jnp.where(left, flow_a, complex_rows(flow_a, coupled[1]))
    flow_b = jnp.where(left, flow_b, complex_rows(flow_b, coupled[0]))
    flow = complex_rows(flow_a, second) + flow_b
    for side, out_ref in enumerate((top_ref, bottom_ref)):
        span = slice(side * lanes, (side + 1) * lanes)
        out_ref[: 2 * size, :] = both[:, span]
        out_ref[2 * size :, :] = flow[:, span]


def item_of(info_ref, item):
    return jnp.where(info_ref[0] == 0, item, 3 - item)


def entry_state(info_ref, lead_ref, state_ref):
    return jnp.where(info_ref[1] == 0, lead_ref[...], state_ref[...])


def gather_kernel(info_ref, lead_ref, *refs):
    pieces, (high_ref, low_ref, flow_ref, out_ref) = refs[:8], refs[8:]
    lanes = pieces[0].shape[1]
    count = 4 * lanes
    for shift in range(4):
        place = lax.rem(info_ref[3] + shift, 4)
        for side in range(2):
            piece = pieces[2 * shift + side]
            span = slice(side * lanes, (side + 1) * lanes)
            high, low = split(piece[:count, :])
            high_ref[place, :, span] = high
            low_ref[place, :, span] = low
            flow_ref[place, :, span] = piece[count:, :]
    state = lead_ref[...]
    for item in range(4):
        index = item_of(info_ref, item)
        state = times(split(state), (high_ref[index], low_ref[index])) + flow_ref[index]
    out_ref[...] = state


def row_map_kernel(
    info_ref, high_ref, low_ref, flow_ref, row_high_ref, row_low_ref, row_flow_ref, half_ref
):
    maps, flows = [], []
    for item in range(4):
        index = item_of(info_ref, item)
        maps.append((high_ref[index], low_ref[index]))
        flows.append(flow_ref[index])
    size = high_ref.shape[2]
    early = times(maps[0], maps[1])
    early_flow = times(split(flows[0]), maps[1]) + flows[1]
    late = split(times(maps[2], maps[3]))
    late_flow = times(split(flows[2]), maps[3]) + flows[3]
    half_ref[: 2 * size, :] = early
    half_ref[2 * size :, :] = early_flow
    high, low = split(times(split(early), late))
    row_high_ref[...] = high
    row_low_ref[...] = low
    row_flow_ref[...] = times(split(early_flow), late) + late_flow


def row_kernel(info_ref, lead_ref, state_ref, high_ref, low_ref, flow_ref, out_ref):
    state = entry_state(info_ref, lead_ref, state_ref)
    out_ref[...] = times(split(state), (high_ref[...], low_ref[...])) + flow_ref[...]


def prefix_kernel(
    info_ref, high_ref, low_ref, flow_ref, half_ref, first_ref, x_ref, qa_ref, out_ref, inner_ref
):
    size = high_ref.shape[2]
    left = info_ref[0] == 0
    one, three = item_of(info_ref, 0), item_of(info_ref, 2)
    rows = lax.broadcasted_iota(jnp.int32, (2 * size + 32, size), 0)
    cols = lax.broadcasted_iota(jnp.int32, (2 * size + 32, size), 1)
    half = half_ref[...]
    third = (high_ref[three], low_ref[three])
    whole_row = times(split(half[: 2 * size]), third)
    whole_flow = times(split(half[2 * size :]), third) + flow_ref[three]
    none = (rows == cols).astype(F32)
    single = high_ref[one].astype(F32) + low_ref[one].astype(F32)
    single = jnp.concatenate([single, flow_ref[one]], axis=0)
    triple = jnp.concatenate([whole_row, whole_flow], axis=0)
    count = info_ref[2]
    low_half = jnp.where(count == 0, none, single)
    out_ref[...] = jnp.where(count < 2, low_half, jnp.where(count == 2, half, triple))
    second = split(x_ref[1])
    first = first_ref[...]
    inner_ref[: 2 * size, :] = jnp.where(left, times(split(first), second), first)
    inner_ref[2 * size :, :] = times(split(qa_ref[...]), second)


def entry_map_kernel(info_ref, prefix_ref, inner_ref, x_ref, high_ref, low_ref, flow_ref):
    size = x_ref.shape[2]
    left = info_ref[0] == 0
    prefix, flow = split(prefix_ref[: 2 * size, :]), split(prefix_ref[2 * size :, :])
    turn = split(x_ref[0])
    inner = split(inner_ref[: 2 * size, :])
    item_a = jnp.where(left, times(prefix, turn), prefix_ref[: 2 * size, :])
    flow_ref[0] = jnp.where(left, times(flow, turn), prefix_ref[2 * size :, :])
    item_b = times(prefix, inner)
    flow_ref[1] = times(flow, inner) + inner_ref[2 * size :, :]
    for item, value in enumerate((item_a, item_b)):
        high, low = split(value)
        high_ref[item] = high
        low_ref[item] = low


def inflow_kernel(info_ref, lead_ref, state_ref, high_ref, low_ref, flow_ref, out_ref):
    state = split(entry_state(info_ref, lead_ref, state_ref))
    for item in range(2):
        value = times(state, (high_ref[item], low_ref[item])) + flow_ref[item]
        for dest in range(8):
            put(out_ref, dest, 32 * item, value)


def arrange_kernel(
    place_ref, inject_ref, recv_ref, base_ref, extra_ref, high_ref, low_ref, out_ref
):
    lead = recv_ref.shape[1] // 16
    modes = inject_ref.shape[1]
    width = base_ref.shape[1]
    for slab in range(2):
        for kind in range(4):
            high, low = split(stacked(recv_ref, (slab * 4 + kind) * lead, lead))
            sweep, part = divmod(kind, 2)
            high_ref[slab, sweep, part] = high
            low_ref[slab, sweep, part] = low
    for sweep in range(2):
        target = jnp.broadcast_to(
            inject_ref[sweep : sweep + 1, :].astype(F32), (width, modes)
        ).T
        for part in range(2):
            start = (2 * sweep + part) * modes
            rows = unpacked_rows(place_ref, inject_ref, base_ref, sweep, part)
            rows = rows + extra_ref[start : start + modes, :]
            for slab in range(2):
                chosen = target == (place_ref[0] + slab).astype(F32)
                out_ref[sweep, slab, part] = jnp.where(chosen, rows, 0.0)


def state_kernel(last_ref, high_ref, low_ref, base_ref, left_ref, right_ref):
    modes = base_ref.shape[3]
    for sweep, out_ref in enumerate((left_ref, right_ref)):
        for slab in range(2):
            item = slab if sweep == 0 else 1 - slab
            pieces = []
            for part in range(2):
                start = item * 32 + part * 16
                for member in range(4):
                    pieces.append(taken(last_ref, sweep * 4 + member, start, 16))
            parts = split(jnp.concatenate(pieces, axis=0))
            by = [
                mm3(parts, (high_ref[slab, sweep, part], low_ref[slab, sweep, part]))
                for part in range(2)
            ]
            value = combined(by[0], by[1])
            for part in range(2):
                rows = value[part * modes : (part + 1) * modes]
                out_ref[slab, part] = base_ref[sweep, slab, part] + rows


def params(limit=LIMIT):
    return pltpu.CompilerParams(vmem_limit_bytes=limit)


def whole(shape):
    zeros = (0,) * len(shape)
    return pl.BlockSpec(shape, lambda *_: zeros)


SMEM = pl.BlockSpec(memory_space=pltpu.SMEM)
VMEM = pl.BlockSpec(memory_space=pltpu.VMEM)
ANY = pl.BlockSpec(memory_space=pl.ANY)


def exchange(value):
    return lax.all_to_all(value, "col", split_axis=0, concat_axis=0, tiled=True)


def on_device(diag_inverse, couplings, sources, inject, leads):
    orbitals = diag_inverse.shape[2]
    width = diag_inverse.shape[3]
    size = couplings.shape[2]
    modes = sources.shape[3]
    lead = size // 8
    part_rows = orbitals // 8
    slabs = lax.axis_size("slab")
    slab_index = lax.axis_index("slab")
    col_index = lax.axis_index("col")
    team = col_index // 4
    member = col_index % 4
    first = slab_index * 2
    place = jnp.stack([first, jnp.zeros_like(first)]).astype(jnp.int32)
    position = jnp.where(team == 0, slab_index, slabs - 1 - slab_index)
    info = jnp.stack([team, position // 4, position % 4, slab_index % 4]).astype(jnp.int32)
    block_rows = 4 * lead + 32
    sources = jnp.transpose(sources, (0, 1, 3, 2))
    leads = jnp.transpose(leads, (0, 1, 3, 2))

    sent = pl.pallas_call(
        interface_kernel,
        grid=(1,),
        in_specs=[whole(inject.shape), ANY, ANY],
        out_specs=whole((8, 2 * block_rows, LANES)),
        out_shape=jax.ShapeDtypeStruct((8, 2 * block_rows, LANES), F32),
        scratch_shapes=[
            pltpu.VMEM((2, 2, 2, size, width), F32),
            pltpu.VMEM(sources.shape, F32),
            pltpu.SemaphoreType.DMA((2, 2, 2)),
            pltpu.SemaphoreType.DMA,
        ],
        compiler_params=params(LARGE),
        name="interface_terms",
    )(inject, sources, diag_inverse.reshape(2, 2, size, orbitals // size, width))
    sent, inject_after = lax.optimization_barrier((sent, inject))
    received = exchange(sent)

    def chunk_terms(place):
        terms = jax.ShapeDtypeStruct((2, 2 * lead + 4 * PACK, width), BF16)
        high, low = pl.pallas_call(
            select_kernel,
            in_specs=[SMEM, VMEM, VMEM],
            out_specs=[VMEM, VMEM],
            out_shape=[terms, terms],
            compiler_params=params(),
            name="select_terms",
        )(place, inject_after, sources)
        return pl.pallas_call(
            spread_kernel,
            grid=(8,),
            in_specs=[
                whole(terms.shape),
                whole(terms.shape),
                pl.BlockSpec((2, 2, part_rows, width), lambda step: (0, 0, step, 0)),
            ],
            out_specs=[
                pl.BlockSpec((1, 16 * lead, LANES), lambda step: (step, 0, 0)),
                pl.BlockSpec((1, 4 * PACK, part_rows), lambda step: (step, 0, 0)),
            ],
            out_shape=[
                jax.ShapeDtypeStruct((8, 16 * lead, LANES), F32),
                jax.ShapeDtypeStruct((8, 4 * PACK, part_rows), F32),
            ],
            compiler_params=params(LARGE),
            name="spread_terms",
        )(high, low, diag_inverse)

    def summed(flows):
        return lax.psum_scatter(flows, "col", scatter_dimension=0, tiled=False)

    spread, flows = chunk_terms(place)
    turned = pl.pallas_call(
        coupling_kernel,
        in_specs=[SMEM, VMEM],
        out_specs=VMEM,
        out_shape=jax.ShapeDtypeStruct((2, 2 * size, size), F32),
        compiler_params=params(),
        name="coupling_rows",
    )(info, couplings)
    own_inject = lax.dynamic_slice(inject, (team, member * 16), (1, 16))[0]
    own_inject = jnp.concatenate([own_inject, own_inject])
    marks = jnp.stack([own_inject == first + team, own_inject == first + 1 - team])
    marks = jnp.broadcast_to(marks.astype(F32)[:, :, None], (2, 32, size))
    own_lead = lax.dynamic_slice(leads, (team, 0, member * 16, 0), (1, 2, 16, size))
    own_lead = own_lead.reshape(32, size)
    base = summed(flows)
    owners = jnp.arange(slabs, dtype=jnp.int32)[:, None, None]
    counts = jnp.sum((inject_after[None] >> 1 == owners).astype(jnp.int32), axis=2)
    chunks = (jnp.max(counts) + PACK - 1) // PACK

    def more(chunk, extra):
        place = jnp.stack([first, chunk]).astype(jnp.int32)
        flows = chunk_terms(place)[1]
        return pl.pallas_call(
            expand_kernel,
            in_specs=[SMEM, VMEM, VMEM, VMEM],
            out_specs=VMEM,
            out_shape=jax.ShapeDtypeStruct((4 * modes, part_rows), F32),
            compiler_params=params(),
            name="expand_terms",
        )(place, inject, summed(flows), extra)

    extra = lax.fori_loop(1, chunks, more, jnp.zeros((4 * modes, part_rows), F32))
    received, turned, marks, own_lead, spread, extra = lax.optimization_barrier(
        (received, turned, marks, own_lead, spread, extra)
    )
    rows = exchange(spread)

    top, bottom, flow_a, first_map = pl.pallas_call(
        pair_map_kernel,
        in_specs=[SMEM, VMEM, VMEM, VMEM],
        out_specs=[VMEM] * 4,
        out_shape=[
            jax.ShapeDtypeStruct((2 * size + 32, size // 2), F32),
            jax.ShapeDtypeStruct((2 * size + 32, size // 2), F32),
            jax.ShapeDtypeStruct((32, size), F32),
            jax.ShapeDtypeStruct((2 * size, size), F32),
        ],
        compiler_params=params(),
        name="pair_map",
    )(info, received, turned, marks)

    def turn(value, step):
        return lax.ppermute(
            value, "slab", [(slab, slab // 4 * 4 + (slab + step) % 4) for slab in range(slabs)]
        )

    before_top, after_bottom = turn(top, 1), turn(bottom, -1)
    before_bottom, after_top = turn(bottom, 1), turn(top, -1)
    across_top, across_bottom = turn(before_top, 1), turn(after_bottom, -1)
    pieces = (after_top, after_bottom, across_top, across_bottom, before_top, before_bottom)
    row_maps = [
        jax.ShapeDtypeStruct((4, 2 * size, size), BF16),
        jax.ShapeDtypeStruct((4, 2 * size, size), BF16),
        jax.ShapeDtypeStruct((4, 32, size), F32),
    ]
    state_shape = jax.ShapeDtypeStruct((32, size), F32)
    *maps, flow = pl.pallas_call(
        gather_kernel,
        in_specs=[SMEM] + [VMEM] * 9,
        out_specs=[VMEM] * 4,
        out_shape=row_maps + [state_shape],
        compiler_params=params(),
        name="gather_maps",
    )(info, own_lead, top, bottom, *pieces)

    cols = lax.axis_size("col")
    pairs = []
    for slab in range(slabs):
        for col in range(cols):
            target = (slab + (4 if col < 4 else -4)) % slabs
            pairs.append((slab * cols + col, target * cols + col))

    def local(kernel, name, shapes, *args):
        single = not isinstance(shapes, list)
        return pl.pallas_call(
            kernel,
            in_specs=[SMEM] + [VMEM] * (len(args) - 1),
            out_specs=VMEM if single else [VMEM] * len(shapes),
            out_shape=shapes,
            compiler_params=params(),
            name=name,
        )(*args)

    def hop(value):
        return lax.ppermute(value, ("slab", "col"), pairs)

    full = jax.ShapeDtypeStruct((2 * size + 32, size), F32)
    half_map = jax.ShapeDtypeStruct((2 * size, size), BF16)
    flow = hop(flow)
    *row_map, half_row = local(
        row_map_kernel, "row_map", [half_map, half_map, state_shape, full], info, *maps
    )
    flow = local(row_kernel, "row_step", state_shape, info, own_lead, flow, *row_map)
    flow, half_row = lax.optimization_barrier((flow, half_row))
    flow = hop(flow)
    prefix, inner_map = local(
        prefix_kernel,
        "prefix_map",
        [full, full],
        info,
        *maps,
        half_row,
        first_map,
        turned,
        flow_a,
    )
    flow = local(row_kernel, "row_step", state_shape, info, own_lead, flow, *row_map)
    flow, prefix, inner_map = lax.optimization_barrier((flow, prefix, inner_map))
    flow = hop(flow)
    two_maps = [
        jax.ShapeDtypeStruct((2, 2 * size, size), BF16),
        jax.ShapeDtypeStruct((2, 2 * size, size), BF16),
        jax.ShapeDtypeStruct((2, 32, size), F32),
    ]
    entry = local(entry_map_kernel, "entry_map", two_maps, info, prefix, inner_map, turned)
    last = local(
        inflow_kernel,
        "inflow",
        jax.ShapeDtypeStruct((8, 2 * 64, LANES), F32),
        info,
        own_lead,
        flow,
        *entry,
    )
    rows, base, last = lax.optimization_barrier((rows, base, last))
    last = exchange(last)
    arranged = [
        jax.ShapeDtypeStruct((2, 2, 2, size, part_rows), BF16),
        jax.ShapeDtypeStruct((2, 2, 2, size, part_rows), BF16),
        jax.ShapeDtypeStruct((2, 2, 2, modes, part_rows), F32),
    ]
    arranged = local(
        arrange_kernel, "arrange_rows", arranged, place, inject, rows, base, extra
    )

    shape = jax.ShapeDtypeStruct((2, 2, modes, part_rows), F32)
    left, right = pl.pallas_call(
        state_kernel,
        in_specs=[VMEM] * 4,
        out_specs=[VMEM, VMEM],
        out_shape=[shape, shape],
        compiler_params=params(),
        name="states",
    )(last, *arranged)
    return jnp.transpose(left, (0, 1, 3, 2)), jnp.transpose(right, (0, 1, 3, 2))


def solution(mesh):
    placed = (
        P(("energy", "slab"), None, None, "col"),
        P(("energy", "slab"), None, None, None),
        P("energy", None, "col", None),
        P(),
        P("energy", None, None, None),
    )

    return jax.shard_map(
        on_device,
        mesh=mesh,
        in_specs=placed,
        out_specs=(
            P(("energy", "slab"), None, "col", None),
            P(("energy", "slab"), None, "col", None),
        ),
        check_vma=False,
    )
```
